256 devices in a mesh: vel: 32 (over z, x), space: 8 (over y, core).
Axes of the slice: x: 4, y: 4, z: 8, core: 2. Of those that a mesh axis runs over, the one named last changes fastest.
Arguments:
- distribution: float32 [3, 32768, 16, 256], P(None, 'vel', 'space'), may hold values from 0.005 to 2.5, as said below
- wall_temp: float32 [1024], P('space'), may hold values from 0.6 to 1.6
- coverage: float32 [12, 1024], P(None, 'space'), may hold values from 0 to 0.15
- face_cell: int32 [8, 128], P('space'), may hold values from 0 to 127, each once within a row
- face_owner: int32 [1024], P('space'), may hold values from 0 to 3
- stoichiometry: int32 [12, 3], replicated, may hold values from 0 to 2
- sticking: float32 [4, 3], replicated, may hold values from 0.1 to 0.9
- surface_rates: float32 [4, 2, 12], replicated, may hold values from 0.02 to 2
Outputs:
- advanced: float32 [3, 32768, 16, 256], P(None, 'vel', 'space')
- new_coverage: float32 [12, 1024], P(None, 'space')
The draws below stay inside these ranges and needn't reach their ends.
Inputs may be any that keep to these rules, and one draw needn't show every extreme that they name: `distribution`: positive everywhere. `face_cell`: row p lists each wall column x * 64 + z of space block p once, x counted within the block.
All inputs are finite; a program needn't handle non-finite values.
Results may differ from the reference program's by a relative error of at most 0.0001.
Values sent between devices are 32-bit elements; how exact they have to be, the bound alone decides.
No kernel may reach another device: no remote copies, remote signals or barrier semaphores. Data moves between devices by JAX's collectives and lax.ppermute only.
A program may use at most 192 MiB of HBM per device.

```python
import math
import jax
import jax.numpy as jnp
from jax import lax

S = 3
VG = 32
NV = 32768
NY = 4
NZ = 64
CX = 2
NX = 16
FACE_DEV = 128
FACES = 1024
NSURF = 12
PATCHES = 4
NEWTON = 8
N_SPACE = 8


SPEED_LIMIT = 4.0


SPECIES_MASS = (1.0, 2.0, 4.0)


def component_drawn(position):
    spacing = 2.0 * SPEED_LIMIT / VG
    return (position.astype(jnp.float32) + 0.5) * spacing - SPEED_LIMIT


def draw_distribution(key, part):
    key = jax.random.fold_in(key, 11)
    subkeys = jax.random.split(key, 5)
    cells_yz = NY * NZ
    vel_index = jnp.arange(NV, dtype=jnp.int32)
    speed_x = component_drawn(vel_index % VG)[None, :, None, None]
    speed_y = component_drawn(vel_index // VG % VG)[None, :, None, None]
    speed_z = component_drawn(vel_index // (VG * VG))[None, :, None, None]
    molecule_weights = jnp.array(SPECIES_MASS, jnp.float32)[:, None, None, None]
    temp_low, temp_high, spread = (0.7, 1.4, 0.4)
    base_temp = jax.random.uniform(subkeys[0], (1, 1, NX, cells_yz), jnp.float32, temp_low, temp_high)
    drift = jax.random.uniform(subkeys[1], (3, 1, 1, NX, cells_yz), jnp.float32, -0.4, 0.4)
    amplitude = jax.random.uniform(subkeys[2], (S, 1, NX, cells_yz), jnp.float32, 0.6, 1.4)
    roughness = jax.random.uniform(subkeys[3], (S, NV, NX, cells_yz), jnp.float32, 1.0 - spread, 1.0 + spread)
    background = jax.random.uniform(subkeys[4], (S, NV, NX, cells_yz), jnp.float32, 0.005, 0.015)
    offset_x = speed_x - drift[0]
    offset_y = speed_y - drift[1]
    offset_z = speed_z - drift[2]
    relative_velocity_norm_sq = offset_x * offset_x + offset_y * offset_y + offset_z * offset_z
    return amplitude * jnp.exp(-molecule_weights * relative_velocity_norm_sq / (2.0 * base_temp)) * roughness + background


def place_ends(values, key, smallest, top_value):
    longest = values.shape.index(max(values.shape))
    spots = []
    for shift in (0, 1):
        where = [jax.random.randint(jax.random.fold_in(key, axis), (), 0, length) for axis, length in enumerate(values.shape)]
        where[longest] = (where[longest] + shift) % values.shape[longest]
        spots.append(tuple(where))
    return values.at[spots[0]].set(smallest).at[spots[1]].set(top_value)


def shard_levels(stream_key, dims, cuts, smallest, top_value):
    factor_of = 1.0
    for dim, parts in cuts:
        draws = jax.random.uniform(jax.random.fold_in(jax.random.fold_in(stream_key, 6), dim), (parts,), jnp.float32, smallest / len(cuts), top_value / len(cuts))
        factor_of = factor_of * jnp.repeat(jnp.exp(draws), dims[dim] // parts).reshape((-1,) + (1,) * (len(dims) - 1 - dim))
    return factor_of


def setup_inputs(seed: int = 0) -> dict:
    seeds = jax.random.split(jax.random.key(seed), 9)
    return {
        "distribution": draw_distribution(jax.random.fold_in(seeds[8], 71), 0),
        "wall_temp": jnp.clip(0.6 + 1.0 * jax.random.uniform(seeds[1], (FACES,), jnp.float32) ** shard_levels(seeds[1], (FACES,), ((0, 8),), -0.2, 0.2), 0.6, 1.6),
        "coverage": jnp.clip(0.15 * jax.random.uniform(seeds[2], (NSURF, FACES), jnp.float32) ** shard_levels(seeds[2], (NSURF, FACES), ((1, 8),), -0.2, 0.2), 0.0, 0.15),
        "face_cell": jax.vmap(lambda own: jax.random.permutation(own, FACE_DEV))(jax.random.split(seeds[3], N_SPACE)).reshape((N_SPACE, FACE_DEV)).astype(jnp.int32),
        "face_owner": place_ends(jax.random.randint(seeds[4], (FACES,), 0, PATCHES), jax.random.fold_in(seeds[4], 1), 0, PATCHES - 1).astype(jnp.int32),
        "stoichiometry": place_ends(jax.random.randint(seeds[5], (NSURF, S), 0, 3), jax.random.fold_in(seeds[5], 1), 0, 2).astype(jnp.int32),
        "sticking": jnp.clip(jnp.exp(jax.random.uniform(seeds[6], (PATCHES, S), jnp.float32, math.log(0.1), math.log(0.9))), 0.1, 0.9),
        "surface_rates": jnp.clip(jnp.exp(jax.random.uniform(seeds[7], (PATCHES, 2, NSURF), jnp.float32, math.log(0.02), math.log(2.0))), 0.02, 2.0),
    }


SPEED_LIMIT = 4.0
SPECIES_MASS = (1.0, 2.0, 4.0)
COLLISION_RATE = (0.3, 0.2, 0.15)
TIME_STEP = 0.08
SURFACE_STEP = 2.0
DAMPING = 0.25
ACTIVATION = 2.0


def component(position):
    spacing = 2.0 * SPEED_LIMIT / VG
    return (position.astype(jnp.float32) + 0.5) * spacing - SPEED_LIMIT


def velocity_grid(vel_index):
    return component(vel_index % VG), component((vel_index // VG) % VG), component(vel_index // (VG * VG))


def surface_solve(incident, wall_temps, start_cov, owners, stoichiometry, sticking, surface_rates):
    precise = lax.Precision.HIGHEST
    patch_ids = jnp.arange(sticking.shape[0], dtype=jnp.int32)
    onehot = (owners[None, :] == patch_ids[:, None]).astype(jnp.float32)
    stick_face = jnp.dot(sticking.T, onehot, precision=precise)
    arrhenius = jnp.exp(ACTIVATION * (1.0 - 1.0 / wall_temps))
    desorb = jnp.dot(surface_rates[:, 0, :].T, onehot, precision=precise) * arrhenius[None, :]
    lateral = jnp.dot(surface_rates[:, 1, :].T, onehot, precision=precise)
    counts = stoichiometry.astype(jnp.float32)
    share_in = counts / (1.0 + jnp.sum(counts, axis=0, keepdims=True))
    share_out = counts / (1.0 + jnp.sum(counts, axis=1, keepdims=True))
    feed_rate = jnp.dot(share_in, stick_face * incident, precision=precise)
    covers = start_cov
    for newton_turn in range(NEWTON):
        vacant = 1.0 - jnp.sum(covers, axis=0, keepdims=True)
        cubed_cov = covers * covers * covers
        net_rate = feed_rate * vacant - desorb * covers - lateral * cubed_cov
        residual = covers - start_cov - SURFACE_STEP * net_rate
        diagonal = 1.0 + SURFACE_STEP * (desorb + 3.0 * lateral * covers * covers)
        scaled = residual / diagonal
        coupling = SURFACE_STEP * feed_rate / diagonal
        update = scaled - coupling * (jnp.sum(scaled, axis=0, keepdims=True) / (1.0 + jnp.sum(coupling, axis=0, keepdims=True)))
        covers = covers - DAMPING * update
    released = desorb * covers + lateral * covers * covers * covers
    vacant = 1.0 - jnp.sum(covers, axis=0, keepdims=True)
    emitted = incident * (1.0 - stick_face * vacant) + jnp.dot(share_out.T, released, precision=precise)
    return covers, emitted


def upwind(velocity, field, lower_cell, upper_cell):
    return jnp.maximum(velocity, 0.0) * (field - lower_cell) + jnp.minimum(velocity, 0.0) * (upper_cell - field)


def reference(distribution, wall_temp, coverage, face_cell, face_owner, stoichiometry, sticking, surface_rates):
    spacing = 2.0 * SPEED_LIMIT / VG
    weight = spacing * spacing * spacing
    speed_x, speed_y, speed_z = velocity_grid(jnp.arange(NV, dtype=jnp.int32))
    speed_sq = speed_x * speed_x + speed_y * speed_y + speed_z * speed_z
    molecule_weights = jnp.array(SPECIES_MASS, jnp.float32)
    field = distribution.reshape(S, NV, NX, NY, NZ)
    wall_layer = field[:, :, :, 0, :].reshape(S, NV, NX * NZ)
    toward = jnp.maximum(-speed_y, 0.0)
    incoming_cols = weight * jnp.sum(toward[None, :, None] * wall_layer, axis=1)
    blocks = jnp.arange(NX // CX, dtype=jnp.int32)
    face_col = (blocks[:, None] * FACE_DEV + face_cell).reshape(-1).astype(jnp.int32)
    incident = incoming_cols[:, face_col]
    outward = jnp.maximum(speed_y, 0.0)
    norm_rows = []
    for constituent_number in range(S):
        emission_shape = jnp.exp(-molecule_weights[constituent_number] * speed_sq[:, None] / (2.0 * wall_temp[None, :]))
        norm_rows.append(weight * jnp.sum(outward[:, None] * emission_shape, axis=0))
    normalizer = jnp.stack(norm_rows)
    covers, emitted = surface_solve(incident, wall_temp, coverage, face_owner, stoichiometry, sticking, surface_rates)
    wall_density = emitted / normalizer
    col_density = jnp.zeros((S, NX * NZ), jnp.float32).at[:, face_col].set(wall_density)
    col_temp = jnp.zeros((NX * NZ,), jnp.float32).at[face_col].set(wall_temp)
    wall_ghost = col_density[:, None, :] * jnp.exp(-molecule_weights[:, None, None] * speed_sq[None, :, None] / (2.0 * col_temp[None, None, :]))
    wall_ghost = wall_ghost.reshape(S, NV, NX, 1, NZ)
    cross_x = speed_x[None, :, None, None, None]
    cross_y = speed_y[None, :, None, None, None]
    cross_z = speed_z[None, :, None, None, None]
    left_cell = jnp.roll(field, 1, axis=2)
    right_cell = jnp.roll(field, -1, axis=2)
    lower_cell = jnp.concatenate([wall_ghost, field[:, :, :, :-1]], axis=3)
    upper_cell = jnp.concatenate([field[:, :, :, 1:], field[:, :, :, -1:]], axis=3)
    back_cell = jnp.roll(field, 1, axis=4)
    front_cell = jnp.roll(field, -1, axis=4)
    transported = field - TIME_STEP * (upwind(cross_x, field, left_cell, right_cell) + upwind(cross_y, field, lower_cell, upper_cell) + upwind(cross_z, field, back_cell, front_cell))
    cells = NX * NY * NZ
    flattened = transported.reshape(S, NV, cells)
    density = weight * jnp.sum(flattened, axis=1)
    mom_x = weight * jnp.sum(speed_x[None, :, None] * flattened, axis=1)
    mom_y = weight * jnp.sum(speed_y[None, :, None] * flattened, axis=1)
    mom_z = weight * jnp.sum(speed_z[None, :, None] * flattened, axis=1)
    thermal_motion_work = weight * jnp.sum(speed_sq[None, :, None] * flattened, axis=1)
    combined_gas_weight = jnp.sum(density, axis=0)
    constituent_weight_per_volume = jnp.sum(molecule_weights[:, None] * density, axis=0)
    bulk_x = jnp.sum(molecule_weights[:, None] * mom_x, axis=0) / constituent_weight_per_volume
    bulk_y = jnp.sum(molecule_weights[:, None] * mom_y, axis=0) / constituent_weight_per_volume
    bulk_z = jnp.sum(molecule_weights[:, None] * mom_z, axis=0) / constituent_weight_per_volume
    mean_flow_norm_sq = bulk_x * bulk_x + bulk_y * bulk_y + bulk_z * bulk_z
    gas_heat_level = (jnp.sum(molecule_weights[:, None] * thermal_motion_work, axis=0) - constituent_weight_per_volume * mean_flow_norm_sq) / (3.0 * combined_gas_weight)
    offset_x = speed_x[:, None] - bulk_x[None, :]
    offset_y = speed_y[:, None] - bulk_y[None, :]
    offset_z = speed_z[:, None] - bulk_z[None, :]
    relative_velocity_norm_sq = offset_x * offset_x + offset_y * offset_y + offset_z * offset_z
    outputs = []
    for constituent_number in range(S):
        maxwellian_argument = jnp.exp(-molecule_weights[constituent_number] * relative_velocity_norm_sq / (2.0 * gas_heat_level[None, :]))
        maxwell_norm = weight * jnp.sum(maxwellian_argument, axis=0)
        maxwell = density[constituent_number][None, :] * maxwellian_argument / maxwell_norm[None, :]
        relaxation = 1.0 - jnp.exp(-TIME_STEP * COLLISION_RATE[constituent_number] * combined_gas_weight)
        outputs.append(flattened[constituent_number] + relaxation[None, :] * (maxwell - flattened[constituent_number]))
    advanced = jnp.stack(outputs).reshape(S, NV, NX, NY * NZ)
    return advanced, covers
```

```python
import jax
import jax.numpy as jnp
from jax import lax
from jax.experimental import pallas as pl
from jax.experimental.pallas import tpu as pltpu
from jax.sharding import PartitionSpec as P

S = 3
VG = 32
NZ = 64
CX = 2
NEWTON = 8
NSURF = 12
PATCHES = 4
N_VEL = 32
N_SPACE = 8

SPEED_LIMIT = 4.0
SPACING = 2.0 * SPEED_LIMIT / VG
WEIGHT = SPACING * SPACING * SPACING
SPECIES_MASS = (1.0, 2.0, 4.0)
COLLISION_RATE = (0.3, 0.2, 0.15)
TIME_STEP = 0.08
SURFACE_STEP = 2.0
DAMPING = 0.25
ACTIVATION = 2.0

PAIRS = VG // 2
HALF = PAIRS // 2
BLOCKS = 12
KYS = S * VG // BLOCKS
TILE = (8, 128)
PRECISE = lax.Precision.HIGHEST


def rows():
    return lax.broadcasted_iota(jnp.int32, TILE, 0)


def lanes():
    return lax.broadcasted_iota(jnp.int32, TILE, 1)


def down(value, by):
    return pltpu.roll(value, by % 8, 0)


def along(value, by):
    return pltpu.roll(value, by % 128, 1)


def pair_speed():
    parity = (rows() >= 4).astype(jnp.float32)
    return (parity + 0.5) * SPACING - SPEED_LIMIT


def speed_of(position):
    return (position.astype(jnp.float32) + 0.5) * SPACING - SPEED_LIMIT


def moments_kernel(kz_ref, f_ref, own_ref, rim_ref, acc_ref):
    step = pl.program_id(0)
    species = step // 4
    quarter = step % 4
    half = quarter // 2
    base = pair_speed()
    speeds = [jnp.abs(base + 2.0 * SPACING * j) for j in range(PAIRS)]

    @pl.when(quarter == 0)
    def _():
        acc_ref[species] = jnp.zeros((20,) + TILE, jnp.float32)

    def one(k, carry):
        zero = jnp.zeros(TILE, jnp.float32)
        sums = []
        for side in range(2):
            n0, n1, n2, n3 = zero, zero, zero, zero
            for j in range(side * HALF, (side + 1) * HALF):
                f = f_ref[k, 8 * j : 8 * j + 8, :]
                g = f * speeds[j]
                n0 = n0 + f
                n1 = n1 + g
                g = g * speeds[j]
                n2 = n2 + g
                n3 = n3 + g * speeds[j]
            sums.append((n0, n1, n2, n3))
        (a0, a1, a2, a3), (b0, b1, b2, b3) = sums
        cy = speed_of(quarter * KYS + k)
        cy2 = cy * cy
        acy = jnp.abs(cy)
        d = a0 + b0
        x1 = b1 - a1
        e = a2 + b2 + cy2 * d
        yd = cy * d
        new = (
            d, x1, yd, e,
            b1, b2, cy * b1, b3 + cy2 * b1,
            a1, -a2, cy * a1, a3 + cy2 * a1,
            acy * d, acy * x1, acy * yd, acy * e,
        )
        return tuple(c + n for c, n in zip(carry, new))

    start = tuple(jnp.zeros(TILE, jnp.float32) for _ in range(16))
    total = lax.fori_loop(0, KYS, one, start)
    for q in range(12):
        acc_ref[species, q] += total[q]
    for q in range(4):
        acc_ref[species, 12 + 4 * half + q] += total[12 + q]

    @pl.when(step == BLOCKS - 1)
    def _():
        row = rows()
        lane = lanes()
        cz = speed_of(kz_ref[0])
        acz = jnp.abs(cz)
        rise = cz > 0.0
        odd = row % 2 == 1
        upper_h = (row // 2) % 2 == 1
        low = lane < 64
        own = []
        rim = []
        incident = []
        for s in range(S):
            full = []
            for q in range(20):
                v = acc_ref[s, q]
                full.append(v + down(v, 4))
            for q in range(4):
                b, xp, xm = full[q], full[4 + q], full[8 + q]
                ym, yp = full[12 + q], full[16 + q]
                zp = jnp.where(lane % 64 == 0, along(b, 65), along(b, 1))
                zm = jnp.where(lane % 64 == 63, along(b, 63), along(b, 127))
                shifted_z = jnp.where(rise, zp, zm)
                rp = along(yp, 64)
                rm = along(ym, 64)
                from_low = jnp.where(low, jnp.where(upper_h, down(rp, 2), 0.0), rp)
                from_high = jnp.where(low, rm, jnp.where(upper_h, ym, down(rm, -2)))
                inner = jnp.where(odd, down(xp, 1), down(xm, -1))
                stay = (1.0 - TIME_STEP * acz) * b - TIME_STEP * (xp + xm + yp + ym)
                own.append(
                    stay
                    + TIME_STEP * (acz * shifted_z + from_low + from_high + inner)
                )
                rim.append(TIME_STEP * jnp.where(odd, xp, xm))
            ym = full[12]
            incident.append(jnp.where(low, ym, along(down(ym, -1), 64)))
        for values, out in ((own, own_ref), (rim, rim_ref)):
            packed = [values[0], values[4], values[8]]
            momenta = [0.0, 0.0, 0.0, 0.0]
            for s in range(S):
                m = SPECIES_MASS[s]
                d, px, py, e = values[4 * s : 4 * s + 4]
                momenta[0] = momenta[0] + m * px
                momenta[1] = momenta[1] + m * py
                momenta[2] = momenta[2] + (m * cz) * d
                momenta[3] = momenta[3] + m * (e + cz * cz * d)
            packed = packed + momenta
            if out is own_ref:
                last = jnp.where(
                    row == 4,
                    down(incident[0], 4),
                    jnp.where(
                        row == 5,
                        down(incident[1], 5),
                        jnp.where(row == 6, down(incident[2], 6), 0.0),
                    ),
                )
            else:
                last = jnp.zeros(TILE, jnp.float32)
            packed.append(last)
            for t in range(4):
                out[t] = WEIGHT * jnp.where(row < 4, packed[2 * t], packed[2 * t + 1])


def pack_kernel(f_ref, rise_ref, fall_ref):
    odd = rows() % 2 == 1

    def one(k, carry):
        for t in range(4):
            a = f_ref[k, 16 * t : 16 * t + 8, :]
            b = f_ref[k, 16 * t + 8 : 16 * t + 16, :]
            fall_ref[k, 8 * t : 8 * t + 8, :] = jnp.where(odd, down(b, 1), a)
            a = f_ref[k, 64 + 16 * t : 64 + 16 * t + 8, :]
            b = f_ref[k, 64 + 16 * t + 8 : 64 + 16 * t + 16, :]
            rise_ref[k, 8 * t : 8 * t + 8, :] = jnp.where(odd, a, down(b, -1))
        return carry

    lax.fori_loop(0, KYS, one, 0)


def spread_kernel(own_ref, left_ref, right_ref, out_ref):
    odd = rows() % 2 == 1
    for t in range(4):
        moved = jnp.where(odd, down(right_ref[t], 1), down(left_ref[t], -1))
        value = own_ref[t] + moved
        for peer in range(N_VEL):
            out_ref[peer, t] = value


def selector(face_cell):
    column = lax.broadcasted_iota(jnp.int32, (128, 128), 0)
    return (column == face_cell).astype(jnp.float32)


def to_tile(value):
    row = rows() % 4
    low = lanes() < 64
    wide = jnp.broadcast_to(value, TILE)
    return jnp.where(
        jnp.logical_and(row == 0, low),
        wide,
        jnp.where(jnp.logical_and(row == 1, low), along(wide, 64), 0.0),
    )


def wall_kernel(
    kz_ref, stoich_ref, stick_ref, rates_ref, temp_ref, cover_ref, cell_ref, owner_ref,
    surface_ref, sums_ref, wall_x_ref, wall_y_ref,
):
    select = selector(cell_ref[...])
    pieces = jnp.concatenate(
        [cover_ref[...], temp_ref[...], owner_ref[...].astype(jnp.float32),
         jnp.zeros((2, 128), jnp.float32)], axis=0,
    )
    placed = lax.dot_general(
        pieces, select, (((1,), (1,)), ((), ())), precision=PRECISE,
        preferred_element_type=jnp.float32,
    )
    temp = placed[12:13]
    owner = placed[13:14]
    arrhenius = jnp.exp(ACTIVATION * (1.0 - 1.0 / temp))
    zero = jnp.zeros((1, 128), jnp.float32)
    masks = [jnp.abs(owner - float(p)) < 0.5 for p in range(PATCHES)]

    def by_owner(read):
        value = zero
        for p in range(PATCHES):
            value = jnp.where(masks[p], read(p), value)
        return value

    surface_ref[0] = jnp.concatenate([placed[0:12], jnp.zeros((4, 128), jnp.float32)], axis=0)
    desorb = [by_owner(lambda p: rates_ref[p, 0, j]) * arrhenius for j in range(NSURF)]
    lateral = [by_owner(lambda p: rates_ref[p, 1, j]) for j in range(NSURF)]
    stick = [by_owner(lambda p: stick_ref[p, s]) for s in range(S)]
    surface_ref[1] = jnp.concatenate(desorb + [zero] * 4, axis=0)
    surface_ref[2] = jnp.concatenate(lateral + [zero] * 4, axis=0)
    counts = [[stoich_ref[j, s].astype(jnp.float32) for s in range(S)] for j in range(NSURF)]
    for s in range(S):
        column_sum = counts[0][s]
        for j in range(1, NSURF):
            column_sum = column_sum + counts[j][s]
        into = jnp.concatenate(
            [(zero + counts[j][s]) / (zero + (1.0 + column_sum)) * stick[s] for j in range(NSURF)]
            + [zero] * 4, axis=0,
        )
        out = jnp.concatenate(
            [(zero + counts[j][s]) / (zero + (1.0 + counts[j][0] + counts[j][1] + counts[j][2]))
             for j in range(NSURF)]
            + [zero] * 4, axis=0,
        )
        surface_ref[3 + s] = into
        surface_ref[6 + s] = out

    k_rows = lax.broadcasted_iota(jnp.int32, (VG, 128), 0)
    c = speed_of(k_rows)
    up = jnp.maximum(c, 0.0)
    cz = speed_of(kz_ref[0])
    temp_tile = to_tile(temp)
    inside = temp_tile > 0.0
    safe = jnp.where(inside, temp_tile, 1.0)
    base = pair_speed()
    for s in range(S):
        m = SPECIES_MASS[s]
        e = jnp.exp(-m * (c * c) / (2.0 * temp))

        def total(v):
            return jnp.sum(v, axis=0, keepdims=True)

        s0 = total(e)
        s1 = total(c * e)
        s2 = total(c * c * e)
        u1 = total(up * e)
        u2 = total(up * c * e)
        u3 = total(up * c * c * e)
        norm = WEIGHT * u1 * s0 * s0
        scale = WEIGHT * TIME_STEP
        sums_ref[s] = jnp.concatenate(
            [
                1.0 / norm,
                scale * u1 * s0 * s0,
                scale * u1 * s1 * s0,
                scale * u2 * s0 * s0,
                scale * u1 * s0 * s1,
                scale * (u3 * s0 * s0 + u1 * s2 * s0 + u1 * s0 * s2),
                stick[s],
                zero,
            ],
            axis=0,
        )
        rate = -m / (2.0 * safe)
        ez = jnp.where(inside, jnp.exp(rate * (cz * cz)), 0.0)
        for j in range(PAIRS):
            cx = base + 2.0 * SPACING * j
            wall_x_ref[s, j] = jnp.exp(rate * (cx * cx))
            cy = (PAIRS + j + 0.5) * SPACING - SPEED_LIMIT
            wall_y_ref[s, j] = (TIME_STEP * cy) * ez * jnp.exp(rate * (cy * cy))


def solve_kernel(
    kz_ref, parts_ref, surface_ref, sums_ref, cell_ref,
    cover_ref, ex_ref, ey_ref, coef_ref,
):
    row = rows()
    totals = []
    for t in range(4):
        v = parts_ref[0, t]
        for peer in range(1, N_VEL):
            v = v + parts_ref[peer, t]
        totals.append(v)
    incident = [totals[3][4 + s : 5 + s] for s in range(S)]
    start = surface_ref[0]
    desorb = surface_ref[1]
    lateral = surface_ref[2]
    feed = (
        surface_ref[3] * incident[0]
        + surface_ref[4] * incident[1]
        + surface_ref[5] * incident[2]
    )
    covers = start

    def total(v):
        return jnp.sum(v, axis=0, keepdims=True)

    for _ in range(NEWTON):
        vacant = 1.0 - total(covers)
        squared = covers * covers
        net = feed * vacant - desorb * covers - lateral * (squared * covers)
        residual = covers - start - SURFACE_STEP * net
        inverse = 1.0 / (1.0 + SURFACE_STEP * (desorb + 3.0 * lateral * squared))
        scaled = residual * inverse
        coupling = SURFACE_STEP * feed * inverse
        update = scaled - coupling * (total(scaled) / (1.0 + total(coupling)))
        covers = covers - DAMPING * update
    released = desorb * covers + lateral * (covers * covers * covers)
    vacant = 1.0 - total(covers)
    cover_face = jnp.dot(
        covers, selector(cell_ref[...]), precision=PRECISE, preferred_element_type=jnp.float32
    )
    cover_ref[...] = cover_face[0:NSURF]

    def quantity(q):
        v = totals[q // 2]
        other = down(v, 4)
        return jnp.where(row < 4, v, other) if q % 2 == 0 else jnp.where(row < 4, other, v)

    dens = [quantity(s) for s in range(S)]
    mom = [quantity(3 + a) for a in range(3)]
    energy = quantity(6)
    wall_dens = []
    for s in range(S):
        m = SPECIES_MASS[s]
        emitted = incident[s] * (1.0 - sums_ref[s, 6:7] * vacant) + total(
            surface_ref[6 + s] * released
        )
        wd = emitted * sums_ref[s, 0:1]
        wall_dens.append(to_tile(wd))
        dens[s] = dens[s] + to_tile(wd * sums_ref[s, 1:2])
        for a in range(3):
            mom[a] = mom[a] + to_tile((m * wd) * sums_ref[s, 2 + a : 3 + a])
        energy = energy + to_tile((m * wd) * sums_ref[s, 5:6])
    gas = dens[0] + dens[1] + dens[2]
    mass = SPECIES_MASS[0] * dens[0] + SPECIES_MASS[1] * dens[1] + SPECIES_MASS[2] * dens[2]
    bulk = [v / mass for v in mom]
    flow = bulk[0] * bulk[0] + bulk[1] * bulk[1] + bulk[2] * bulk[2]
    temperature = (energy - mass * flow) / (3.0 * gas)
    base = pair_speed()
    cz = speed_of(kz_ref[0])
    for s in range(S):
        rate = -SPECIES_MASS[s] / (2.0 * temperature)

        def pair_table(drift, store):
            sum_pairs = jnp.zeros(TILE, jnp.float32)
            for j in range(PAIRS):
                off = (base + 2.0 * SPACING * j) - drift
                e = jnp.exp(rate * (off * off))
                if store:
                    ex_ref[s, j] = e
                sum_pairs = sum_pairs + e
            return sum_pairs + down(sum_pairs, 4)

        sum_x = pair_table(bulk[0], True)
        sum_z = pair_table(bulk[2], False)
        sum_y = jnp.zeros(TILE, jnp.float32)
        tables = []
        for k in range(VG):
            off = ((k + 0.5) * SPACING - SPEED_LIMIT) - bulk[1]
            e = jnp.exp(rate * (off * off))
            tables.append(e)
            sum_y = sum_y + e
        keep = jnp.exp((-TIME_STEP * COLLISION_RATE[s]) * gas)
        off = cz - bulk[2]
        own_z = jnp.exp(rate * (off * off))
        factor = (1.0 - keep) * dens[s] * own_z / (WEIGHT * sum_x * sum_y * sum_z)
        for k in range(VG):
            ey_ref[s, k] = tables[k] * factor
        coef_ref[s, 0] = keep
        coef_ref[s, 1] = keep * wall_dens[s]


def step_kernel(
    kz_ref, f_ref, left_ref, right_ref, wall_x_ref, wall_y_ref, ex_ref, ey_ref, coef_ref, out_ref,
):
    step = pl.program_id(0)
    species = step // 4
    quarter = step % 4
    row = rows()
    lane = lanes()
    odd = row % 2 == 1
    upper_h = (row // 2) % 2 == 1
    low = lane < 64
    cz = speed_of(kz_ref[0])
    acz = jnp.abs(cz)
    rise_z = cz > 0.0
    shift_z = jnp.where(rise_z, 1, 127)
    edge = (lane % 64) == jnp.where(rise_z, 63, 0)
    base = pair_speed()
    keep = coef_ref[species, 0]
    wall_scale = coef_ref[species, 1]
    coef_z = (TIME_STEP * acz) * keep
    drift = TIME_STEP * keep

    def body(lower):
        def one(k, carry):
            ky = quarter * KYS + k
            cy = speed_of(ky)
            acy = jnp.abs(cy)
            coef_y = acy * drift
            coef_own = keep - coef_z - coef_y
            if lower:
                at_wall = jnp.logical_and(low, jnp.logical_not(upper_h))
                coef_y = jnp.where(at_wall, 0.0, coef_y)
                wall = wall_y_ref[species, ky - PAIRS] * wall_scale
            else:
                at_top = jnp.logical_and(jnp.logical_not(low), upper_h)
                coef_own = jnp.where(at_top, coef_own + coef_y, coef_own)
                coef_y = jnp.where(at_top, 0.0, coef_y)
            ey = ey_ref[species, ky]
            for j in range(PAIRS):
                f = f_ref[k, 8 * j : 8 * j + 8, :]
                coef_x = jnp.abs(base + 2.0 * SPACING * j) * drift
                t = (j % HALF) // 2
                if j < HALF:
                    halo = right_ref[k, 8 * t : 8 * t + 8, :]
                    if j % 2 == 0:
                        halo = down(halo, 1)
                    fnx = jnp.where(odd, halo, down(f, -1))
                else:
                    halo = left_ref[k, 8 * t : 8 * t + 8, :]
                    if j % 2 == 0:
                        halo = down(halo, -1)
                    fnx = jnp.where(odd, down(f, 1), halo)
                swapped = along(f, 64)
                if lower:
                    fny = jnp.where(low, down(swapped, 2), swapped)
                else:
                    fny = jnp.where(low, swapped, down(swapped, -2))
                fnz = pltpu.roll(jnp.where(edge, swapped, f), shift_z, 1)
                value = (
                    coef_own * f
                    + coef_x * (fnx - f)
                    + coef_y * fny
                    + coef_z * fnz
                    + ex_ref[species, j] * ey
                )
                if lower:
                    value = value + wall_x_ref[species, j] * wall
                out_ref[k, 8 * j : 8 * j + 8, :] = value
            return carry

        lax.fori_loop(0, KYS, one, 0)

    @pl.when(quarter < 2)
    def _():
        body(False)

    @pl.when(quarter >= 2)
    def _():
        body(True)


def whole(*shape):
    return pl.BlockSpec(shape, lambda i: (0,) * len(shape))


def block(size):
    return pl.BlockSpec((KYS, size, 128), lambda i: (i, 0, 0))


SMEM = pl.BlockSpec(memory_space=pltpu.SMEM)
VMEM = pl.BlockSpec(memory_space=pltpu.VMEM)
F32 = jnp.float32


def shape(*dims):
    return jax.ShapeDtypeStruct(dims, F32)


def shifted(value, axis, by):
    peers = lax.axis_size(axis)
    return lax.ppermute(value, axis, [(i, (i + by) % peers) for i in range(peers)])


def per_device(
    distribution, wall_temp, coverage, face_cell, face_owner, stoichiometry, sticking, surface_rates
):
    kz = lax.axis_index("vel").astype(jnp.int32).reshape(1)
    field = (
        distribution.reshape(S, VG * VG, CX, 2, 128)
        .transpose(0, 1, 3, 2, 4)
        .reshape(S * VG, 128, 128)
    )
    own, rim = pl.pallas_call(
        moments_kernel,
        grid=(BLOCKS,),
        in_specs=[SMEM, block(128)],
        out_specs=[whole(4, 8, 128)] * 2,
        out_shape=[shape(4, 8, 128)] * 2,
        scratch_shapes=[pltpu.VMEM((S, 20, 8, 128), F32)],
    )(kz, field)
    rim_left = shifted(rim, "space", 1)
    rim_right = shifted(rim, "space", -1)
    rise, fall = pl.pallas_call(
        pack_kernel,
        grid=(BLOCKS,),
        in_specs=[block(128)],
        out_specs=[block(32)] * 2,
        out_shape=[shape(S * VG, 32, 128)] * 2,
    )(field)
    from_left = shifted(rise, "space", 1)
    from_right = shifted(fall, "space", -1)
    copies = pl.pallas_call(
        spread_kernel,
        in_specs=[VMEM] * 3,
        out_specs=VMEM,
        out_shape=shape(N_VEL, 4, 8, 128),
    )(own, rim_left, rim_right)
    parts = lax.all_to_all(copies, "vel", 0, 0)
    face_row = face_cell.reshape(1, 128)
    surface, sums, wall_x, wall_y = pl.pallas_call(
        wall_kernel,
        in_specs=[SMEM] * 4 + [VMEM] * 4,
        out_specs=[VMEM] * 4,
        out_shape=[shape(9, 16, 128), shape(S, 8, 128), shape(S, 16, 8, 128), shape(S, 16, 8, 128)],
    )(
        kz, stoichiometry, sticking, surface_rates,
        wall_temp.reshape(1, 128), coverage, face_row, face_owner.reshape(1, 128),
    )
    covers, ex, ey, coef = pl.pallas_call(
        solve_kernel,
        in_specs=[SMEM] + [VMEM] * 4,
        out_specs=[VMEM] * 4,
        out_shape=[
            shape(NSURF, 128), shape(S, 16, 8, 128), shape(S, 32, 8, 128), shape(S, 2, 8, 128)
        ],
    )(kz, parts, surface, sums, face_row)
    advanced = pl.pallas_call(
        step_kernel,
        grid=(BLOCKS,),
        in_specs=[
            SMEM, block(128), block(32), block(32),
            whole(S, 16, 8, 128), whole(S, 16, 8, 128), whole(S, 16, 8, 128),
            whole(S, 32, 8, 128), whole(S, 2, 8, 128),
        ],
        out_specs=block(128),
        out_shape=shape(S * VG, 128, 128),
    )(kz, field, from_left, from_right, wall_x, wall_y, ex, ey, coef)
    advanced = (
        advanced.reshape(S, VG * VG, 2, CX, 128)
        .transpose(0, 1, 3, 2, 4)
        .reshape(distribution.shape)
    )
    return advanced, covers


def solution(mesh):
    return jax.shard_map(
        per_device,
        mesh=mesh,
        in_specs=(
            P(None, "vel", "space", None),
            P("space"),
            P(None, "space"),
            P("space", None),
            P("space"),
            P(),
            P(),
            P(),
        ),
        out_specs=(P(None, "vel", "space", None), P(None, "space")),
        check_vma=False,
    )
```

```python
import jax
import jax.numpy as jnp
from jax import lax
from jax.experimental import pallas as pl
from jax.experimental.pallas import tpu as pltpu
from jax.sharding import Mesh
from jax.sharding import PartitionSpec as P

S = 3
VG = 32
NZ = 64
CX = 2
NEWTON = 8
NSURF = 12
PATCHES = 4
N_Z = 8
N_X = 4

SPEED_LIMIT = 4.0
SPACING = 2.0 * SPEED_LIMIT / VG
WEIGHT = SPACING * SPACING * SPACING
SPECIES_MASS = (1.0, 2.0, 4.0)
COLLISION_RATE = (0.3, 0.2, 0.15)
TIME_STEP = 0.08
SURFACE_STEP = 2.0
DAMPING = 0.25
ACTIVATION = 2.0

PAIRS = VG // 2
HALF = PAIRS // 2
BLOCKS = 12
KYS = S * VG // BLOCKS
TILE = (8, 128)
PRECISE = lax.Precision.HIGHEST


def rows():
    return lax.broadcasted_iota(jnp.int32, TILE, 0)


def lanes():
    return lax.broadcasted_iota(jnp.int32, TILE, 1)


def down(value, by):
    return pltpu.roll(value, by % 8, 0)


def along(value, by):
    return pltpu.roll(value, by % 128, 1)


def pair_speed():
    parity = (rows() >= 4).astype(jnp.float32)
    return (parity + 0.5) * SPACING - SPEED_LIMIT


def speed_of(position):
    return (position.astype(jnp.float32) + 0.5) * SPACING - SPEED_LIMIT


def chunk(src, dst, sems, c):
    part = pl.ds(c * KYS, KYS)
    return pltpu.make_async_copy(src.at[part], dst.at[part], sems.at[c])


def moments_kernel(
    kz_ref, f_hbm, own_ref, to_right_ref, to_left_ref, rise_ref, fall_ref, f_ref, acc_ref, f_sem,
):
    for c in range(BLOCKS):
        chunk(f_hbm, f_ref, f_sem, c).start()
    base = pair_speed()
    speeds = [jnp.abs(base + 2.0 * SPACING * j) for j in range(PAIRS)]
    acc_ref[...] = jnp.zeros_like(acc_ref)

    def one(k, carry):
        zero = jnp.zeros(TILE, jnp.float32)
        sums = []
        for side in range(2):
            n0, n1, n2, n3 = zero, zero, zero, zero
            for j in range(side * HALF, (side + 1) * HALF):
                f = f_ref[k, 8 * j : 8 * j + 8, :]
                g = f * speeds[j]
                n0 = n0 + f
                n1 = n1 + g
                g = g * speeds[j]
                n2 = n2 + g
                n3 = n3 + g * speeds[j]
            sums.append((n0, n1, n2, n3))
        (a0, a1, a2, a3), (b0, b1, b2, b3) = sums
        for h in range(2):
            for q in range(2):
                to = pl.ds(16 * h + 8 * q, 8)
                fall_ref[k, to, :] = f_ref[k, pl.ds(32 * q + 2 * h, 8, 4), :]
                rise_ref[k, to, :] = f_ref[k, pl.ds(64 + 32 * q + 2 * h + 1, 8, 4), :]
        cy = speed_of(k % VG)
        cy2 = cy * cy
        acy = jnp.abs(cy)
        d = a0 + b0
        x1 = b1 - a1
        e = a2 + b2 + cy2 * d
        yd = cy * d
        new = (
            d, x1, yd, e,
            b1, b2, cy * b1, b3 + cy2 * b1,
            a1, -a2, cy * a1, a3 + cy2 * a1,
            acy * d, acy * x1, acy * yd, acy * e,
        )
        return tuple(c + n for c, n in zip(carry, new))

    start = tuple(jnp.zeros(TILE, jnp.float32) for _ in range(16))
    def turn(c, carry):
        species, half = c // 4, c % 4 // 2
        chunk(f_hbm, f_ref, f_sem, c).wait()
        total = lax.fori_loop(0, KYS, lambda i, v: one(c * KYS + i, v), start, unroll=4)
        for q in range(12):
            acc_ref[species, q] += total[q]
        for q in range(4):
            acc_ref[species, 12 + 4 * half + q] += total[12 + q]
        return carry

    lax.fori_loop(0, BLOCKS, turn, 0)
    row = rows()
    lane = lanes()
    cz = speed_of(kz_ref[0])
    acz = jnp.abs(cz)
    rise = cz > 0.0
    odd = row % 2 == 1
    upper_h = (row // 2) % 2 == 1
    low = lane < 64
    own = []
    rim = []
    incident = []
    for s in range(S):
        full = []
        for q in range(20):
            v = acc_ref[s, q]
            full.append(v + down(v, 4))
        for q in range(4):
            b, xp, xm = full[q], full[4 + q], full[8 + q]
            ym, yp = full[12 + q], full[16 + q]
            zp = jnp.where(lane % 64 == 0, along(b, 65), along(b, 1))
            zm = jnp.where(lane % 64 == 63, along(b, 63), along(b, 127))
            shifted_z = jnp.where(rise, zp, zm)
            rp = along(yp, 64)
            rm = along(ym, 64)
            from_low = jnp.where(low, jnp.where(upper_h, down(rp, 2), 0.0), rp)
            from_high = jnp.where(low, rm, jnp.where(upper_h, ym, down(rm, -2)))
            inner = jnp.where(odd, down(xp, 1), down(xm, -1))
            stay = (1.0 - TIME_STEP * acz) * b - TIME_STEP * (xp + xm + yp + ym)
            own.append(
                stay
                + TIME_STEP * (acz * shifted_z + from_low + from_high + inner)
            )
            rim.append(TIME_STEP * jnp.where(odd, xp, xm))
        ym = full[12]
        incident.append(jnp.where(low, ym, along(down(ym, -1), 64)))
    for values, out in ((own, own_ref), (rim, None)):
        packed = [values[0], values[4], values[8]]
        momenta = [0.0, 0.0, 0.0, 0.0]
        for s in range(S):
            m = SPECIES_MASS[s]
            d, px, py, e = values[4 * s : 4 * s + 4]
            momenta[0] = momenta[0] + m * px
            momenta[1] = momenta[1] + m * py
            momenta[2] = momenta[2] + (m * cz) * d
            momenta[3] = momenta[3] + m * (e + cz * cz * d)
        packed = packed + momenta
        if out is own_ref:
            last = jnp.where(
                row == 4,
                down(incident[0], 4),
                jnp.where(
                    row == 5,
                    down(incident[1], 5),
                    jnp.where(row == 6, down(incident[2], 6), 0.0),
                ),
            )
        else:
            last = jnp.zeros(TILE, jnp.float32)
        packed.append(last)
        for t in range(4):
            value = WEIGHT * jnp.where(row < 4, packed[2 * t], packed[2 * t + 1])
            if out is own_ref:
                out[t] = value
            else:
                to_right_ref[t] = jnp.where(odd, 0.0, down(value, -1))
                to_left_ref[t] = jnp.where(odd, down(value, 1), 0.0)


def selector(face_cell):
    column = lax.broadcasted_iota(jnp.int32, (128, 128), 0)
    return (column == face_cell).astype(jnp.float32)


def to_tile(value):
    row = rows() % 4
    low = lanes() < 64
    wide = jnp.broadcast_to(value, TILE)
    return jnp.where(
        jnp.logical_and(row == 0, low),
        wide,
        jnp.where(jnp.logical_and(row == 1, low), along(wide, 64), 0.0),
    )


def wall_kernel(
    kz_ref, stoich_ref, stick_ref, rates_ref, temp_ref, cover_ref, cell_ref, owner_ref,
    surface_ref, sums_ref, wall_x_ref, wall_y_ref,
):
    select = selector(cell_ref[...])
    pieces = jnp.concatenate(
        [cover_ref[...], temp_ref[...], owner_ref[...].astype(jnp.float32),
         jnp.zeros((2, 128), jnp.float32)], axis=0,
    )
    placed = lax.dot_general(
        pieces, select, (((1,), (1,)), ((), ())), precision=PRECISE,
        preferred_element_type=jnp.float32,
    )
    temp = placed[12:13]
    owner = placed[13:14]
    arrhenius = jnp.exp(ACTIVATION * (1.0 - 1.0 / temp))
    zero = jnp.zeros((1, 128), jnp.float32)
    masks = [jnp.abs(owner - float(p)) < 0.5 for p in range(PATCHES)]

    def by_owner(read):
        value = zero
        for p in range(PATCHES):
            value = jnp.where(masks[p], read(p), value)
        return value

    surface_ref[0] = jnp.concatenate([placed[0:12], jnp.zeros((4, 128), jnp.float32)], axis=0)
    desorb = [by_owner(lambda p: rates_ref[p, 0, j]) * arrhenius for j in range(NSURF)]
    lateral = [by_owner(lambda p: rates_ref[p, 1, j]) for j in range(NSURF)]
    stick = [by_owner(lambda p: stick_ref[p, s]) for s in range(S)]
    surface_ref[1] = jnp.concatenate(desorb + [zero] * 4, axis=0)
    surface_ref[2] = jnp.concatenate(lateral + [zero] * 4, axis=0)
    counts = [[stoich_ref[j, s].astype(jnp.float32) for s in range(S)] for j in range(NSURF)]
    for s in range(S):
        column_sum = counts[0][s]
        for j in range(1, NSURF):
            column_sum = column_sum + counts[j][s]
        into = jnp.concatenate(
            [(zero + counts[j][s]) / (zero + (1.0 + column_sum)) * stick[s] for j in range(NSURF)]
            + [zero] * 4, axis=0,
        )
        out = jnp.concatenate(
            [(zero + counts[j][s]) / (zero + (1.0 + counts[j][0] + counts[j][1] + counts[j][2]))
             for j in range(NSURF)]
            + [zero] * 4, axis=0,
        )
        surface_ref[3 + s] = into
        surface_ref[6 + s] = out

    k_rows = lax.broadcasted_iota(jnp.int32, (VG, 128), 0)
    c = speed_of(k_rows)
    up = jnp.maximum(c, 0.0)
    cz = speed_of(kz_ref[0])
    cy = c[VG // 2 :]
    temps = [temp, pltpu.roll(temp, 64, 1)]
    for s in range(S):
        m = SPECIES_MASS[s]
        e = jnp.exp(-m * (c * c) / (2.0 * temp))

        def total(v):
            return jnp.sum(v, axis=0, keepdims=True)

        s0 = total(e)
        s1 = total(c * e)
        s2 = total(c * c * e)
        u1 = total(up * e)
        u2 = total(up * c * e)
        u3 = total(up * c * c * e)
        norm = WEIGHT * u1 * s0 * s0
        scale = WEIGHT * TIME_STEP
        sums_ref[s] = jnp.concatenate(
            [
                1.0 / norm,
                scale * u1 * s0 * s0,
                scale * u1 * s1 * s0,
                scale * u2 * s0 * s0,
                scale * u1 * s0 * s1,
                scale * (u3 * s0 * s0 + u1 * s2 * s0 + u1 * s0 * s2),
                stick[s],
                zero,
            ],
            axis=0,
        )
        for x in range(CX):
            rate = -m / (2.0 * temps[x])
            wall_x_ref[s, x] = jnp.exp(rate * (c * c))
            wall_y_ref[s, x] = (TIME_STEP * cy) * jnp.exp(rate * (cy * cy)) * jnp.exp(rate * (cz * cz))


def step_kernel(
    kz_ref, parts_ref, surface_ref, sums_ref, cell_ref, wall_x_ref, wall_y_ref,
    left_ref, right_ref, f_hbm,
    cover_ref, out_hbm,
    f_ref, out_ref, ex_ref, ey_ref, wy_ref, f_sem, out_sem,
):
    for c in range(BLOCKS):
        chunk(f_hbm, f_ref, f_sem, c).start()
    row = rows()
    totals = []
    for t in range(4):
        v = parts_ref[0, t]
        for peer in range(1, N_Z):
            v = v + parts_ref[peer, t]
        totals.append(v)
    incident = [totals[3][4 + s : 5 + s] for s in range(S)]
    start = surface_ref[0]
    desorb = surface_ref[1]
    lateral = surface_ref[2]
    feed = (
        surface_ref[3] * incident[0]
        + surface_ref[4] * incident[1]
        + surface_ref[5] * incident[2]
    )
    covers = start

    def total(v):
        return jnp.sum(v, axis=0, keepdims=True)

    for _ in range(NEWTON):
        vacant = 1.0 - total(covers)
        squared = covers * covers
        net = feed * vacant - desorb * covers - lateral * (squared * covers)
        residual = covers - start - SURFACE_STEP * net
        inverse = 1.0 / (1.0 + SURFACE_STEP * (desorb + 3.0 * lateral * squared))
        scaled = residual * inverse
        coupling = SURFACE_STEP * feed * inverse
        update = scaled - coupling * (total(scaled) / (1.0 + total(coupling)))
        covers = covers - DAMPING * update
    released = desorb * covers + lateral * (covers * covers * covers)
    vacant = 1.0 - total(covers)
    cover_face = jnp.dot(
        covers, selector(cell_ref[...]), precision=PRECISE, preferred_element_type=jnp.float32
    )
    cover_ref[...] = cover_face[0:NSURF]

    def quantity(q):
        v = totals[q // 2]
        other = down(v, 4)
        return jnp.where(row < 4, v, other) if q % 2 == 0 else jnp.where(row < 4, other, v)

    dens = [quantity(s) for s in range(S)]
    mom = [quantity(3 + a) for a in range(3)]
    energy = quantity(6)
    wall_dens = []
    for s in range(S):
        m = SPECIES_MASS[s]
        emitted = incident[s] * (1.0 - sums_ref[s, 6:7] * vacant) + total(
            surface_ref[6 + s] * released
        )
        wd = emitted * sums_ref[s, 0:1]
        wall_dens.append(wd)
        dens[s] = dens[s] + to_tile(wd * sums_ref[s, 1:2])
        for a in range(3):
            mom[a] = mom[a] + to_tile((m * wd) * sums_ref[s, 2 + a : 3 + a])
        energy = energy + to_tile((m * wd) * sums_ref[s, 5:6])
    gas = dens[0] + dens[1] + dens[2]
    mass = SPECIES_MASS[0] * dens[0] + SPECIES_MASS[1] * dens[1] + SPECIES_MASS[2] * dens[2]
    bulk = [v / mass for v in mom]
    flow = bulk[0] * bulk[0] + bulk[1] * bulk[1] + bulk[2] * bulk[2]
    temperature = (energy - mass * flow) / (3.0 * gas)
    cz = speed_of(kz_ref[0])
    grid = speed_of(lax.broadcasted_iota(jnp.int32, (VG, 128), 0))
    keeps = []
    for s in range(S):
        rate = -SPECIES_MASS[s] / (2.0 * temperature)
        keep = jnp.exp((-TIME_STEP * COLLISION_RATE[s]) * gas)
        off = cz - bulk[2]
        scale = (1.0 - keep) * dens[s] * jnp.exp(rate * (off * off))
        keeps.append(keep)
        for r in range(4):
            at = slice(r, r + 1)

            def table(drift):
                gap = grid - drift[at]
                return jnp.exp(rate[at] * (gap * gap))

            ex = table(bulk[0])
            ey = table(bulk[1])
            factor = scale[at] / (WEIGHT * total(ex) * total(ey) * total(table(bulk[2])))
            ex_ref[s, r] = ex
            ey_ref[s, r] = ey * factor
        other = pltpu.roll(wall_dens[s], 64, 1)
        wy_ref[s, 0] = wall_y_ref[s, 0] * wall_dens[s]
        wy_ref[s, 1] = wall_y_ref[s, 1] * other

    lane = lanes()
    low = lane < 64
    acz = jnp.abs(cz)
    rise_z = cz > 0.0
    shift_z = jnp.where(rise_z, 1, 127)
    edge = (lane % 64) == jnp.where(rise_z, 63, 0)
    coef_z = TIME_STEP * acz
    octet = speed_of(lax.broadcasted_iota(jnp.int32, TILE, 0))
    coef_x = [TIME_STEP * jnp.abs(octet + 8.0 * SPACING * q) for q in range(4)]

    for s in range(S):
        keep = [jnp.broadcast_to(keeps[s][r : r + 1], TILE) for r in range(4)]
        for lower in (False, True):

            def one(k, carry, s=s, lower=lower, keep=keep):
                ky = k - s * VG
                acy = jnp.abs(speed_of(ky))
                coef_y = TIME_STEP * acy
                coef_own = 1.0 - coef_z - coef_y
                ey = [
                    jnp.broadcast_to(ey_ref[s, r, pl.ds(ky, 1), :], TILE) for r in range(4)
                ]
                if lower:
                    wy = [
                        jnp.broadcast_to(wy_ref[s, x, pl.ds(ky - PAIRS, 1), :], TILE)
                        for x in range(CX)
                    ]
                for q in range(4):
                    f = [f_ref[k, pl.ds(32 * q + r, 8, 4), :] for r in range(4)]
                    far = [along(v, 64) for v in f]
                    for r in range(4):
                        h, x = r // 2, r % 2
                        if q < 2:
                            near = f[r + 1] if x == 0 else right_ref[k, pl.ds(16 * h + 8 * q, 8), :]
                        else:
                            near = (
                                f[r - 1] if x == 1
                                else left_ref[k, pl.ds(16 * h + 8 * (q - 2), 8), :]
                            )
                        value = (
                            coef_own * f[r]
                            + coef_x[q] * (near - f[r])
                            + coef_z * pltpu.roll(jnp.where(edge, far[r], f[r]), shift_z, 1)
                        )
                        if lower and h == 0:
                            wall = wall_x_ref[s, x, 8 * q : 8 * q + 8, :] * wy[x]
                            value = value + jnp.where(low, wall, coef_y * far[r])
                        elif lower or h == 0:
                            value = value + coef_y * jnp.where(low, far[x], far[x + 2])
                        else:
                            value = value + coef_y * jnp.where(low, far[r], f[r])
                        value = keep[r] * value + ex_ref[s, r, 8 * q : 8 * q + 8, :] * ey[r]
                        out_ref[k, pl.ds(32 * q + r, 8, 4), :] = value
                return carry

            for part in range(2):
                c = 4 * s + 2 * int(lower) + part
                chunk(f_hbm, f_ref, f_sem, c).wait()
                lax.fori_loop(0, KYS, lambda i, v: one(c * KYS + i, v), 0, unroll=4)
                chunk(out_ref, out_hbm, out_sem, c).start()
    for c in range(BLOCKS):
        chunk(out_ref, out_hbm, out_sem, c).wait()


SMEM = pl.BlockSpec(memory_space=pltpu.SMEM)
VMEM = pl.BlockSpec(memory_space=pltpu.VMEM)
HBM = pl.BlockSpec(memory_space=pl.ANY)
F32 = jnp.float32
BIG = pltpu.CompilerParams(vmem_limit_bytes=16 * 1024 * 1024)
DMA = pltpu.SemaphoreType.DMA


def shape(*dims):
    return jax.ShapeDtypeStruct(dims, F32)


def shifted(value, axis, by):
    peers = lax.axis_size(axis)
    return lax.ppermute(value, axis, [(i, (i + by) % peers) for i in range(peers)])


def near(value):
    return pltpu.with_memory_space_constraint(value, pltpu.VMEM)


def moments_call(kz, field):
    return pl.pallas_call(
        moments_kernel,
        in_specs=[SMEM, HBM],
        out_specs=[VMEM] * 5,
        out_shape=[pltpu.VMEM((4, 8, 128), F32)] * 3
        + [pltpu.VMEM((S * VG, 32, 128), F32)] * 2,
        scratch_shapes=[
            pltpu.VMEM((S * VG, 128, 128), F32),
            pltpu.VMEM((S, 20, 8, 128), F32),
            DMA((BLOCKS,)),
        ],
        compiler_params=BIG,
    )(kz, field)


def wall_call(*args):
    return pl.pallas_call(
        wall_kernel,
        in_specs=[SMEM] * 4 + [VMEM] * 4,
        out_specs=[VMEM] * 4,
        out_shape=[
            pltpu.VMEM((9, 16, 128), F32),
            pltpu.VMEM((S, 8, 128), F32),
            pltpu.VMEM((S, CX, VG, 128), F32),
            pltpu.VMEM((S, CX, VG // 2, 128), F32),
        ],
    )(*args)


def step_call(*args):
    return pl.pallas_call(
        step_kernel,
        in_specs=[SMEM] + [VMEM] * 8 + [HBM],
        out_specs=[VMEM, HBM],
        out_shape=[shape(NSURF, 128), shape(S * VG, 128, 128)],
        scratch_shapes=[
            pltpu.VMEM((S * VG, 128, 128), F32),
            pltpu.VMEM((S * VG, 128, 128), F32),
            pltpu.VMEM((S, 4, VG, 128), F32),
            pltpu.VMEM((S, 4, VG, 128), F32),
            pltpu.VMEM((S, CX, VG // 2, 128), F32),
            DMA((BLOCKS,)),
            DMA((BLOCKS,)),
        ],
        compiler_params=BIG,
    )(*args)


def per_device(
    distribution, wall_temp, coverage, face_cell, face_owner, stoichiometry, sticking, surface_rates
):
    kz = lax.axis_index(("z", "x")).astype(jnp.int32).reshape(1)
    field = (
        distribution.reshape(S, VG * VG, CX, 2, 128)
        .transpose(0, 1, 3, 2, 4)
        .reshape(S * VG, 128, 128)
    )
    field = pltpu.with_memory_space_constraint(field, pltpu.HBM)
    own, to_right, to_left, rise, fall = moments_call(kz, field)
    own = own + shifted(to_right, "space", 1) + shifted(to_left, "space", -1)
    own, rise, fall = lax.optimization_barrier((own, rise, fall))
    from_left = shifted(rise, "space", 1)
    from_right = shifted(fall, "space", -1)
    own = own + shifted(own, "x", 1) + shifted(own, "x", 3) + shifted(own, "x", 2)
    copies = jnp.broadcast_to(own[None], (N_Z,) + own.shape)
    parts = lax.all_to_all(copies, "z", 0, 0)
    face_row = face_cell.reshape(1, 128)
    surface, sums, wall_x, wall_y = wall_call(
        kz, stoichiometry, sticking, surface_rates,
        wall_temp.reshape(1, 128), coverage, face_row, face_owner.reshape(1, 128),
    )
    covers, advanced = step_call(
        kz, near(parts), near(surface), near(sums), face_row, near(wall_x), near(wall_y),
        near(from_left), near(from_right), field,
    )
    advanced = (
        advanced.reshape(S, VG * VG, 2, CX, 128)
        .transpose(0, 1, 3, 2, 4)
        .reshape(distribution.shape)
    )
    return advanced, covers


def solution(mesh):
    fine = Mesh(mesh.devices.reshape(N_Z, N_X, mesh.shape["space"]), ("z", "x", "space"))
    return jax.shard_map(
        per_device,
        mesh=fine,
        in_specs=(
            P(None, ("z", "x"), "space", None),
            P("space"),
            P(None, "space"),
            P("space", None),
            P("space"),
            P(),
            P(),
            P(),
        ),
        out_specs=(P(None, ("z", "x"), "space", None), P(None, "space")),
        check_vma=False,
    )
```

```python
import functools

import jax
import jax.numpy as jnp
from jax import lax
from jax.experimental import pallas as pl
from jax.experimental.pallas import tpu as pltpu
from jax.sharding import Mesh
from jax.sharding import PartitionSpec as P

S = 3
VG = 32
NZ = 64
CX = 2
NEWTON = 8
NSURF = 12
PATCHES = 4
N_Z = 8
N_X = 4

SPEED_LIMIT = 4.0
SPACING = 2.0 * SPEED_LIMIT / VG
WEIGHT = SPACING * SPACING * SPACING
SPECIES_MASS = (1.0, 2.0, 4.0)
COLLISION_RATE = (0.3, 0.2, 0.15)
TIME_STEP = 0.08
SURFACE_STEP = 2.0
DAMPING = 0.25
ACTIVATION = 2.0

PAIRS = VG // 2
HALF = PAIRS // 2
BLOCKS = 12
KYS = S * VG // BLOCKS
GROUP = KYS // 2
TILE = (8, 128)
PRECISE = lax.Precision.HIGHEST


def rows():
    return lax.broadcasted_iota(jnp.int32, TILE, 0)


def lanes():
    return lax.broadcasted_iota(jnp.int32, TILE, 1)


def down(value, by):
    return pltpu.roll(value, by % 8, 0)


def along(value, by):
    return pltpu.roll(value, by % 128, 1)


def pair_speed():
    parity = (rows() >= 4).astype(jnp.float32)
    return (parity + 0.5) * SPACING - SPEED_LIMIT


def speed_of(position):
    return (position.astype(jnp.float32) + 0.5) * SPACING - SPEED_LIMIT


def chunk(src, dst, sems, c):
    part = pl.ds(c * KYS, KYS)
    return pltpu.make_async_copy(src.at[part], dst.at[part], sems.at[c])


def half_chunk(src, dst, sems, c):
    part = pl.ds(c * GROUP, GROUP)
    return pltpu.make_async_copy(src.at[part], dst.at[part], sems.at[c])


def moments_kernel(
    kz_ref, f_hbm, own_ref, to_right_ref, to_left_ref, f_ref, rise_ref, fall_ref, acc_ref, f_sem,
):
    for c in range(BLOCKS):
        chunk(f_hbm, f_ref, f_sem, c).start()
    base = pair_speed()
    speeds = [jnp.abs(base + 2.0 * SPACING * j) for j in range(PAIRS)]
    acc_ref[...] = jnp.zeros_like(acc_ref)

    def one(k, carry):
        zero = jnp.zeros(TILE, jnp.float32)
        sums = []
        for side in range(2):
            n0, n1, n2, n3 = zero, zero, zero, zero
            for j in range(side * HALF, (side + 1) * HALF):
                f = f_ref[k, 8 * j : 8 * j + 8, :]
                g = f * speeds[j]
                n0 = n0 + f
                n1 = n1 + g
                g = g * speeds[j]
                n2 = n2 + g
                n3 = n3 + g * speeds[j]
            sums.append((n0, n1, n2, n3))
        (a0, a1, a2, a3), (b0, b1, b2, b3) = sums
        for h in range(2):
            for q in range(2):
                to = pl.ds(16 * h + 8 * q, 8)
                fall_ref[k, to, :] = f_ref[k, pl.ds(32 * q + 2 * h, 8, 4), :]
                rise_ref[k, to, :] = f_ref[k, pl.ds(64 + 32 * q + 2 * h + 1, 8, 4), :]
        cy = speed_of(k % VG)
        cy2 = cy * cy
        acy = jnp.abs(cy)
        d = a0 + b0
        x1 = b1 - a1
        e = a2 + b2 + cy2 * d
        yd = cy * d
        new = (
            d, x1, yd, e,
            b1, b2, cy * b1, b3 + cy2 * b1,
            a1, -a2, cy * a1, a3 + cy2 * a1,
            acy * d, acy * x1, acy * yd, acy * e,
        )
        return tuple(c + n for c, n in zip(carry, new))

    start = tuple(jnp.zeros(TILE, jnp.float32) for _ in range(16))
    def turn(c, carry):
        species, half = c // 4, c % 4 // 2
        chunk(f_hbm, f_ref, f_sem, c).wait()
        total = lax.fori_loop(0, KYS, lambda i, v: one(c * KYS + i, v), start, unroll=4)
        for q in range(12):
            acc_ref[species, q] += total[q]
        for q in range(4):
            acc_ref[species, 12 + 4 * half + q] += total[12 + q]
        return carry

    lax.fori_loop(0, BLOCKS, turn, 0)
    row = rows()
    lane = lanes()
    cz = speed_of(kz_ref[0])
    acz = jnp.abs(cz)
    rise = cz > 0.0
    odd = row % 2 == 1
    upper_h = (row // 2) % 2 == 1
    low = lane < 64
    own = []
    rim = []
    incident = []
    for s in range(S):
        full = []
        for q in range(20):
            v = acc_ref[s, q]
            full.append(v + down(v, 4))
        for q in range(4):
            b, xp, xm = full[q], full[4 + q], full[8 + q]
            ym, yp = full[12 + q], full[16 + q]
            zp = jnp.where(lane % 64 == 0, along(b, 65), along(b, 1))
            zm = jnp.where(lane % 64 == 63, along(b, 63), along(b, 127))
            shifted_z = jnp.where(rise, zp, zm)
            rp = along(yp, 64)
            rm = along(ym, 64)
            from_low = jnp.where(low, jnp.where(upper_h, down(rp, 2), 0.0), rp)
            from_high = jnp.where(low, rm, jnp.where(upper_h, ym, down(rm, -2)))
            inner = jnp.where(odd, down(xp, 1), down(xm, -1))
            stay = (1.0 - TIME_STEP * acz) * b - TIME_STEP * (xp + xm + yp + ym)
            own.append(
                stay
                + TIME_STEP * (acz * shifted_z + from_low + from_high + inner)
            )
            rim.append(TIME_STEP * jnp.where(odd, xp, xm))
        ym = full[12]
        incident.append(jnp.where(low, ym, along(down(ym, -1), 64)))
    for values, out in ((own, own_ref), (rim, None)):
        packed = [values[0], values[4], values[8]]
        momenta = [0.0, 0.0, 0.0, 0.0]
        for s in range(S):
            m = SPECIES_MASS[s]
            d, px, py, e = values[4 * s : 4 * s + 4]
            momenta[0] = momenta[0] + m * px
            momenta[1] = momenta[1] + m * py
            momenta[2] = momenta[2] + (m * cz) * d
            momenta[3] = momenta[3] + m * (e + cz * cz * d)
        packed = packed + momenta
        if out is own_ref:
            last = jnp.where(
                row == 4,
                down(incident[0], 4),
                jnp.where(
                    row == 5,
                    down(incident[1], 5),
                    jnp.where(row == 6, down(incident[2], 6), 0.0),
                ),
            )
        else:
            last = jnp.zeros(TILE, jnp.float32)
        packed.append(last)
        for t in range(4):
            value = WEIGHT * jnp.where(row < 4, packed[2 * t], packed[2 * t + 1])
            if out is own_ref:
                out[t] = value
            else:
                to_right_ref[t] = jnp.where(odd, 0.0, down(value, -1))
                to_left_ref[t] = jnp.where(odd, down(value, 1), 0.0)


def selector(face_cell):
    column = lax.broadcasted_iota(jnp.int32, (128, 128), 0)
    return (column == face_cell).astype(jnp.float32)


def to_tile(value):
    row = rows() % 4
    low = lanes() < 64
    wide = jnp.broadcast_to(value, TILE)
    return jnp.where(
        jnp.logical_and(row == 0, low),
        wide,
        jnp.where(jnp.logical_and(row == 1, low), along(wide, 64), 0.0),
    )


def wall_kernel(
    kz_ref, stoich_ref, stick_ref, rates_ref, temp_ref, cover_ref, cell_ref, owner_ref,
    surface_ref, sums_ref, wall_x_ref, wall_y_ref,
):
    select = selector(cell_ref[...])
    pieces = jnp.concatenate(
        [cover_ref[...], temp_ref[...], owner_ref[...].astype(jnp.float32),
         jnp.zeros((2, 128), jnp.float32)], axis=0,
    )
    placed = lax.dot_general(
        pieces, select, (((1,), (1,)), ((), ())), precision=PRECISE,
        preferred_element_type=jnp.float32,
    )
    temp = placed[12:13]
    owner = placed[13:14]
    arrhenius = jnp.exp(ACTIVATION * (1.0 - 1.0 / temp))
    zero = jnp.zeros((1, 128), jnp.float32)
    masks = [jnp.abs(owner - float(p)) < 0.5 for p in range(PATCHES)]

    def by_owner(read):
        value = zero
        for p in range(PATCHES):
            value = jnp.where(masks[p], read(p), value)
        return value

    surface_ref[0] = jnp.concatenate([placed[0:12], jnp.zeros((4, 128), jnp.float32)], axis=0)
    desorb = [by_owner(lambda p: rates_ref[p, 0, j]) * arrhenius for j in range(NSURF)]
    lateral = [by_owner(lambda p: rates_ref[p, 1, j]) for j in range(NSURF)]
    stick = [by_owner(lambda p: stick_ref[p, s]) for s in range(S)]
    surface_ref[1] = jnp.concatenate(desorb + [zero] * 4, axis=0)
    surface_ref[2] = jnp.concatenate(lateral + [zero] * 4, axis=0)
    counts = [[stoich_ref[s, j].astype(jnp.float32) for s in range(S)] for j in range(NSURF)]
    for s in range(S):
        column_sum = counts[0][s]
        for j in range(1, NSURF):
            column_sum = column_sum + counts[j][s]
        into = jnp.concatenate(
            [(zero + counts[j][s]) / (zero + (1.0 + column_sum)) * stick[s] for j in range(NSURF)]
            + [zero] * 4, axis=0,
        )
        out = jnp.concatenate(
            [(zero + counts[j][s]) / (zero + (1.0 + counts[j][0] + counts[j][1] + counts[j][2]))
             for j in range(NSURF)]
            + [zero] * 4, axis=0,
        )
        surface_ref[3 + s] = into
        surface_ref[6 + s] = out

    k_rows = lax.broadcasted_iota(jnp.int32, (VG, 128), 0)
    c = speed_of(k_rows)
    up = jnp.maximum(c, 0.0)
    cz = speed_of(kz_ref[0])
    cy = c[VG // 2 :]
    temps = [temp, pltpu.roll(temp, 64, 1)]
    low = lax.broadcasted_iota(jnp.int32, (VG, 128), 1) < 64
    for s in range(S):
        m = SPECIES_MASS[s]
        e = jnp.exp(-m * (c * c) / (2.0 * temp))

        def total(v):
            return jnp.sum(v, axis=0, keepdims=True)

        s0 = total(e)
        s1 = total(c * e)
        s2 = total(c * c * e)
        u1 = total(up * e)
        u2 = total(up * c * e)
        u3 = total(up * c * c * e)
        norm = WEIGHT * u1 * s0 * s0
        scale = WEIGHT * TIME_STEP
        sums_ref[s] = jnp.concatenate(
            [
                1.0 / norm,
                scale * u1 * s0 * s0,
                scale * u1 * s1 * s0,
                scale * u2 * s0 * s0,
                scale * u1 * s0 * s1,
                scale * (u3 * s0 * s0 + u1 * s2 * s0 + u1 * s0 * s2),
                stick[s],
                zero,
            ],
            axis=0,
        )
        for x in range(CX):
            rate = -m / (2.0 * temps[x])
            wall_x_ref[s, x] = jnp.where(low, jnp.exp(rate * (c * c)), 0.0)
            wall_y_ref[s, x] = (cy / jnp.abs(cz)) * jnp.exp(rate * (cy * cy)) * jnp.exp(rate * (cz * cz))


def shift_kernel(s, kz_ref, f_ref, t_ref, z0_ref, z1_ref):
    low = lanes() < 64
    cz = speed_of(kz_ref[0])
    acz = jnp.abs(cz)
    coef_z = TIME_STEP * acz
    octet = speed_of(lax.broadcasted_iota(jnp.int32, TILE, 0))
    coef_x = [jnp.abs(octet + 8.0 * SPACING * q) / acz for q in range(4)]
    source = lax.broadcasted_iota(jnp.int32, (256, 128), 0) % 128
    target = lax.broadcasted_iota(jnp.int32, (256, 128), 1)
    wanted = target // 64 * 64 + (target % 64 + jnp.where(cz > 0.0, 63, 1)) % 64
    turn = (source == wanted).astype(jnp.float32).astype(jnp.bfloat16)

    def along_z(first, to):
        value = f_ref[pl.ds(first, GROUP)].reshape(GROUP * 128, 128)
        high = value.astype(jnp.bfloat16)
        rest = (value - high.astype(jnp.float32)).astype(jnp.bfloat16)
        to[...] = jnp.dot(
            jnp.concatenate([high, rest], axis=1), turn, preferred_element_type=jnp.float32
        )

    def advance(first, lower, z_ref):
        for i in range(GROUP):
            k = first + i
            coef_y = jnp.abs(speed_of(k % VG)) / acz
            own = (1.0 / coef_z - 1.0) - coef_y
            for q in range(4):
                f = [f_ref[k, pl.ds(32 * q + r, 8, 4), :] for r in range(4)]
                far = [along(v, 64) for v in f]
                coef_own = own - coef_x[q]
                for r in range(4):
                    h, x = r // 2, r % 2
                    value = coef_own * f[r] + z_ref[pl.ds(128 * i + 32 * q + r, 8, 4), :]
                    if q < 2 and x == 0:
                        value = value + coef_x[q] * f[r + 1]
                    if q >= 2 and x == 1:
                        value = value + coef_x[q] * f[r - 1]
                    if lower and h == 0:
                        value = value + jnp.where(low, 0.0, coef_y * far[r])
                    elif lower or h == 0:
                        value = value + coef_y * jnp.where(low, far[x], far[x + 2])
                    else:
                        value = value + coef_y * jnp.where(low, far[r], f[r])
                    t_ref[k - s * VG, 32 * r + 8 * q : 32 * r + 8 * q + 8, :] = value

    def one_chunk(c, lower):
        first = s * VG + c * KYS
        after = s * VG + jnp.minimum(c + 1, 3) * KYS
        along_z(first + GROUP, z1_ref)
        advance(first, lower, z0_ref)
        along_z(after, z0_ref)
        advance(first + GROUP, lower, z1_ref)

    along_z(s * VG, z0_ref)
    for lower in (False, True):

        def part(p, carry, lower=lower):
            one_chunk(2 * int(lower) + p, lower)
            return carry

        lax.fori_loop(0, 2, part, 0)


def step_kernel(
    kz_ref, part0_ref, part1_ref, part2_ref, part3_ref, surface_ref, sums_ref, cell_ref,
    wall_x_ref, wall_y_ref, left_ref, right_ref, t0_ref, t1_ref, t2_ref,
    cover_ref, out_hbm,
    out_ref, ex_ref, ey_ref, wy_ref, keep_ref, out_sem,
):
    row = rows()
    totals = []
    for t in range(4):
        totals.append((part0_ref[t] + part1_ref[t]) + (part2_ref[t] + part3_ref[t]))
    incident = [totals[3][4 + s : 5 + s] for s in range(S)]
    start = [surface_ref[0, j : j + 1, :] for j in range(NSURF)]
    desorb = [surface_ref[1, j : j + 1, :] for j in range(NSURF)]
    lateral = [surface_ref[2, j : j + 1, :] for j in range(NSURF)]
    feed = [
        surface_ref[3, j : j + 1, :] * incident[0]
        + surface_ref[4, j : j + 1, :] * incident[1]
        + surface_ref[5, j : j + 1, :] * incident[2]
        for j in range(NSURF)
    ]

    def tree(values):
        values = list(values)
        while len(values) > 1:
            values = [
                values[i] + values[i + 1] if i + 1 < len(values) else values[i]
                for i in range(0, len(values), 2)
            ]
        return values[0]

    def total(v):
        return jnp.sum(v, axis=0, keepdims=True)

    covers = start
    for _ in range(NEWTON):
        vacant = 1.0 - tree(covers)
        scaled, coupling = [], []
        for j in range(NSURF):
            th = covers[j]
            squared = lateral[j] * (th * th)
            net = feed[j] * vacant - desorb[j] * th - squared * th
            residual = th - start[j] - SURFACE_STEP * net
            inverse = 1.0 / (1.0 + SURFACE_STEP * (desorb[j] + 3.0 * squared))
            scaled.append(residual * inverse)
            coupling.append((SURFACE_STEP * feed[j]) * inverse)
        ratio = tree(scaled) / (1.0 + tree(coupling))
        covers = [
            th - DAMPING * (y - u * ratio) for th, y, u in zip(covers, scaled, coupling)
        ]
    released = [
        desorb[j] * covers[j] + lateral[j] * (covers[j] * covers[j] * covers[j])
        for j in range(NSURF)
    ]
    vacant = 1.0 - tree(covers)

    def quantity(q):
        v = totals[q // 2]
        other = down(v, 4)
        return jnp.where(row < 4, v, other) if q % 2 == 0 else jnp.where(row < 4, other, v)

    dens = [quantity(s) for s in range(S)]
    mom = [quantity(3 + a) for a in range(3)]
    energy = quantity(6)
    wall_dens = []
    wall_mom = [0.0, 0.0, 0.0]
    wall_energy = 0.0
    for s in range(S):
        m = SPECIES_MASS[s]
        emitted = incident[s] * (1.0 - sums_ref[s, 6:7] * vacant) + tree(
            [surface_ref[6 + s, j : j + 1, :] * released[j] for j in range(NSURF)]
        )
        wd = emitted * sums_ref[s, 0:1]
        wall_dens.append(wd)
        dens[s] = dens[s] + to_tile(wd * sums_ref[s, 1:2])
        for a in range(3):
            wall_mom[a] = wall_mom[a] + (m * wd) * sums_ref[s, 2 + a : 3 + a]
        wall_energy = wall_energy + (m * wd) * sums_ref[s, 5:6]
    mom = [mom[a] + to_tile(wall_mom[a]) for a in range(3)]
    energy = energy + to_tile(wall_energy)
    gas = dens[0] + dens[1] + dens[2]
    mass = SPECIES_MASS[0] * dens[0] + SPECIES_MASS[1] * dens[1] + SPECIES_MASS[2] * dens[2]
    bulk = [v / mass for v in mom]
    flow = bulk[0] * bulk[0] + bulk[1] * bulk[1] + bulk[2] * bulk[2]
    temperature = (energy - mass * flow) / (3.0 * gas)
    cz = speed_of(kz_ref[0])
    acz = jnp.abs(cz)
    coef_z = TIME_STEP * acz
    grid = speed_of(lax.broadcasted_iota(jnp.int32, (VG, 128), 0))
    for s in range(S):
        rate = -SPECIES_MASS[s] / (2.0 * temperature)
        keep = jnp.exp((-TIME_STEP * COLLISION_RATE[s]) * gas)
        off = cz - bulk[2]
        scale = (1.0 - keep) * dens[s] * jnp.exp(rate * (off * off))
        keep_ref[s] = coef_z * keep
        for r in range(4):
            at = slice(r, r + 1)

            def table(drift):
                gap = grid - drift[at]
                return jnp.exp(rate[at] * (gap * gap))

            ex = table(bulk[0])
            ey = table(bulk[1])
            factor = scale[at] / (WEIGHT * total(ex) * total(ey) * total(table(bulk[2])))
            ex_ref[s, r] = ex
            ey_ref[s, r] = ey * factor
        other = pltpu.roll(wall_dens[s], 64, 1)
        wy_ref[s, 0] = wall_y_ref[s, 0] * wall_dens[s]
        wy_ref[s, 1] = wall_y_ref[s, 1] * other

    octet = speed_of(lax.broadcasted_iota(jnp.int32, TILE, 0))
    coef_x = [jnp.abs(octet + 8.0 * SPACING * q) / acz for q in range(4)]

    def advance(first, s, lower):
        t_ref = (t0_ref, t1_ref, t2_ref)[s]
        keep = [jnp.broadcast_to(keep_ref[s, r : r + 1, :], TILE) for r in range(4)]
        for i in range(GROUP):
            k = first + i
            ky = k - s * VG
            ey = [jnp.broadcast_to(ey_ref[s, r, pl.ds(ky, 1), :], TILE) for r in range(4)]
            if lower:
                wy = [
                    jnp.broadcast_to(wy_ref[s, x, pl.ds(ky - PAIRS, 1), :], TILE)
                    for x in range(CX)
                ]
            for q in range(4):
                for r in range(4):
                    h, x = r // 2, r % 2
                    value = t_ref[ky, 32 * r + 8 * q : 32 * r + 8 * q + 8, :]
                    if q < 2 and x == 1:
                        value = value + coef_x[q] * right_ref[k, pl.ds(16 * h + 8 * q, 8), :]
                    if q >= 2 and x == 0:
                        value = value + coef_x[q] * left_ref[k, pl.ds(16 * h + 8 * (q - 2), 8), :]
                    if lower and h == 0:
                        value = value + wall_x_ref[s, x, 8 * q : 8 * q + 8, :] * wy[x]
                    value = keep[r] * value + ex_ref[s, r, 8 * q : 8 * q + 8, :] * ey[r]
                    out_ref[k, pl.ds(32 * q + r, 8, 4), :] = value

    for s in range(S):
        for lower in (False, True):

            def part(p, carry, s=s, lower=lower):
                g = 8 * s + 4 * int(lower) + p
                advance(g * GROUP, s, lower)
                half_chunk(out_ref, out_hbm, out_sem, g).start()
                return carry

            lax.fori_loop(0, 4, part, 0)
    cover_ref[...] = jnp.dot(
        jnp.concatenate(covers, axis=0), selector(cell_ref[...]), precision=PRECISE,
        preferred_element_type=jnp.float32,
    )
    for c in range(2 * BLOCKS):
        half_chunk(out_ref, out_hbm, out_sem, c).wait()


SMEM = pl.BlockSpec(memory_space=pltpu.SMEM)
VMEM = pl.BlockSpec(memory_space=pltpu.VMEM)
HBM = pl.BlockSpec(memory_space=pl.ANY)
F32 = jnp.float32
BIG = pltpu.CompilerParams(vmem_limit_bytes=16 * 1024 * 1024)
SMALL = pltpu.CompilerParams(vmem_limit_bytes=4 * 1024 * 1024)
DMA = pltpu.SemaphoreType.DMA


def shape(*dims):
    return jax.ShapeDtypeStruct(dims, F32)


def shifted(value, axis, by):
    peers = lax.axis_size(axis)
    return lax.ppermute(value, axis, [(i, (i + by) % peers) for i in range(peers)])


def near(value):
    return pltpu.with_memory_space_constraint(value, pltpu.VMEM)


def moments_call(kz, field):
    return pl.pallas_call(
        moments_kernel,
        in_specs=[SMEM, HBM],
        out_specs=[VMEM] * 6,
        out_shape=[pltpu.VMEM((4, 8, 128), F32)] * 3
        + [pltpu.VMEM((S * VG, 128, 128), F32)]
        + [pltpu.VMEM((S * VG, 32, 128), F32)] * 2,
        scratch_shapes=[
            pltpu.VMEM((S, 20, 8, 128), F32),
            DMA((BLOCKS,)),
        ],
        compiler_params=BIG,
    )(kz, field)


def wall_call(*args):
    return pl.pallas_call(
        wall_kernel,
        in_specs=[SMEM] * 4 + [VMEM] * 4,
        out_specs=[VMEM] * 4,
        out_shape=[
            pltpu.VMEM((9, 16, 128), F32),
            pltpu.VMEM((S, 8, 128), F32),
            pltpu.VMEM((S, CX, VG, 128), F32),
            pltpu.VMEM((S, CX, VG // 2, 128), F32),
        ],
        compiler_params=SMALL,
    )(*args)


def shift_call(s, kz, field):
    return pl.pallas_call(
        functools.partial(shift_kernel, s),
        in_specs=[SMEM, VMEM],
        out_specs=VMEM,
        out_shape=pltpu.VMEM((VG, 128, 128), F32),
        scratch_shapes=[
            pltpu.VMEM((GROUP * 128, 128), F32),
            pltpu.VMEM((GROUP * 128, 128), F32),
        ],
        compiler_params=BIG,
    )(kz, near(field))


def step_call(*args):
    return pl.pallas_call(
        step_kernel,
        in_specs=[SMEM] + [VMEM] * 14,
        out_specs=[VMEM, HBM],
        out_shape=[shape(NSURF, 128), shape(S * VG, 128, 128)],
        scratch_shapes=[
            pltpu.VMEM((S * VG, 128, 128), F32),
            pltpu.VMEM((S, 4, VG, 128), F32),
            pltpu.VMEM((S, 4, VG, 128), F32),
            pltpu.VMEM((S, CX, VG // 2, 128), F32),
            pltpu.VMEM((S, 8, 128), F32),
            DMA((2 * BLOCKS,)),
        ],
        compiler_params=BIG,
    )(*args)


def paired(value, axis):
    peers = lax.axis_size(axis)
    return lax.ppermute(value, axis, [(i, i ^ 1) for i in range(peers)])


def per_device(
    distribution, wall_temp, coverage, face_cell, face_owner, stoichiometry, sticking, surface_rates
):
    kz = lax.axis_index(("z", "x")).astype(jnp.int32).reshape(1)
    field = (
        distribution.reshape(S, VG * VG, CX, 2, 128)
        .transpose(0, 1, 3, 2, 4)
        .reshape(S * VG, 128, 128)
    )
    field = pltpu.with_memory_space_constraint(field, pltpu.HBM)
    own, to_right, to_left, held, rise, fall = moments_call(kz, field)
    together = lax.optimization_barrier
    face_row = face_cell.reshape(1, 128)

    temp, own = together((wall_temp.reshape(1, 128), own))
    walls = wall_call(
        kz, stoichiometry.T, sticking, surface_rates, temp, coverage, face_row,
        face_owner.reshape(1, 128),
    )
    own = own + shifted(to_right, "space", 1) + shifted(to_left, "space", -1)
    own, rise, fall, held, walls = together((own, rise, fall, held, walls))

    from_left = shifted(rise, "space", 1)
    from_right = shifted(fall, "space", -1)
    moved0 = shift_call(0, kz, held)
    own = own + shifted(own, "x", 1) + shifted(own, "x", 3) + shifted(own, "x", 2)
    own, moved0, held = together((own, moved0, held))

    moved1 = shift_call(1, kz, held)
    own = own + paired(own, "z")
    own, moved1, held = together((own, moved1, held))

    moved2 = shift_call(2, kz, held)
    parts = [own, shifted(own, "z", 2), shifted(own, "z", 6), shifted(own, "z", 4)]
    surface, sums, wall_x, wall_y = walls
    vmem = [near(v) for v in parts + [surface, sums]]
    covers, advanced = step_call(
        kz, *vmem, face_row, near(wall_x), near(wall_y), near(from_left), near(from_right),
        near(moved0), near(moved1), near(moved2),
    )
    advanced = (
        advanced.reshape(S, VG * VG, 2, CX, 128)
        .transpose(0, 1, 3, 2, 4)
        .reshape(distribution.shape)
    )
    return advanced, covers


def solution(mesh):
    fine = Mesh(mesh.devices.reshape(N_Z, N_X, mesh.shape["space"]), ("z", "x", "space"))
    return jax.shard_map(
        per_device,
        mesh=fine,
        in_specs=(
            P(None, ("z", "x"), "space", None),
            P("space"),
            P(None, "space"),
            P("space", None),
            P("space"),
            P(),
            P(),
            P(),
        ),
        out_specs=(P(None, ("z", "x"), "space", None), P(None, "space")),
        check_vma=False,
    )
```

```python
import functools

import jax
import jax.numpy as jnp
from jax import lax
from jax.experimental import pallas as pl
from jax.experimental.pallas import tpu as pltpu
from jax.sharding import Mesh
from jax.sharding import PartitionSpec as P

S = 3
VG = 32
NZ = 64
CX = 2
NEWTON = 8
NSURF = 12
PATCHES = 4
N_Z = 8
N_X = 4

SPEED_LIMIT = 4.0
SPACING = 2.0 * SPEED_LIMIT / VG
WEIGHT = SPACING * SPACING * SPACING
SPECIES_MASS = (1.0, 2.0, 4.0)
COLLISION_RATE = (0.3, 0.2, 0.15)
TIME_STEP = 0.08
SURFACE_STEP = 2.0
DAMPING = 0.25
ACTIVATION = 2.0

PAIRS = VG // 2
HALF = PAIRS // 2
BLOCKS = 12
KYS = S * VG // BLOCKS
GROUP = KYS // 2
TILE = (8, 128)
PRECISE = lax.Precision.HIGHEST


def rows():
    return lax.broadcasted_iota(jnp.int32, TILE, 0)


def lanes():
    return lax.broadcasted_iota(jnp.int32, TILE, 1)


def down(value, by):
    return pltpu.roll(value, by % 8, 0)


def along(value, by):
    return pltpu.roll(value, by % 128, 1)


def pair_speed():
    parity = (rows() >= 4).astype(jnp.float32)
    return (parity + 0.5) * SPACING - SPEED_LIMIT


def speed_of(position):
    return (position.astype(jnp.float32) + 0.5) * SPACING - SPEED_LIMIT


def chunk(src, dst, sems, c):
    part = pl.ds(c * KYS, KYS)
    return pltpu.make_async_copy(src.at[part], dst.at[part], sems.at[c])


def half_chunk(src, dst, sems, c):
    part = pl.ds(c * GROUP, GROUP)
    return pltpu.make_async_copy(src.at[part], dst.at[part], sems.at[c])


def moments_kernel(
    f_hbm, own_ref, to_far_ref, to_near_ref, f_ref, far_ref, near_ref, acc_ref, f_sem,
):
    for c in range(BLOCKS):
        chunk(f_hbm, f_ref, f_sem, c).start()
    base = pair_speed()
    speeds = [jnp.abs(base + 2.0 * SPACING * j) for j in range(PAIRS)]
    acc_ref[...] = jnp.zeros_like(acc_ref)
    second = lax.axis_index("space") % 2 == 1
    far_row = jnp.where(second, 65, 0)
    near_row = 65 - far_row

    def one(k, carry):
        zero = jnp.zeros(TILE, jnp.float32)
        sums = []
        for side in range(2):
            n0, n1, n2, n3 = zero, zero, zero, zero
            for j in range(side * HALF, (side + 1) * HALF):
                f = f_ref[k, 8 * j : 8 * j + 8, :]
                g = f * speeds[j]
                n0 = n0 + f
                n1 = n1 + g
                g = g * speeds[j]
                n2 = n2 + g
                n3 = n3 + g * speeds[j]
            sums.append((n0, n1, n2, n3))
        (a0, a1, a2, a3), (b0, b1, b2, b3) = sums
        for h in range(2):
            for q in range(2):
                to = pl.ds(16 * h + 8 * q, 8)
                far_ref[k, to, :] = f_ref[k, pl.ds(far_row + 32 * q + 2 * h, 8, 4), :]
                near_ref[k, to, :] = f_ref[k, pl.ds(near_row + 32 * q + 2 * h, 8, 4), :]
        cy = speed_of(k % VG)
        cy2 = cy * cy
        acy = jnp.abs(cy)
        d = a0 + b0
        x1 = b1 - a1
        e = a2 + b2 + cy2 * d
        yd = cy * d
        new = (
            d, x1, yd, e,
            b1, b2, cy * b1, b3 + cy2 * b1,
            a1, -a2, cy * a1, a3 + cy2 * a1,
            acy * d, acy * x1, acy * yd, acy * e,
        )
        return tuple(c + n for c, n in zip(carry, new))

    start = tuple(jnp.zeros(TILE, jnp.float32) for _ in range(16))
    def turn(c, carry):
        species, half = c // 4, c % 4 // 2
        chunk(f_hbm, f_ref, f_sem, c).wait()
        total = lax.fori_loop(0, KYS, lambda i, v: one(c * KYS + i, v), start, unroll=8)
        for q in range(12):
            acc_ref[species, q] += total[q]
        for q in range(4):
            acc_ref[species, 12 + 4 * half + q] += total[12 + q]
        return carry

    lax.fori_loop(0, BLOCKS, turn, 0)
    row = rows()
    lane = lanes()
    cz = own_speed_z()
    acz = jnp.abs(cz)
    rise = cz > 0.0
    odd = row % 2 == 1
    upper_h = (row // 2) % 2 == 1
    low = lane < 64
    own = []
    rim = []
    incident = []
    for s in range(S):
        full = []
        for q in range(20):
            v = acc_ref[s, q]
            full.append(v + down(v, 4))
        for q in range(4):
            b, xp, xm = full[q], full[4 + q], full[8 + q]
            ym, yp = full[12 + q], full[16 + q]
            zp = jnp.where(lane % 64 == 0, along(b, 65), along(b, 1))
            zm = jnp.where(lane % 64 == 63, along(b, 63), along(b, 127))
            shifted_z = jnp.where(rise, zp, zm)
            rp = along(yp, 64)
            rm = along(ym, 64)
            from_low = jnp.where(low, jnp.where(upper_h, down(rp, 2), 0.0), rp)
            from_high = jnp.where(low, rm, jnp.where(upper_h, ym, down(rm, -2)))
            inner = jnp.where(odd, down(xp, 1), down(xm, -1))
            stay = (1.0 - TIME_STEP * acz) * b - TIME_STEP * (xp + xm + yp + ym)
            own.append(
                stay
                + TIME_STEP * (acz * shifted_z + from_low + from_high + inner)
            )
            rim.append(TIME_STEP * jnp.where(odd, xp, xm))
        ym = full[12]
        incident.append(jnp.where(low, ym, along(down(ym, -1), 64)))
    for values, out in ((own, own_ref), (rim, None)):
        packed = [values[0], values[4], values[8]]
        momenta = [0.0, 0.0, 0.0, 0.0]
        for s in range(S):
            m = SPECIES_MASS[s]
            d, px, py, e = values[4 * s : 4 * s + 4]
            momenta[0] = momenta[0] + m * px
            momenta[1] = momenta[1] + m * py
            momenta[2] = momenta[2] + (m * cz) * d
            momenta[3] = momenta[3] + m * (e + cz * cz * d)
        packed = packed + momenta
        if out is own_ref:
            last = jnp.where(
                row == 4,
                down(incident[0], 4),
                jnp.where(
                    row == 5,
                    down(incident[1], 5),
                    jnp.where(row == 6, down(incident[2], 6), 0.0),
                ),
            )
        else:
            last = jnp.zeros(TILE, jnp.float32)
        packed.append(last)
        for t in range(4):
            value = WEIGHT * jnp.where(row < 4, packed[2 * t], packed[2 * t + 1])
            if out is own_ref:
                out[t] = value
            else:
                to_right = jnp.where(odd, 0.0, down(value, -1))
                to_left = jnp.where(odd, down(value, 1), 0.0)
                to_far_ref[t] = jnp.where(second, to_right, to_left)
                to_near_ref[t] = jnp.where(second, to_left, to_right)


def own_speed_z():
    return speed_of(lax.axis_index("z") * lax.axis_size("x") + lax.axis_index("x"))


def selector(face_cell):
    column = lax.broadcasted_iota(jnp.int32, (128, 128), 0)
    return (column == face_cell).astype(jnp.float32)


def to_tile(value):
    row = rows() % 4
    low = lanes() < 64
    wide = jnp.broadcast_to(value, TILE)
    return jnp.where(
        jnp.logical_and(row == 0, low),
        wide,
        jnp.where(jnp.logical_and(row == 1, low), along(wide, 64), 0.0),
    )


def wall_kernel(
    stoich_ref, stick_ref, rates_ref, temp_ref, cover_ref, cell_ref, owner_ref,
    surface_ref, sums_ref, wall_x_ref, wall_y_ref,
):
    select = selector(cell_ref[...])
    pieces = jnp.concatenate(
        [cover_ref[...], temp_ref[...], owner_ref[...].astype(jnp.float32),
         jnp.zeros((2, 128), jnp.float32)], axis=0,
    )
    placed = lax.dot_general(
        pieces, select, (((1,), (1,)), ((), ())), precision=PRECISE,
        preferred_element_type=jnp.float32,
    )
    temp = placed[12:13]
    owner = placed[13:14]
    arrhenius = jnp.exp(ACTIVATION * (1.0 - 1.0 / temp))
    zero = jnp.zeros((1, 128), jnp.float32)
    masks = [jnp.abs(owner - float(p)) < 0.5 for p in range(PATCHES)]

    def by_owner(read):
        value = zero
        for p in range(PATCHES):
            value = jnp.where(masks[p], read(p), value)
        return value

    surface_ref[0] = jnp.concatenate([placed[0:12], jnp.zeros((4, 128), jnp.float32)], axis=0)
    desorb = [by_owner(lambda p: rates_ref[p, 0, j]) * arrhenius for j in range(NSURF)]
    lateral = [by_owner(lambda p: rates_ref[p, 1, j]) for j in range(NSURF)]
    stick = [by_owner(lambda p: stick_ref[p, s]) for s in range(S)]
    surface_ref[1] = jnp.concatenate(desorb + [zero] * 4, axis=0)
    surface_ref[2] = jnp.concatenate(lateral + [zero] * 4, axis=0)
    counts = [[stoich_ref[s, j].astype(jnp.float32) for s in range(S)] for j in range(NSURF)]
    for s in range(S):
        column_sum = counts[0][s]
        for j in range(1, NSURF):
            column_sum = column_sum + counts[j][s]
        into = jnp.concatenate(
            [(zero + counts[j][s]) / (zero + (1.0 + column_sum)) * stick[s] for j in range(NSURF)]
            + [zero] * 4, axis=0,
        )
        out = jnp.concatenate(
            [(zero + counts[j][s]) / (zero + (1.0 + counts[j][0] + counts[j][1] + counts[j][2]))
             for j in range(NSURF)]
            + [zero] * 4, axis=0,
        )
        surface_ref[3 + s] = into
        surface_ref[6 + s] = out

    k_rows = lax.broadcasted_iota(jnp.int32, (VG, 128), 0)
    c = speed_of(k_rows)
    up = jnp.maximum(c, 0.0)
    cz = own_speed_z()
    cy = c[VG // 2 :]
    temps = [temp, pltpu.roll(temp, 64, 1)]
    low = lax.broadcasted_iota(jnp.int32, (VG, 128), 1) < 64
    for s in range(S):
        m = SPECIES_MASS[s]
        e = jnp.exp(-m * (c * c) / (2.0 * temp))

        def total(v):
            return jnp.sum(v, axis=0, keepdims=True)

        s0 = total(e)
        s1 = total(c * e)
        s2 = total(c * c * e)
        u1 = total(up * e)
        u2 = total(up * c * e)
        u3 = total(up * c * c * e)
        norm = WEIGHT * u1 * s0 * s0
        scale = WEIGHT * TIME_STEP
        sums_ref[s] = jnp.concatenate(
            [
                1.0 / norm,
                scale * u1 * s0 * s0,
                scale * u1 * s1 * s0,
                scale * u2 * s0 * s0,
                scale * u1 * s0 * s1,
                scale * (u3 * s0 * s0 + u1 * s2 * s0 + u1 * s0 * s2),
                stick[s],
                zero,
            ],
            axis=0,
        )
        for x in range(CX):
            rate = -m / (2.0 * temps[x])
            wall_x_ref[s, x] = jnp.where(low, jnp.exp(rate * (c * c)), 0.0)
            wall_y_ref[s, x] = (cy / jnp.abs(cz)) * jnp.exp(rate * (cy * cy)) * jnp.exp(rate * (cz * cz))


def shift_kernel(s, f_ref, t_ref, z0_ref, z1_ref):
    low = lanes() < 64
    cz = own_speed_z()
    acz = jnp.abs(cz)
    coef_z = TIME_STEP * acz
    octet = speed_of(lax.broadcasted_iota(jnp.int32, TILE, 0))
    coef_x = [jnp.abs(octet + 8.0 * SPACING * q) / acz for q in range(4)]
    source = lax.broadcasted_iota(jnp.int32, (256, 128), 0) % 128
    target = lax.broadcasted_iota(jnp.int32, (256, 128), 1)
    wanted = target // 64 * 64 + (target % 64 + jnp.where(cz > 0.0, 63, 1)) % 64
    turn = (source == wanted).astype(jnp.float32).astype(jnp.bfloat16)

    def along_z(first, to):
        value = f_ref[pl.ds(first, GROUP)].reshape(GROUP * 128, 128)
        high = value.astype(jnp.bfloat16)
        rest = (value - high.astype(jnp.float32)).astype(jnp.bfloat16)
        to[...] = jnp.dot(
            jnp.concatenate([high, rest], axis=1), turn, preferred_element_type=jnp.float32
        )

    def advance(first, lower, z_ref):
        for i in range(GROUP):
            k = first + i
            coef_y = jnp.abs(speed_of(k % VG)) / acz
            own = (1.0 / coef_z - 1.0) - coef_y
            for q in range(4):
                f = [f_ref[k, pl.ds(32 * q + r, 8, 4), :] for r in range(4)]
                far = [along(v, 64) for v in f]
                coef_own = own - coef_x[q]
                for r in range(4):
                    h, x = r // 2, r % 2
                    value = coef_own * f[r] + z_ref[pl.ds(128 * i + 32 * q + r, 8, 4), :]
                    if q < 2 and x == 0:
                        value = value + coef_x[q] * f[r + 1]
                    if q >= 2 and x == 1:
                        value = value + coef_x[q] * f[r - 1]
                    if lower and h == 0:
                        value = value + jnp.where(low, 0.0, coef_y * far[r])
                    elif lower or h == 0:
                        value = value + coef_y * jnp.where(low, far[x], far[x + 2])
                    else:
                        value = value + coef_y * jnp.where(low, far[r], f[r])
                    t_ref[k - s * VG, 32 * r + 8 * q : 32 * r + 8 * q + 8, :] = value

    def one_chunk(c, lower):
        first = s * VG + c * KYS
        after = s * VG + jnp.minimum(c + 1, 3) * KYS
        along_z(first + GROUP, z1_ref)
        advance(first, lower, z0_ref)
        along_z(after, z0_ref)
        advance(first + GROUP, lower, z1_ref)

    along_z(s * VG, z0_ref)
    for lower in (False, True):

        def part(p, carry, lower=lower):
            one_chunk(2 * int(lower) + p, lower)
            return carry

        lax.fori_loop(0, 2, part, 0)


def step_kernel(
    part0_ref, part1_ref, part2_ref, part3_ref, surface_ref, sums_ref, cell_ref,
    wall_x_ref, wall_y_ref, far_ref, near_ref, t0_ref, t1_ref, t2_ref,
    cover_ref, out_hbm,
    out_ref, ex_ref, ey_ref, wy_ref, keep_ref, out_sem,
):
    row = rows()
    totals = []
    for t in range(4):
        totals.append((part0_ref[t] + part1_ref[t]) + (part2_ref[t] + part3_ref[t]))
    incident = [totals[3][4 + s : 5 + s] for s in range(S)]
    start = [surface_ref[0, j : j + 1, :] for j in range(NSURF)]
    desorb = [surface_ref[1, j : j + 1, :] for j in range(NSURF)]
    lateral = [surface_ref[2, j : j + 1, :] for j in range(NSURF)]
    feed = [
        surface_ref[3, j : j + 1, :] * incident[0]
        + surface_ref[4, j : j + 1, :] * incident[1]
        + surface_ref[5, j : j + 1, :] * incident[2]
        for j in range(NSURF)
    ]

    def tree(values):
        values = list(values)
        while len(values) > 1:
            values = [
                values[i] + values[i + 1] if i + 1 < len(values) else values[i]
                for i in range(0, len(values), 2)
            ]
        return values[0]

    def total(v):
        return jnp.sum(v, axis=0, keepdims=True)

    covers = start
    for _ in range(NEWTON):
        vacant = 1.0 - tree(covers)
        scaled, coupling = [], []
        for j in range(NSURF):
            th = covers[j]
            squared = lateral[j] * (th * th)
            net = feed[j] * vacant - desorb[j] * th - squared * th
            residual = th - start[j] - SURFACE_STEP * net
            inverse = 1.0 / (1.0 + SURFACE_STEP * (desorb[j] + 3.0 * squared))
            scaled.append(residual * inverse)
            coupling.append((SURFACE_STEP * feed[j]) * inverse)
        ratio = tree(scaled) / (1.0 + tree(coupling))
        covers = [
            th - DAMPING * (y - u * ratio) for th, y, u in zip(covers, scaled, coupling)
        ]
    released = [
        desorb[j] * covers[j] + lateral[j] * (covers[j] * covers[j] * covers[j])
        for j in range(NSURF)
    ]
    vacant = 1.0 - tree(covers)

    def quantity(q):
        v = totals[q // 2]
        other = down(v, 4)
        return jnp.where(row < 4, v, other) if q % 2 == 0 else jnp.where(row < 4, other, v)

    dens = [quantity(s) for s in range(S)]
    mom = [quantity(3 + a) for a in range(3)]
    energy = quantity(6)
    wall_dens = []
    wall_mom = [0.0, 0.0, 0.0]
    wall_energy = 0.0
    for s in range(S):
        m = SPECIES_MASS[s]
        emitted = incident[s] * (1.0 - sums_ref[s, 6:7] * vacant) + tree(
            [surface_ref[6 + s, j : j + 1, :] * released[j] for j in range(NSURF)]
        )
        wd = emitted * sums_ref[s, 0:1]
        wall_dens.append(wd)
        dens[s] = dens[s] + to_tile(wd * sums_ref[s, 1:2])
        for a in range(3):
            wall_mom[a] = wall_mom[a] + (m * wd) * sums_ref[s, 2 + a : 3 + a]
        wall_energy = wall_energy + (m * wd) * sums_ref[s, 5:6]
    mom = [mom[a] + to_tile(wall_mom[a]) for a in range(3)]
    energy = energy + to_tile(wall_energy)
    gas = dens[0] + dens[1] + dens[2]
    mass = SPECIES_MASS[0] * dens[0] + SPECIES_MASS[1] * dens[1] + SPECIES_MASS[2] * dens[2]
    bulk = [v / mass for v in mom]
    flow = bulk[0] * bulk[0] + bulk[1] * bulk[1] + bulk[2] * bulk[2]
    temperature = (energy - mass * flow) / (3.0 * gas)
    cz = own_speed_z()
    acz = jnp.abs(cz)
    coef_z = TIME_STEP * acz
    grid = speed_of(lax.broadcasted_iota(jnp.int32, (VG, 128), 0))
    for s in range(S):
        rate = -SPECIES_MASS[s] / (2.0 * temperature)
        keep = jnp.exp((-TIME_STEP * COLLISION_RATE[s]) * gas)
        off = cz - bulk[2]
        scale = (1.0 - keep) * dens[s] * jnp.exp(rate * (off * off))
        keep_ref[s] = coef_z * keep
        for r in range(4):
            at = slice(r, r + 1)

            def table(drift):
                gap = grid - drift[at]
                return jnp.exp(rate[at] * (gap * gap))

            ex = table(bulk[0])
            ey = table(bulk[1])
            factor = scale[at] / (WEIGHT * total(ex) * total(ey) * total(table(bulk[2])))
            ex_ref[s, r] = ex
            ey_ref[s, r] = ey * factor
        other = pltpu.roll(wall_dens[s], 64, 1)
        wy_ref[s, 0] = wall_y_ref[s, 0] * wall_dens[s]
        wy_ref[s, 1] = wall_y_ref[s, 1] * other

    octet = speed_of(lax.broadcasted_iota(jnp.int32, TILE, 0))
    coef_x = [jnp.abs(octet + 8.0 * SPACING * q) / acz for q in range(4)]
    second = lax.axis_index("space") % 2 == 1

    def advance(first, s, lower):
        t_ref = (t0_ref, t1_ref, t2_ref)[s]
        keep = [jnp.broadcast_to(keep_ref[s, r : r + 1, :], TILE) for r in range(4)]
        for i in range(GROUP):
            k = first + i
            ky = k - s * VG
            ey = [jnp.broadcast_to(ey_ref[s, r, pl.ds(ky, 1), :], TILE) for r in range(4)]
            if lower:
                wy = [
                    jnp.broadcast_to(wy_ref[s, x, pl.ds(ky - PAIRS, 1), :], TILE)
                    for x in range(CX)
                ]
            for q in range(4):
                for r in range(4):
                    h, x = r // 2, r % 2
                    value = t_ref[ky, 32 * r + 8 * q : 32 * r + 8 * q + 8, :]
                    at = pl.ds(16 * h + 8 * (q % 2), 8)
                    if q < 2 and x == 1:
                        beside = jnp.where(second, far_ref[k, at, :], near_ref[k, at, :])
                        value = value + coef_x[q] * beside
                    if q >= 2 and x == 0:
                        beside = jnp.where(second, near_ref[k, at, :], far_ref[k, at, :])
                        value = value + coef_x[q] * beside
                    if lower and h == 0:
                        value = value + wall_x_ref[s, x, 8 * q : 8 * q + 8, :] * wy[x]
                    value = keep[r] * value + ex_ref[s, r, 8 * q : 8 * q + 8, :] * ey[r]
                    out_ref[k, pl.ds(32 * q + r, 8, 4), :] = value

    for s in range(S):
        for lower in (False, True):

            def part(p, carry, s=s, lower=lower):
                g = 8 * s + 4 * int(lower) + p
                advance(g * GROUP, s, lower)
                half_chunk(out_ref, out_hbm, out_sem, g).start()
                return carry

            lax.fori_loop(0, 4, part, 0)
    cover_ref[...] = jnp.dot(
        jnp.concatenate(covers, axis=0), selector(cell_ref[...]), precision=PRECISE,
        preferred_element_type=jnp.float32,
    )
    for c in range(2 * BLOCKS):
        half_chunk(out_ref, out_hbm, out_sem, c).wait()


SMEM = pl.BlockSpec(memory_space=pltpu.SMEM)
VMEM = pl.BlockSpec(memory_space=pltpu.VMEM)
HBM = pl.BlockSpec(memory_space=pl.ANY)
F32 = jnp.float32
BIG = pltpu.CompilerParams(vmem_limit_bytes=16 * 1024 * 1024)
SMALL = pltpu.CompilerParams(vmem_limit_bytes=4 * 1024 * 1024)
DMA = pltpu.SemaphoreType.DMA
LONG = pl.CostEstimate(flops=10**10, bytes_accessed=10**7, transcendentals=0)


def shape(*dims):
    return jax.ShapeDtypeStruct(dims, F32)


def shifted(value, axis, by):
    peers = lax.axis_size(axis)
    return lax.ppermute(value, axis, [(i, (i + by) % peers) for i in range(peers)])


def near(value):
    return pltpu.with_memory_space_constraint(value, pltpu.VMEM)


def moments_call(field):
    return pl.pallas_call(
        moments_kernel,
        in_specs=[HBM],
        out_specs=[VMEM] * 6,
        out_shape=[pltpu.VMEM((4, 8, 128), F32)] * 3
        + [pltpu.VMEM((S * VG, 128, 128), F32)]
        + [pltpu.VMEM((S * VG, 32, 128), F32)] * 2,
        scratch_shapes=[
            pltpu.VMEM((S, 20, 8, 128), F32),
            DMA((BLOCKS,)),
        ],
        compiler_params=BIG,
    )(field)


def wall_call(*args):
    return pl.pallas_call(
        wall_kernel,
        in_specs=[SMEM] * 3 + [VMEM] * 4,
        out_specs=[VMEM] * 4,
        out_shape=[
            pltpu.VMEM((9, 16, 128), F32),
            pltpu.VMEM((S, 8, 128), F32),
            pltpu.VMEM((S, CX, VG, 128), F32),
            pltpu.VMEM((S, CX, VG // 2, 128), F32),
        ],
        compiler_params=SMALL,
    )(*args)


def shift_call(s, field):
    return pl.pallas_call(
        functools.partial(shift_kernel, s),
        in_specs=[VMEM],
        out_specs=VMEM,
        out_shape=pltpu.VMEM((VG, 128, 128), F32),
        scratch_shapes=[
            pltpu.VMEM((GROUP * 128, 128), F32),
            pltpu.VMEM((GROUP * 128, 128), F32),
        ],
        compiler_params=BIG,
        cost_estimate=LONG,
    )(near(field))


def step_call(*args):
    return pl.pallas_call(
        step_kernel,
        in_specs=[VMEM] * 14,
        out_specs=[VMEM, HBM],
        out_shape=[shape(NSURF, 128), shape(S * VG, 128, 128)],
        scratch_shapes=[
            pltpu.VMEM((S * VG, 128, 128), F32),
            pltpu.VMEM((S, 4, VG, 128), F32),
            pltpu.VMEM((S, 4, VG, 128), F32),
            pltpu.VMEM((S, CX, VG // 2, 128), F32),
            pltpu.VMEM((S, 8, 128), F32),
            DMA((2 * BLOCKS,)),
        ],
        compiler_params=BIG,
    )(*args)


def paired(value, axis):
    peers = lax.axis_size(axis)
    return lax.ppermute(value, axis, [(i, i ^ 1) for i in range(peers)])


def crossed(value, axis, by):
    peers = lax.axis_size(axis)
    pairs = [(i, (i + (by if i % 2 else -by)) % peers) for i in range(peers)]
    return lax.ppermute(value, axis, pairs)


def per_device(
    distribution, wall_temp, coverage, face_cell, face_owner, stoichiometry, sticking, surface_rates
):
    field = (
        distribution.reshape(S, VG * VG, CX, 2, 128)
        .transpose(0, 1, 3, 2, 4)
        .reshape(S * VG, 128, 128)
    )
    field = pltpu.with_memory_space_constraint(field, pltpu.HBM)
    own, to_far, to_near, held, far, nigh = moments_call(field)
    together = lax.optimization_barrier
    face_row = face_cell.reshape(1, 128)

    temp, own = together((wall_temp.reshape(1, 128), own))
    walls = wall_call(
        stoichiometry.T, sticking, surface_rates, temp, coverage, face_row,
        face_owner.reshape(1, 128),
    )
    own = own + crossed(to_far, "space", 1) + paired(to_near, "space")
    own, held, walls = together((own, held, walls))

    far = crossed(near(far), "space", 1)
    nigh = paired(near(nigh), "space")
    moved0 = shift_call(0, held)
    own = own + shifted(own, "x", 1) + shifted(own, "x", 3) + shifted(own, "x", 2)
    own, moved0, held = together((own, moved0, held))

    moved1 = shift_call(1, held)
    own = own + paired(own, "z")
    own, moved1, held = together((own, moved1, held))

    moved2 = shift_call(2, held)
    parts = [own] + [crossed(own, "z", by) for by in (1, 2, 3)]
    surface, sums, wall_x, wall_y = walls
    vmem = [near(v) for v in parts + [surface, sums]]
    covers, advanced = step_call(
        *vmem, face_row, near(wall_x), near(wall_y), near(far), near(nigh),
        near(moved0), near(moved1), near(moved2),
    )
    advanced = (
        advanced.reshape(S, VG * VG, 2, CX, 128)
        .transpose(0, 1, 3, 2, 4)
        .reshape(distribution.shape)
    )
    return advanced, covers


def solution(mesh):
    fine = Mesh(mesh.devices.reshape(N_Z, N_X, mesh.shape["space"]), ("z", "x", "space"))
    return jax.shard_map(
        per_device,
        mesh=fine,
        in_specs=(
            P(None, ("z", "x"), "space", None),
            P("space"),
            P(None, "space"),
            P("space", None),
            P("space"),
            P(),
            P(),
            P(),
        ),
        out_specs=(P(None, ("z", "x"), "space", None), P(None, "space")),
        check_vma=False,
    )
```

```python
import functools

import jax
import jax.numpy as jnp
from jax import lax
from jax.experimental import pallas as pl
from jax.experimental.pallas import tpu as pltpu
from jax.sharding import Mesh
from jax.sharding import PartitionSpec as P

S = 3
VG = 32
NZ = 64
CX = 2
NEWTON = 8
NSURF = 12
PATCHES = 4
N_Z = 8
N_X = 4

SPEED_LIMIT = 4.0
SPACING = 2.0 * SPEED_LIMIT / VG
WEIGHT = SPACING * SPACING * SPACING
SPECIES_MASS = (1.0, 2.0, 4.0)
COLLISION_RATE = (0.3, 0.2, 0.15)
TIME_STEP = 0.08
SURFACE_STEP = 2.0
DAMPING = 0.25
ACTIVATION = 2.0

PAIRS = VG // 2
HALF = PAIRS // 2
BLOCKS = 12
KYS = S * VG // BLOCKS
GROUP = KYS // 2
TILE = (8, 128)
PRECISE = lax.Precision.HIGHEST


def rows():
    return lax.broadcasted_iota(jnp.int32, TILE, 0)


def lanes():
    return lax.broadcasted_iota(jnp.int32, TILE, 1)


def down(value, by):
    return pltpu.roll(value, by % 8, 0)


def along(value, by):
    return pltpu.roll(value, by % 128, 1)


def pair_speed():
    parity = (rows() >= 4).astype(jnp.float32)
    return (parity + 0.5) * SPACING - SPEED_LIMIT


def speed_of(position):
    return (position.astype(jnp.float32) + 0.5) * SPACING - SPEED_LIMIT


def chunk(src, dst, sems, c):
    part = pl.ds(c * KYS, KYS)
    return pltpu.make_async_copy(src.at[part], dst.at[part], sems.at[c])


def half_chunk(src, dst, sems, c):
    part = pl.ds(c * GROUP, GROUP)
    return pltpu.make_async_copy(src.at[part], dst.at[part], sems.at[c])


def moments_kernel(
    f_hbm, own_ref, to_far_ref, to_near_ref, f_ref, far_ref, near_ref, acc_ref, f_sem,
):
    for c in range(BLOCKS):
        chunk(f_hbm, f_ref, f_sem, c).start()
    base = pair_speed()
    speeds = [jnp.abs(base + 2.0 * SPACING * j) for j in range(PAIRS)]
    acc_ref[...] = jnp.zeros_like(acc_ref)
    second = lax.axis_index("space") % 2 == 1
    far_row = jnp.where(second, 65, 0)
    near_row = 65 - far_row

    def one(k, carry):
        zero = jnp.zeros(TILE, jnp.float32)
        sums = []
        for side in range(2):
            n0, n1, n2, n3 = zero, zero, zero, zero
            for j in range(side * HALF, (side + 1) * HALF):
                f = f_ref[k, 8 * j : 8 * j + 8, :]
                g = f * speeds[j]
                n0 = n0 + f
                n1 = n1 + g
                g = g * speeds[j]
                n2 = n2 + g
                n3 = n3 + g * speeds[j]
            sums.append((n0, n1, n2, n3))
        (a0, a1, a2, a3), (b0, b1, b2, b3) = sums
        for h in range(2):
            for q in range(2):
                to = pl.ds(16 * h + 8 * q, 8)
                far_ref[k, to, :] = f_ref[k, pl.ds(far_row + 32 * q + 2 * h, 8, 4), :]
                near_ref[k, to, :] = f_ref[k, pl.ds(near_row + 32 * q + 2 * h, 8, 4), :]
        cy = speed_of(k % VG)
        cy2 = cy * cy
        acy = jnp.abs(cy)
        d = a0 + b0
        x1 = b1 - a1
        e = a2 + b2 + cy2 * d
        yd = cy * d
        new = (
            d, x1, yd, e,
            b1, b2, cy * b1, b3 + cy2 * b1,
            a1, -a2, cy * a1, a3 + cy2 * a1,
            acy * d, acy * x1, acy * yd, acy * e,
        )
        return tuple(c + n for c, n in zip(carry, new))

    start = tuple(jnp.zeros(TILE, jnp.float32) for _ in range(16))
    def turn(c, carry):
        species, half = c // 4, c % 4 // 2
        chunk(f_hbm, f_ref, f_sem, c).wait()
        total = lax.fori_loop(0, KYS, lambda i, v: one(c * KYS + i, v), start, unroll=8)
        for q in range(12):
            acc_ref[species, q] += total[q]
        for q in range(4):
            acc_ref[species, 12 + 4 * half + q] += total[12 + q]
        return carry

    lax.fori_loop(0, BLOCKS, turn, 0)
    row = rows()
    lane = lanes()
    cz = own_speed_z()
    acz = jnp.abs(cz)
    rise = cz > 0.0
    odd = row % 2 == 1
    upper_h = (row // 2) % 2 == 1
    low = lane < 64
    own = []
    rim = []
    incident = []
    for s in range(S):
        full = []
        for q in range(20):
            v = acc_ref[s, q]
            full.append(v + down(v, 4))
        for q in range(4):
            b, xp, xm = full[q], full[4 + q], full[8 + q]
            ym, yp = full[12 + q], full[16 + q]
            zp = jnp.where(lane % 64 == 0, along(b, 65), along(b, 1))
            zm = jnp.where(lane % 64 == 63, along(b, 63), along(b, 127))
            shifted_z = jnp.where(rise, zp, zm)
            rp = along(yp, 64)
            rm = along(ym, 64)
            from_low = jnp.where(low, jnp.where(upper_h, down(rp, 2), 0.0), rp)
            from_high = jnp.where(low, rm, jnp.where(upper_h, ym, down(rm, -2)))
            inner = jnp.where(odd, down(xp, 1), down(xm, -1))
            stay = (1.0 - TIME_STEP * acz) * b - TIME_STEP * (xp + xm + yp + ym)
            own.append(
                stay
                + TIME_STEP * (acz * shifted_z + from_low + from_high + inner)
            )
            rim.append(TIME_STEP * jnp.where(odd, xp, xm))
        ym = full[12]
        incident.append(jnp.where(low, ym, along(down(ym, -1), 64)))
    for values, out in ((own, own_ref), (rim, None)):
        packed = [values[0], values[4], values[8]]
        momenta = [0.0, 0.0, 0.0, 0.0]
        for s in range(S):
            m = SPECIES_MASS[s]
            d, px, py, e = values[4 * s : 4 * s + 4]
            momenta[0] = momenta[0] + m * px
            momenta[1] = momenta[1] + m * py
            momenta[2] = momenta[2] + (m * cz) * d
            momenta[3] = momenta[3] + m * (e + cz * cz * d)
        packed = packed + momenta
        if out is own_ref:
            last = jnp.where(
                row == 4,
                down(incident[0], 4),
                jnp.where(
                    row == 5,
                    down(incident[1], 5),
                    jnp.where(row == 6, down(incident[2], 6), 0.0),
                ),
            )
        else:
            last = jnp.zeros(TILE, jnp.float32)
        packed.append(last)
        for t in range(4):
            value = WEIGHT * jnp.where(row < 4, packed[2 * t], packed[2 * t + 1])
            if out is own_ref:
                out[t] = value
            else:
                to_right = jnp.where(odd, 0.0, down(value, -1))
                to_left = jnp.where(odd, down(value, 1), 0.0)
                to_far_ref[t] = jnp.where(second, to_right, to_left)
                to_near_ref[t] = jnp.where(second, to_left, to_right)


def own_speed_z():
    return speed_of(lax.axis_index("z") * lax.axis_size("x") + lax.axis_index("x"))


def selector(face_cell):
    column = lax.broadcasted_iota(jnp.int32, (128, 128), 0)
    return (column == face_cell).astype(jnp.float32)


def to_tile(value):
    row = rows() % 4
    low = lanes() < 64
    wide = jnp.broadcast_to(value, TILE)
    return jnp.where(
        jnp.logical_and(row == 0, low),
        wide,
        jnp.where(jnp.logical_and(row == 1, low), along(wide, 64), 0.0),
    )


def wall_kernel(
    stoich_ref, stick_ref, rates_ref, temp_ref, cover_ref, cell_ref, owner_ref,
    surface_ref, sums_ref, wall_x_ref, wall_y_ref,
):
    select = selector(cell_ref[...])
    pieces = jnp.concatenate(
        [cover_ref[...], temp_ref[...], owner_ref[...].astype(jnp.float32),
         jnp.zeros((2, 128), jnp.float32)], axis=0,
    )
    placed = lax.dot_general(
        pieces, select, (((1,), (1,)), ((), ())), precision=PRECISE,
        preferred_element_type=jnp.float32,
    )
    temp = placed[12:13]
    owner = placed[13:14]
    arrhenius = jnp.exp(ACTIVATION * (1.0 - 1.0 / temp))
    zero = jnp.zeros((1, 128), jnp.float32)
    masks = [jnp.abs(owner - float(p)) < 0.5 for p in range(PATCHES)]

    def by_owner(read):
        value = zero
        for p in range(PATCHES):
            value = jnp.where(masks[p], read(p), value)
        return value

    surface_ref[0] = jnp.concatenate([placed[0:12], jnp.zeros((4, 128), jnp.float32)], axis=0)
    desorb = [by_owner(lambda p: rates_ref[p, 0, j]) * arrhenius for j in range(NSURF)]
    lateral = [by_owner(lambda p: rates_ref[p, 1, j]) for j in range(NSURF)]
    stick = [by_owner(lambda p: stick_ref[p, s]) for s in range(S)]
    surface_ref[1] = jnp.concatenate(desorb + [zero] * 4, axis=0)
    surface_ref[2] = jnp.concatenate(lateral + [zero] * 4, axis=0)
    counts = [[stoich_ref[s, j].astype(jnp.float32) for s in range(S)] for j in range(NSURF)]
    for s in range(S):
        column_sum = counts[0][s]
        for j in range(1, NSURF):
            column_sum = column_sum + counts[j][s]
        into = jnp.concatenate(
            [(zero + counts[j][s]) / (zero + (1.0 + column_sum)) * stick[s] for j in range(NSURF)]
            + [zero] * 4, axis=0,
        )
        out = jnp.concatenate(
            [(zero + counts[j][s]) / (zero + (1.0 + counts[j][0] + counts[j][1] + counts[j][2]))
             for j in range(NSURF)]
            + [zero] * 4, axis=0,
        )
        surface_ref[3 + s] = into
        surface_ref[6 + s] = out

    k_rows = lax.broadcasted_iota(jnp.int32, (VG, 128), 0)
    c = speed_of(k_rows)
    up = jnp.maximum(c, 0.0)
    cz = own_speed_z()
    cy = c[VG // 2 :]
    temps = [temp, pltpu.roll(temp, 64, 1)]
    low = lax.broadcasted_iota(jnp.int32, (VG, 128), 1) < 64
    for s in range(S):
        m = SPECIES_MASS[s]
        e = jnp.exp(-m * (c * c) / (2.0 * temp))

        def total(v):
            return jnp.sum(v, axis=0, keepdims=True)

        s0 = total(e)
        s1 = total(c * e)
        s2 = total(c * c * e)
        u1 = total(up * e)
        u2 = total(up * c * e)
        u3 = total(up * c * c * e)
        norm = WEIGHT * u1 * s0 * s0
        scale = WEIGHT * TIME_STEP
        sums_ref[s] = jnp.concatenate(
            [
                1.0 / norm,
                scale * u1 * s0 * s0,
                scale * u1 * s1 * s0,
                scale * u2 * s0 * s0,
                scale * u1 * s0 * s1,
                scale * (u3 * s0 * s0 + u1 * s2 * s0 + u1 * s0 * s2),
                stick[s],
                zero,
            ],
            axis=0,
        )
        for x in range(CX):
            rate = -m / (2.0 * temps[x])
            wall_x_ref[s, x] = jnp.where(low, jnp.exp(rate * (c * c)), 0.0)
            wall_y_ref[s, x] = (cy / jnp.abs(cz)) * jnp.exp(rate * (cy * cy)) * jnp.exp(rate * (cz * cz))


def shift_kernel(s, f_ref, t_ref, z0_ref, z1_ref):
    low = lanes() < 64
    cz = own_speed_z()
    acz = jnp.abs(cz)
    coef_z = TIME_STEP * acz
    octet = speed_of(lax.broadcasted_iota(jnp.int32, TILE, 0))
    coef_x = [jnp.abs(octet + 8.0 * SPACING * q) / acz for q in range(4)]
    source = lax.broadcasted_iota(jnp.int32, (256, 128), 0) % 128
    target = lax.broadcasted_iota(jnp.int32, (256, 128), 1)
    wanted = target // 64 * 64 + (target % 64 + jnp.where(cz > 0.0, 63, 1)) % 64
    turn = (source == wanted).astype(jnp.float32).astype(jnp.bfloat16)

    def along_z(first, to):
        value = f_ref[pl.ds(first, GROUP)].reshape(GROUP * 128, 128)
        high = value.astype(jnp.bfloat16)
        rest = (value - high.astype(jnp.float32)).astype(jnp.bfloat16)
        to[...] = jnp.dot(
            jnp.concatenate([high, rest], axis=1), turn, preferred_element_type=jnp.float32
        )

    def advance(first, lower, z_ref):
        for i in range(GROUP):
            k = first + i
            coef_y = jnp.abs(speed_of(k % VG)) / acz
            own = (1.0 / coef_z - 1.0) - coef_y
            for q in range(4):
                f = [f_ref[k, pl.ds(32 * q + r, 8, 4), :] for r in range(4)]
                far = [along(v, 64) for v in f]
                coef_own = own - coef_x[q]
                for r in range(4):
                    h, x = r // 2, r % 2
                    value = coef_own * f[r] + z_ref[pl.ds(128 * i + 32 * q + r, 8, 4), :]
                    if q < 2 and x == 0:
                        value = value + coef_x[q] * f[r + 1]
                    if q >= 2 and x == 1:
                        value = value + coef_x[q] * f[r - 1]
                    if lower and h == 0:
                        value = value + jnp.where(low, 0.0, coef_y * far[r])
                    elif lower or h == 0:
                        value = value + coef_y * jnp.where(low, far[x], far[x + 2])
                    else:
                        value = value + coef_y * jnp.where(low, far[r], f[r])
                    t_ref[k - s * VG, 32 * r + 8 * q : 32 * r + 8 * q + 8, :] = value

    def one_chunk(c, lower):
        first = s * VG + c * KYS
        after = s * VG + jnp.minimum(c + 1, 3) * KYS
        along_z(first + GROUP, z1_ref)
        advance(first, lower, z0_ref)
        along_z(after, z0_ref)
        advance(first + GROUP, lower, z1_ref)

    along_z(s * VG, z0_ref)
    for lower in (False, True):

        def part(p, carry, lower=lower):
            one_chunk(2 * int(lower) + p, lower)
            return carry

        lax.fori_loop(0, 2, part, 0)


def step_kernel(
    part0_ref, part1_ref, part2_ref, part3_ref, surface_ref, sums_ref, cell_ref,
    wall_x_ref, wall_y_ref, far_ref, near_ref, t0_ref, t1_ref, t2_ref,
    cover_ref, out_hbm,
    out_ref, ex_ref, ey_ref, wy_ref, keep_ref, out_sem,
):
    row = rows()
    totals = []
    for t in range(4):
        totals.append((part0_ref[t] + part1_ref[t]) + (part2_ref[t] + part3_ref[t]))
    incident = [totals[3][4 + s : 5 + s] for s in range(S)]
    start = [surface_ref[0, j : j + 1, :] for j in range(NSURF)]
    desorb = [surface_ref[1, j : j + 1, :] for j in range(NSURF)]
    lateral = [surface_ref[2, j : j + 1, :] for j in range(NSURF)]
    feed = [
        surface_ref[3, j : j + 1, :] * incident[0]
        + surface_ref[4, j : j + 1, :] * incident[1]
        + surface_ref[5, j : j + 1, :] * incident[2]
        for j in range(NSURF)
    ]

    def tree(values):
        values = list(values)
        while len(values) > 1:
            values = [
                values[i] + values[i + 1] if i + 1 < len(values) else values[i]
                for i in range(0, len(values), 2)
            ]
        return values[0]

    def total(v):
        return jnp.sum(v, axis=0, keepdims=True)

    covers = start
    for _ in range(NEWTON):
        vacant = 1.0 - tree(covers)
        scaled, coupling = [], []
        for j in range(NSURF):
            th = covers[j]
            squared = lateral[j] * (th * th)
            net = feed[j] * vacant - desorb[j] * th - squared * th
            residual = th - start[j] - SURFACE_STEP * net
            inverse = 1.0 / (1.0 + SURFACE_STEP * (desorb[j] + 3.0 * squared))
            scaled.append(residual * inverse)
            coupling.append((SURFACE_STEP * feed[j]) * inverse)
        ratio = tree(scaled) / (1.0 + tree(coupling))
        covers = [
            th - DAMPING * (y - u * ratio) for th, y, u in zip(covers, scaled, coupling)
        ]
    released = [
        desorb[j] * covers[j] + lateral[j] * (covers[j] * covers[j] * covers[j])
        for j in range(NSURF)
    ]
    vacant = 1.0 - tree(covers)

    def quantity(q):
        v = totals[q // 2]
        other = down(v, 4)
        return jnp.where(row < 4, v, other) if q % 2 == 0 else jnp.where(row < 4, other, v)

    dens = [quantity(s) for s in range(S)]
    mom = [quantity(3 + a) for a in range(3)]
    energy = quantity(6)
    wall_dens = []
    wall_mom = [0.0, 0.0, 0.0]
    wall_energy = 0.0
    for s in range(S):
        m = SPECIES_MASS[s]
        emitted = incident[s] * (1.0 - sums_ref[s, 6:7] * vacant) + tree(
            [surface_ref[6 + s, j : j + 1, :] * released[j] for j in range(NSURF)]
        )
        wd = emitted * sums_ref[s, 0:1]
        wall_dens.append(wd)
        dens[s] = dens[s] + to_tile(wd * sums_ref[s, 1:2])
        for a in range(3):
            wall_mom[a] = wall_mom[a] + (m * wd) * sums_ref[s, 2 + a : 3 + a]
        wall_energy = wall_energy + (m * wd) * sums_ref[s, 5:6]
    mom = [mom[a] + to_tile(wall_mom[a]) for a in range(3)]
    energy = energy + to_tile(wall_energy)
    gas = dens[0] + dens[1] + dens[2]
    mass = SPECIES_MASS[0] * dens[0] + SPECIES_MASS[1] * dens[1] + SPECIES_MASS[2] * dens[2]
    bulk = [v / mass for v in mom]
    flow = bulk[0] * bulk[0] + bulk[1] * bulk[1] + bulk[2] * bulk[2]
    temperature = (energy - mass * flow) / (3.0 * gas)
    cz = own_speed_z()
    acz = jnp.abs(cz)
    coef_z = TIME_STEP * acz
    grid = speed_of(lax.broadcasted_iota(jnp.int32, (VG, 128), 0))
    for s in range(S):
        rate = -SPECIES_MASS[s] / (2.0 * temperature)
        keep = jnp.exp((-TIME_STEP * COLLISION_RATE[s]) * gas)
        off = cz - bulk[2]
        scale = (1.0 - keep) * dens[s] * jnp.exp(rate * (off * off))
        keep_ref[s] = coef_z * keep
        for r in range(4):
            at = slice(r, r + 1)

            def table(drift):
                gap = grid - drift[at]
                return jnp.exp(rate[at] * (gap * gap))

            ex = table(bulk[0])
            ey = table(bulk[1])
            factor = scale[at] / (WEIGHT * total(ex) * total(ey) * total(table(bulk[2])))
            ex_ref[s, r] = ex
            ey_ref[s, r] = ey * factor
        other = pltpu.roll(wall_dens[s], 64, 1)
        wy_ref[s, 0] = wall_y_ref[s, 0] * wall_dens[s]
        wy_ref[s, 1] = wall_y_ref[s, 1] * other

    octet = speed_of(lax.broadcasted_iota(jnp.int32, TILE, 0))
    coef_x = [jnp.abs(octet + 8.0 * SPACING * q) / acz for q in range(4)]
    second = lax.axis_index("space") % 2 == 1

    def advance(first, s, lower):
        t_ref = (t0_ref, t1_ref, t2_ref)[s]
        keep = [jnp.broadcast_to(keep_ref[s, r : r + 1, :], TILE) for r in range(4)]
        for i in range(GROUP):
            k = first + i
            ky = k - s * VG
            ey = [jnp.broadcast_to(ey_ref[s, r, pl.ds(ky, 1), :], TILE) for r in range(4)]
            if lower:
                wy = [
                    jnp.broadcast_to(wy_ref[s, x, pl.ds(ky - PAIRS, 1), :], TILE)
                    for x in range(CX)
                ]
            for q in range(4):
                for r in range(4):
                    h, x = r // 2, r % 2
                    value = t_ref[ky, 32 * r + 8 * q : 32 * r + 8 * q + 8, :]
                    at = pl.ds(16 * h + 8 * (q % 2), 8)
                    if q < 2 and x == 1:
                        beside = jnp.where(second, far_ref[k, at, :], near_ref[k, at, :])
                        value = value + coef_x[q] * beside
                    if q >= 2 and x == 0:
                        beside = jnp.where(second, near_ref[k, at, :], far_ref[k, at, :])
                        value = value + coef_x[q] * beside
                    if lower and h == 0:
                        value = value + wall_x_ref[s, x, 8 * q : 8 * q + 8, :] * wy[x]
                    value = keep[r] * value + ex_ref[s, r, 8 * q : 8 * q + 8, :] * ey[r]
                    out_ref[k, pl.ds(32 * q + r, 8, 4), :] = value

    for s in range(S):
        for lower in (False, True):

            def part(p, carry, s=s, lower=lower):
                g = 8 * s + 4 * int(lower) + p
                advance(g * GROUP, s, lower)
                half_chunk(out_ref, out_hbm, out_sem, g).start()
                return carry

            lax.fori_loop(0, 4, part, 0)
    cover_ref[...] = jnp.dot(
        jnp.concatenate(covers, axis=0), selector(cell_ref[...]), precision=PRECISE,
        preferred_element_type=jnp.float32,
    )
    for c in range(2 * BLOCKS):
        half_chunk(out_ref, out_hbm, out_sem, c).wait()


SMEM = pl.BlockSpec(memory_space=pltpu.SMEM)
VMEM = pl.BlockSpec(memory_space=pltpu.VMEM)
HBM = pl.BlockSpec(memory_space=pl.ANY)
F32 = jnp.float32
BIG = pltpu.CompilerParams(vmem_limit_bytes=16 * 1024 * 1024)
SMALL = pltpu.CompilerParams(vmem_limit_bytes=4 * 1024 * 1024)
DMA = pltpu.SemaphoreType.DMA
LONG = pl.CostEstimate(flops=10**10, bytes_accessed=10**7, transcendentals=0)


def shape(*dims):
    return jax.ShapeDtypeStruct(dims, F32)


def near(value):
    return pltpu.with_memory_space_constraint(value, pltpu.VMEM)


def moments_call(field):
    return pl.pallas_call(
        moments_kernel,
        in_specs=[HBM],
        out_specs=[VMEM] * 6,
        out_shape=[pltpu.VMEM((4, 8, 128), F32)] * 3
        + [pltpu.VMEM((S * VG, 128, 128), F32)]
        + [pltpu.VMEM((S * VG, 32, 128), F32)] * 2,
        scratch_shapes=[
            pltpu.VMEM((S, 20, 8, 128), F32),
            DMA((BLOCKS,)),
        ],
        compiler_params=BIG,
    )(field)


def wall_call(*args):
    return pl.pallas_call(
        wall_kernel,
        in_specs=[SMEM] * 3 + [VMEM] * 4,
        out_specs=[VMEM] * 4,
        out_shape=[
            pltpu.VMEM((9, 16, 128), F32),
            pltpu.VMEM((S, 8, 128), F32),
            pltpu.VMEM((S, CX, VG, 128), F32),
            pltpu.VMEM((S, CX, VG // 2, 128), F32),
        ],
        compiler_params=SMALL,
    )(*args)


def shift_call(s, field):
    return pl.pallas_call(
        functools.partial(shift_kernel, s),
        in_specs=[VMEM],
        out_specs=VMEM,
        out_shape=pltpu.VMEM((VG, 128, 128), F32),
        scratch_shapes=[
            pltpu.VMEM((GROUP * 128, 128), F32),
            pltpu.VMEM((GROUP * 128, 128), F32),
        ],
        compiler_params=BIG,
        cost_estimate=LONG,
    )(near(field))


def step_call(*args):
    return pl.pallas_call(
        step_kernel,
        in_specs=[VMEM] * 14,
        out_specs=[VMEM, HBM],
        out_shape=[shape(NSURF, 128), shape(S * VG, 128, 128)],
        scratch_shapes=[
            pltpu.VMEM((S * VG, 128, 128), F32),
            pltpu.VMEM((S, 4, VG, 128), F32),
            pltpu.VMEM((S, 4, VG, 128), F32),
            pltpu.VMEM((S, CX, VG // 2, 128), F32),
            pltpu.VMEM((S, 8, 128), F32),
            DMA((2 * BLOCKS,)),
        ],
        compiler_params=BIG,
    )(*args)


def paired(value, axis, by=1):
    peers = lax.axis_size(axis)
    return lax.ppermute(value, axis, [(i, i ^ by) for i in range(peers)])


def crossed(value, axis, by):
    peers = lax.axis_size(axis)
    pairs = [(i, (i + (by if i % 2 else -by)) % peers) for i in range(peers)]
    return lax.ppermute(value, axis, pairs)


def per_device(
    distribution, wall_temp, coverage, face_cell, face_owner, stoichiometry, sticking, surface_rates
):
    field = (
        distribution.reshape(S, VG * VG, CX, 2, 128)
        .transpose(0, 1, 3, 2, 4)
        .reshape(S * VG, 128, 128)
    )
    field = pltpu.with_memory_space_constraint(field, pltpu.HBM)
    own, to_far, to_near, held, far, nigh = moments_call(field)
    together = lax.optimization_barrier
    face_row = face_cell.reshape(1, 128)

    temp, own = together((wall_temp.reshape(1, 128), own))
    walls = wall_call(
        stoichiometry.T, sticking, surface_rates, temp, coverage, face_row,
        face_owner.reshape(1, 128),
    )
    own = own + crossed(to_far, "space", 1) + paired(to_near, "space")
    own, held, walls = together((own, held, walls))

    far = crossed(near(far), "space", 1)
    nigh = paired(near(nigh), "space")
    moved0 = shift_call(0, held)
    own = own + paired(own, "x", 1) + paired(own, "x", 3) + paired(own, "x", 2)
    own, moved0, held = together((own, moved0, held))

    moved1 = shift_call(1, held)
    own = own + paired(own, "z")
    own, moved1, held = together((own, moved1, held))

    moved2 = shift_call(2, held)
    parts = [own] + [crossed(own, "z", by) for by in (1, 2, 3)]
    surface, sums, wall_x, wall_y = walls
    vmem = [near(v) for v in parts + [surface, sums]]
    covers, advanced = step_call(
        *vmem, face_row, near(wall_x), near(wall_y), near(far), near(nigh),
        near(moved0), near(moved1), near(moved2),
    )
    advanced = (
        advanced.reshape(S, VG * VG, 2, CX, 128)
        .transpose(0, 1, 3, 2, 4)
        .reshape(distribution.shape)
    )
    return advanced, covers


def solution(mesh):
    fine = Mesh(mesh.devices.reshape(N_Z, N_X, mesh.shape["space"]), ("z", "x", "space"))
    return jax.shard_map(
        per_device,
        mesh=fine,
        in_specs=(
            P(None, ("z", "x"), "space", None),
            P("space"),
            P(None, "space"),
            P("space", None),
            P("space"),
            P(),
            P(),
            P(),
        ),
        out_specs=(P(None, ("z", "x"), "space", None), P(None, "space")),
        check_vma=False,
    )
```

```python
import functools

import jax
import jax.numpy as jnp
from jax import lax
from jax.experimental import pallas as pl
from jax.experimental.pallas import tpu as pltpu
from jax.sharding import Mesh
from jax.sharding import PartitionSpec as P

S = 3
VG = 32
NZ = 64
CX = 2
NEWTON = 8
NSURF = 12
PATCHES = 4
N_Z = 8
N_X = 4

SPEED_LIMIT = 4.0
SPACING = 2.0 * SPEED_LIMIT / VG
WEIGHT = SPACING * SPACING * SPACING
SPECIES_MASS = (1.0, 2.0, 4.0)
COLLISION_RATE = (0.3, 0.2, 0.15)
TIME_STEP = 0.08
SURFACE_STEP = 2.0
DAMPING = 0.25
ACTIVATION = 2.0

PAIRS = VG // 2
HALF = PAIRS // 2
BLOCKS = 12
KYS = S * VG // BLOCKS
GROUP = KYS // 2
TILE = (8, 128)
PRECISE = lax.Precision.HIGHEST


def rows():
    return lax.broadcasted_iota(jnp.int32, TILE, 0)


def lanes():
    return lax.broadcasted_iota(jnp.int32, TILE, 1)


def down(value, by):
    return pltpu.roll(value, by % 8, 0)


def along(value, by):
    return pltpu.roll(value, by % 128, 1)


def pair_speed():
    parity = (rows() >= 4).astype(jnp.float32)
    return (parity + 0.5) * SPACING - SPEED_LIMIT


def speed_of(position):
    return (position.astype(jnp.float32) + 0.5) * SPACING - SPEED_LIMIT


def chunk(src, dst, sems, c):
    part = pl.ds(c * KYS, KYS)
    return pltpu.make_async_copy(src.at[part], dst.at[part], sems.at[c])


def half_chunk(src, dst, sems, c):
    part = pl.ds(c * GROUP, GROUP)
    return pltpu.make_async_copy(src.at[part], dst.at[part], sems.at[c])


def moments_kernel(
    f_hbm, own_ref, to_far_ref, to_near_ref, f_ref, far_ref, near_ref, acc_ref, f_sem,
):
    for c in range(BLOCKS):
        chunk(f_hbm, f_ref, f_sem, c).start()
    base = pair_speed()
    speeds = [jnp.abs(base + 2.0 * SPACING * j) for j in range(PAIRS)]
    acc_ref[...] = jnp.zeros_like(acc_ref)
    second = lax.axis_index("space") % 2 == 1
    far_row = jnp.where(second, 65, 0)
    near_row = 65 - far_row

    def one(k, carry):
        zero = jnp.zeros(TILE, jnp.float32)
        sums = []
        for side in range(2):
            n0, n1, n2, n3 = zero, zero, zero, zero
            for j in range(side * HALF, (side + 1) * HALF):
                f = f_ref[k, 8 * j : 8 * j + 8, :]
                g = f * speeds[j]
                n0 = n0 + f
                n1 = n1 + g
                g = g * speeds[j]
                n2 = n2 + g
                n3 = n3 + g * speeds[j]
            sums.append((n0, n1, n2, n3))
        (a0, a1, a2, a3), (b0, b1, b2, b3) = sums
        for h in range(2):
            for q in range(2):
                to = pl.ds(16 * h + 8 * q, 8)
                far_ref[k, to, :] = f_ref[k, pl.ds(far_row + 32 * q + 2 * h, 8, 4), :]
                near_ref[k, to, :] = f_ref[k, pl.ds(near_row + 32 * q + 2 * h, 8, 4), :]
        cy = speed_of(k % VG)
        cy2 = cy * cy
        acy = jnp.abs(cy)
        d = a0 + b0
        x1 = b1 - a1
        e = a2 + b2 + cy2 * d
        yd = cy * d
        new = (
            d, x1, yd, e,
            b1, b2, cy * b1, b3 + cy2 * b1,
            a1, -a2, cy * a1, a3 + cy2 * a1,
            acy * d, acy * x1, acy * yd, acy * e,
        )
        return tuple(c + n for c, n in zip(carry, new))

    start = tuple(jnp.zeros(TILE, jnp.float32) for _ in range(16))
    def turn(c, carry):
        species, half = c // 4, c % 4 // 2
        chunk(f_hbm, f_ref, f_sem, c).wait()
        total = lax.fori_loop(0, KYS, lambda i, v: one(c * KYS + i, v), start, unroll=8)
        for q in range(12):
            acc_ref[species, q] += total[q]
        for q in range(4):
            acc_ref[species, 12 + 4 * half + q] += total[12 + q]
        return carry

    lax.fori_loop(0, BLOCKS, turn, 0)
    row = rows()
    lane = lanes()
    cz = own_speed_z()
    acz = jnp.abs(cz)
    rise = cz > 0.0
    odd = row % 2 == 1
    upper_h = (row // 2) % 2 == 1
    low = lane < 64
    own = []
    rim = []
    incident = []
    for s in range(S):
        full = []
        for q in range(20):
            v = acc_ref[s, q]
            full.append(v + down(v, 4))
        for q in range(4):
            b, xp, xm = full[q], full[4 + q], full[8 + q]
            ym, yp = full[12 + q], full[16 + q]
            zp = jnp.where(lane % 64 == 0, along(b, 65), along(b, 1))
            zm = jnp.where(lane % 64 == 63, along(b, 63), along(b, 127))
            shifted_z = jnp.where(rise, zp, zm)
            rp = along(yp, 64)
            rm = along(ym, 64)
            from_low = jnp.where(low, jnp.where(upper_h, down(rp, 2), 0.0), rp)
            from_high = jnp.where(low, rm, jnp.where(upper_h, ym, down(rm, -2)))
            inner = jnp.where(odd, down(xp, 1), down(xm, -1))
            stay = (1.0 - TIME_STEP * acz) * b - TIME_STEP * (xp + xm + yp + ym)
            own.append(
                stay
                + TIME_STEP * (acz * shifted_z + from_low + from_high + inner)
            )
            rim.append(TIME_STEP * jnp.where(odd, xp, xm))
        ym = full[12]
        incident.append(jnp.where(low, ym, along(down(ym, -1), 64)))
    for values, out in ((own, own_ref), (rim, None)):
        packed = [values[0], values[4], values[8]]
        momenta = [0.0, 0.0, 0.0, 0.0]
        for s in range(S):
            m = SPECIES_MASS[s]
            d, px, py, e = values[4 * s : 4 * s + 4]
            momenta[0] = momenta[0] + m * px
            momenta[1] = momenta[1] + m * py
            momenta[2] = momenta[2] + (m * cz) * d
            momenta[3] = momenta[3] + m * (e + cz * cz * d)
        packed = packed + momenta
        if out is own_ref:
            last = jnp.where(
                row == 4,
                down(incident[0], 4),
                jnp.where(
                    row == 5,
                    down(incident[1], 5),
                    jnp.where(row == 6, down(incident[2], 6), 0.0),
                ),
            )
        else:
            last = jnp.zeros(TILE, jnp.float32)
        packed.append(last)
        for t in range(4):
            value = WEIGHT * jnp.where(row < 4, packed[2 * t], packed[2 * t + 1])
            if out is own_ref:
                out[t] = value
            else:
                to_right = jnp.where(odd, 0.0, down(value, -1))
                to_left = jnp.where(odd, down(value, 1), 0.0)
                to_far_ref[t] = jnp.where(second, to_right, to_left)
                to_near_ref[t] = jnp.where(second, to_left, to_right)


def own_speed_z():
    return speed_of(lax.axis_index("z") * lax.axis_size("x") + lax.axis_index("x"))


def selector(face_cell):
    column = lax.broadcasted_iota(jnp.int32, (128, 128), 0)
    return (column == face_cell).astype(jnp.float32)


def to_tile(value):
    row = rows() % 4
    low = lanes() < 64
    wide = jnp.broadcast_to(value, TILE)
    return jnp.where(
        jnp.logical_and(row == 0, low),
        wide,
        jnp.where(jnp.logical_and(row == 1, low), along(wide, 64), 0.0),
    )


def wall_kernel(
    stoich_ref, stick_ref, rates_ref, temp_ref, cover_ref, cell_ref, owner_ref,
    surface_ref, sums_ref, wall_x_ref, wall_y_ref,
):
    select = selector(cell_ref[...])
    pieces = jnp.concatenate(
        [cover_ref[...], temp_ref[...], owner_ref[...].astype(jnp.float32),
         jnp.zeros((2, 128), jnp.float32)], axis=0,
    )
    placed = lax.dot_general(
        pieces, select, (((1,), (1,)), ((), ())), precision=PRECISE,
        preferred_element_type=jnp.float32,
    )
    temp = placed[12:13]
    owner = placed[13:14]
    arrhenius = jnp.exp(ACTIVATION * (1.0 - 1.0 / temp))
    zero = jnp.zeros((1, 128), jnp.float32)
    masks = [jnp.abs(owner - float(p)) < 0.5 for p in range(PATCHES)]

    def by_owner(read):
        value = zero
        for p in range(PATCHES):
            value = jnp.where(masks[p], read(p), value)
        return value

    surface_ref[0] = jnp.concatenate([placed[0:12], jnp.zeros((4, 128), jnp.float32)], axis=0)
    desorb = [by_owner(lambda p: rates_ref[p, 0, j]) * arrhenius for j in range(NSURF)]
    lateral = [by_owner(lambda p: rates_ref[p, 1, j]) for j in range(NSURF)]
    stick = [by_owner(lambda p: stick_ref[p, s]) for s in range(S)]
    surface_ref[1] = jnp.concatenate(desorb + [zero] * 4, axis=0)
    surface_ref[2] = jnp.concatenate(lateral + [zero] * 4, axis=0)
    counts = [[stoich_ref[s, j].astype(jnp.float32) for s in range(S)] for j in range(NSURF)]
    for s in range(S):
        column_sum = counts[0][s]
        for j in range(1, NSURF):
            column_sum = column_sum + counts[j][s]
        into = jnp.concatenate(
            [(zero + counts[j][s]) / (zero + (1.0 + column_sum)) * stick[s] for j in range(NSURF)]
            + [zero] * 4, axis=0,
        )
        out = jnp.concatenate(
            [(zero + counts[j][s]) / (zero + (1.0 + counts[j][0] + counts[j][1] + counts[j][2]))
             for j in range(NSURF)]
            + [zero] * 4, axis=0,
        )
        surface_ref[3 + s] = into
        surface_ref[6 + s] = out

    k_rows = lax.broadcasted_iota(jnp.int32, (VG, 128), 0)
    c = speed_of(k_rows)
    up = jnp.maximum(c, 0.0)
    cz = own_speed_z()
    cy = c[VG // 2 :]
    temps = [temp, pltpu.roll(temp, 64, 1)]
    low = lax.broadcasted_iota(jnp.int32, (VG, 128), 1) < 64
    for s in range(S):
        m = SPECIES_MASS[s]
        e = jnp.exp(-m * (c * c) / (2.0 * temp))

        def total(v):
            return jnp.sum(v, axis=0, keepdims=True)

        s0 = total(e)
        s1 = total(c * e)
        s2 = total(c * c * e)
        u1 = total(up * e)
        u2 = total(up * c * e)
        u3 = total(up * c * c * e)
        norm = WEIGHT * u1 * s0 * s0
        scale = WEIGHT * TIME_STEP
        sums_ref[s] = jnp.concatenate(
            [
                1.0 / norm,
                scale * u1 * s0 * s0,
                scale * u1 * s1 * s0,
                scale * u2 * s0 * s0,
                scale * u1 * s0 * s1,
                scale * (u3 * s0 * s0 + u1 * s2 * s0 + u1 * s0 * s2),
                stick[s],
                zero,
            ],
            axis=0,
        )
        for x in range(CX):
            rate = -m / (2.0 * temps[x])
            wall_x_ref[s, x] = jnp.where(low, jnp.exp(rate * (c * c)), 0.0)
            wall_y_ref[s, x] = (cy / jnp.abs(cz)) * jnp.exp(rate * (cy * cy)) * jnp.exp(rate * (cz * cz))


def shift_kernel(s, f_ref, t_ref, z0_ref, z1_ref):
    low = lanes() < 64
    cz = own_speed_z()
    acz = jnp.abs(cz)
    coef_z = TIME_STEP * acz
    octet = speed_of(lax.broadcasted_iota(jnp.int32, TILE, 0))
    coef_x = [jnp.abs(octet + 8.0 * SPACING * q) / acz for q in range(4)]
    source = lax.broadcasted_iota(jnp.int32, (256, 128), 0) % 128
    target = lax.broadcasted_iota(jnp.int32, (256, 128), 1)
    wanted = target // 64 * 64 + (target % 64 + jnp.where(cz > 0.0, 63, 1)) % 64
    turn = (source == wanted).astype(jnp.float32).astype(jnp.bfloat16)

    def along_z(first, to):
        value = f_ref[pl.ds(first, GROUP)].reshape(GROUP * 128, 128)
        high = value.astype(jnp.bfloat16)
        rest = (value - high.astype(jnp.float32)).astype(jnp.bfloat16)
        to[...] = jnp.dot(
            jnp.concatenate([high, rest], axis=1), turn, preferred_element_type=jnp.float32
        )

    def advance(first, lower, z_ref):
        for i in range(GROUP):
            k = first + i
            coef_y = jnp.abs(speed_of(k % VG)) / acz
            own = (1.0 / coef_z - 1.0) - coef_y
            for q in range(4):
                f = [f_ref[k, pl.ds(32 * q + r, 8, 4), :] for r in range(4)]
                far = [along(v, 64) for v in f]
                coef_own = own - coef_x[q]
                for r in range(4):
                    h, x = r // 2, r % 2
                    value = coef_own * f[r] + z_ref[pl.ds(128 * i + 32 * q + r, 8, 4), :]
                    if q < 2 and x == 0:
                        value = value + coef_x[q] * f[r + 1]
                    if q >= 2 and x == 1:
                        value = value + coef_x[q] * f[r - 1]
                    if lower and h == 0:
                        value = value + jnp.where(low, 0.0, coef_y * far[r])
                    elif lower or h == 0:
                        value = value + coef_y * jnp.where(low, far[x], far[x + 2])
                    else:
                        value = value + coef_y * jnp.where(low, far[r], f[r])
                    t_ref[k - s * VG, 32 * r + 8 * q : 32 * r + 8 * q + 8, :] = value

    def one_chunk(c, lower):
        first = s * VG + c * KYS
        after = s * VG + jnp.minimum(c + 1, 3) * KYS
        along_z(first + GROUP, z1_ref)
        advance(first, lower, z0_ref)
        along_z(after, z0_ref)
        advance(first + GROUP, lower, z1_ref)

    along_z(s * VG, z0_ref)
    for lower in (False, True):

        def part(p, carry, lower=lower):
            one_chunk(2 * int(lower) + p, lower)
            return carry

        lax.fori_loop(0, 2, part, 0)


def step_kernel(
    part0_ref, part1_ref, part2_ref, part3_ref, surface_ref, sums_ref, cell_ref,
    wall_x_ref, wall_y_ref, far_ref, near_ref, t0_ref, t1_ref, t2_ref,
    cover_ref, out_hbm,
    out_ref, ex_ref, ey_ref, wy_ref, keep_ref, out_sem,
):
    row = rows()
    totals = []
    for t in range(4):
        totals.append((part0_ref[t] + part1_ref[t]) + (part2_ref[t] + part3_ref[t]))
    incident = [totals[3][4 + s : 5 + s] for s in range(S)]
    start = [surface_ref[0, j : j + 1, :] for j in range(NSURF)]
    desorb = [surface_ref[1, j : j + 1, :] for j in range(NSURF)]
    lateral = [surface_ref[2, j : j + 1, :] for j in range(NSURF)]
    feed = [
        surface_ref[3, j : j + 1, :] * incident[0]
        + surface_ref[4, j : j + 1, :] * incident[1]
        + surface_ref[5, j : j + 1, :] * incident[2]
        for j in range(NSURF)
    ]

    def tree(values):
        values = list(values)
        while len(values) > 1:
            values = [
                values[i] + values[i + 1] if i + 1 < len(values) else values[i]
                for i in range(0, len(values), 2)
            ]
        return values[0]

    def total(v):
        return jnp.sum(v, axis=0, keepdims=True)

    covers = start
    for _ in range(NEWTON):
        vacant = 1.0 - tree(covers)
        scaled, coupling = [], []
        for j in range(NSURF):
            th = covers[j]
            squared = lateral[j] * (th * th)
            net = feed[j] * vacant - desorb[j] * th - squared * th
            residual = th - start[j] - SURFACE_STEP * net
            inverse = 1.0 / (1.0 + SURFACE_STEP * (desorb[j] + 3.0 * squared))
            scaled.append(residual * inverse)
            coupling.append((SURFACE_STEP * feed[j]) * inverse)
        ratio = tree(scaled) / (1.0 + tree(coupling))
        covers = [
            th - DAMPING * (y - u * ratio) for th, y, u in zip(covers, scaled, coupling)
        ]
    released = [
        desorb[j] * covers[j] + lateral[j] * (covers[j] * covers[j] * covers[j])
        for j in range(NSURF)
    ]
    vacant = 1.0 - tree(covers)

    def quantity(q):
        v = totals[q // 2]
        other = down(v, 4)
        return jnp.where(row < 4, v, other) if q % 2 == 0 else jnp.where(row < 4, other, v)

    dens = [quantity(s) for s in range(S)]
    mom = [quantity(3 + a) for a in range(3)]
    energy = quantity(6)
    wall_dens = []
    wall_mom = [0.0, 0.0, 0.0]
    wall_energy = 0.0
    for s in range(S):
        m = SPECIES_MASS[s]
        emitted = incident[s] * (1.0 - sums_ref[s, 6:7] * vacant) + tree(
            [surface_ref[6 + s, j : j + 1, :] * released[j] for j in range(NSURF)]
        )
        wd = emitted * sums_ref[s, 0:1]
        wall_dens.append(wd)
        dens[s] = dens[s] + to_tile(wd * sums_ref[s, 1:2])
        for a in range(3):
            wall_mom[a] = wall_mom[a] + (m * wd) * sums_ref[s, 2 + a : 3 + a]
        wall_energy = wall_energy + (m * wd) * sums_ref[s, 5:6]
    mom = [mom[a] + to_tile(wall_mom[a]) for a in range(3)]
    energy = energy + to_tile(wall_energy)
    gas = dens[0] + dens[1] + dens[2]
    mass = SPECIES_MASS[0] * dens[0] + SPECIES_MASS[1] * dens[1] + SPECIES_MASS[2] * dens[2]
    bulk = [v / mass for v in mom]
    flow = bulk[0] * bulk[0] + bulk[1] * bulk[1] + bulk[2] * bulk[2]
    temperature = (energy - mass * flow) / (3.0 * gas)
    cz = own_speed_z()
    acz = jnp.abs(cz)
    coef_z = TIME_STEP * acz
    grid = speed_of(lax.broadcasted_iota(jnp.int32, (VG, 128), 0))
    for s in range(S):
        rate = -SPECIES_MASS[s] / (2.0 * temperature)
        keep = jnp.exp((-TIME_STEP * COLLISION_RATE[s]) * gas)
        off = cz - bulk[2]
        scale = (1.0 - keep) * dens[s] * jnp.exp(rate * (off * off))
        keep_ref[s] = coef_z * keep
        for r in range(4):
            at = slice(r, r + 1)

            def table(drift):
                gap = grid - drift[at]
                return jnp.exp(rate[at] * (gap * gap))

            ex = table(bulk[0])
            ey = table(bulk[1])
            factor = scale[at] / (WEIGHT * total(ex) * total(ey) * total(table(bulk[2])))
            ex_ref[s, r] = ex
            ey_ref[s, r] = ey * factor
        other = pltpu.roll(wall_dens[s], 64, 1)
        wy_ref[s, 0] = wall_y_ref[s, 0] * wall_dens[s]
        wy_ref[s, 1] = wall_y_ref[s, 1] * other

    octet = speed_of(lax.broadcasted_iota(jnp.int32, TILE, 0))
    coef_x = [jnp.abs(octet + 8.0 * SPACING * q) / acz for q in range(4)]
    second = lax.axis_index("space") % 2 == 1

    def advance(first, s, lower):
        t_ref = (t0_ref, t1_ref, t2_ref)[s]
        keep = [jnp.broadcast_to(keep_ref[s, r : r + 1, :], TILE) for r in range(4)]
        for i in range(GROUP):
            k = first + i
            ky = k - s * VG
            ey = [jnp.broadcast_to(ey_ref[s, r, pl.ds(ky, 1), :], TILE) for r in range(4)]
            if lower:
                wy = [
                    jnp.broadcast_to(wy_ref[s, x, pl.ds(ky - PAIRS, 1), :], TILE)
                    for x in range(CX)
                ]
            for q in range(4):
                for r in range(4):
                    h, x = r // 2, r % 2
                    value = t_ref[ky, 32 * r + 8 * q : 32 * r + 8 * q + 8, :]
                    at = pl.ds(16 * h + 8 * (q % 2), 8)
                    if q < 2 and x == 1:
                        beside = jnp.where(second, far_ref[k, at, :], near_ref[k, at, :])
                        value = value + coef_x[q] * beside
                    if q >= 2 and x == 0:
                        beside = jnp.where(second, near_ref[k, at, :], far_ref[k, at, :])
                        value = value + coef_x[q] * beside
                    if lower and h == 0:
                        value = value + wall_x_ref[s, x, 8 * q : 8 * q + 8, :] * wy[x]
                    value = keep[r] * value + ex_ref[s, r, 8 * q : 8 * q + 8, :] * ey[r]
                    out_ref[k, pl.ds(32 * q + r, 8, 4), :] = value

    for s in range(S):
        for lower in (False, True):

            def part(p, carry, s=s, lower=lower):
                g = 8 * s + 4 * int(lower) + p
                advance(g * GROUP, s, lower)
                half_chunk(out_ref, out_hbm, out_sem, g).start()
                return carry

            lax.fori_loop(0, 4, part, 0)
    cover_ref[...] = jnp.dot(
        jnp.concatenate(covers, axis=0), selector(cell_ref[...]), precision=PRECISE,
        preferred_element_type=jnp.float32,
    )
    for c in range(2 * BLOCKS):
        half_chunk(out_ref, out_hbm, out_sem, c).wait()


SMEM = pl.BlockSpec(memory_space=pltpu.SMEM)
VMEM = pl.BlockSpec(memory_space=pltpu.VMEM)
HBM = pl.BlockSpec(memory_space=pl.ANY)
F32 = jnp.float32
BIG = pltpu.CompilerParams(vmem_limit_bytes=16 * 1024 * 1024)
SMALL = pltpu.CompilerParams(vmem_limit_bytes=4 * 1024 * 1024)
DMA = pltpu.SemaphoreType.DMA
LONG = pl.CostEstimate(flops=10**10, bytes_accessed=10**7, transcendentals=0)


def shape(*dims):
    return jax.ShapeDtypeStruct(dims, F32)


def near(value):
    return pltpu.with_memory_space_constraint(value, pltpu.VMEM)


def moments_call(field):
    return pl.pallas_call(
        moments_kernel,
        in_specs=[HBM],
        out_specs=[VMEM] * 6,
        out_shape=[pltpu.VMEM((4, 8, 128), F32)] * 3
        + [pltpu.VMEM((S * VG, 128, 128), F32)]
        + [pltpu.VMEM((S * VG, 32, 128), F32)] * 2,
        scratch_shapes=[
            pltpu.VMEM((S, 20, 8, 128), F32),
            DMA((BLOCKS,)),
        ],
        compiler_params=BIG,
    )(field)


def wall_call(*args):
    return pl.pallas_call(
        wall_kernel,
        in_specs=[SMEM] * 3 + [VMEM] * 4,
        out_specs=[VMEM] * 4,
        out_shape=[
            pltpu.VMEM((9, 16, 128), F32),
            pltpu.VMEM((S, 8, 128), F32),
            pltpu.VMEM((S, CX, VG, 128), F32),
            pltpu.VMEM((S, CX, VG // 2, 128), F32),
        ],
        compiler_params=SMALL,
    )(*args)


def shift_call(s, field):
    return pl.pallas_call(
        functools.partial(shift_kernel, s),
        in_specs=[VMEM],
        out_specs=VMEM,
        out_shape=pltpu.VMEM((VG, 128, 128), F32),
        scratch_shapes=[
            pltpu.VMEM((GROUP * 128, 128), F32),
            pltpu.VMEM((GROUP * 128, 128), F32),
        ],
        compiler_params=BIG,
        cost_estimate=LONG,
    )(near(field))


def step_call(*args):
    return pl.pallas_call(
        step_kernel,
        in_specs=[VMEM] * 14,
        out_specs=[VMEM, HBM],
        out_shape=[shape(NSURF, 128), shape(S * VG, 128, 128)],
        scratch_shapes=[
            pltpu.VMEM((S * VG, 128, 128), F32),
            pltpu.VMEM((S, 4, VG, 128), F32),
            pltpu.VMEM((S, 4, VG, 128), F32),
            pltpu.VMEM((S, CX, VG // 2, 128), F32),
            pltpu.VMEM((S, 8, 128), F32),
            DMA((2 * BLOCKS,)),
        ],
        compiler_params=BIG,
    )(*args)


def paired(value, axis, by=1):
    peers = lax.axis_size(axis)
    return lax.ppermute(value, axis, [(i, i ^ by) for i in range(peers)])


def crossed(value, axis, by):
    peers = lax.axis_size(axis)
    pairs = [(i, (i + (by if i % 2 else -by)) % peers) for i in range(peers)]
    return lax.ppermute(value, axis, pairs)


def per_device(
    distribution, wall_temp, coverage, face_cell, face_owner, stoichiometry, sticking, surface_rates
):
    field = (
        distribution.reshape(S, VG * VG, CX, 2, 128)
        .transpose(0, 1, 3, 2, 4)
        .reshape(S * VG, 128, 128)
    )
    field = pltpu.with_memory_space_constraint(field, pltpu.HBM)
    own, to_far, to_near, held, far, nigh = moments_call(field)
    together = lax.optimization_barrier
    face_row = face_cell.reshape(1, 128)

    own = own + crossed(to_far, "space", 1) + paired(to_near, "space")
    own, held = together((own, held))

    far = crossed(near(far), "space", 1)
    nigh = paired(near(nigh), "space")
    moved0 = shift_call(0, held)
    own = own + paired(own, "x", 1) + paired(own, "x", 2) + paired(own, "x", 3)
    own, moved0, held = together((own, moved0, held))

    moved1 = shift_call(1, held)
    own = own + paired(own, "z")
    own, moved1, held = together((own, moved1, held))

    temp, own = together((wall_temp.reshape(1, 128), own))
    walls = wall_call(
        stoichiometry.T, sticking, surface_rates, temp, coverage, face_row,
        face_owner.reshape(1, 128),
    )
    moved2 = shift_call(2, held)
    parts = [own] + [crossed(own, "z", by) for by in (1, 3, 2)]
    surface, sums, wall_x, wall_y = walls
    vmem = [near(v) for v in parts + [surface, sums]]
    covers, advanced = step_call(
        *vmem, face_row, near(wall_x), near(wall_y), near(far), near(nigh),
        near(moved0), near(moved1), near(moved2),
    )
    advanced = (
        advanced.reshape(S, VG * VG, 2, CX, 128)
        .transpose(0, 1, 3, 2, 4)
        .reshape(distribution.shape)
    )
    return advanced, covers


def solution(mesh):
    fine = Mesh(mesh.devices.reshape(N_Z, N_X, mesh.shape["space"]), ("z", "x", "space"))
    return jax.shard_map(
        per_device,
        mesh=fine,
        in_specs=(
            P(None, ("z", "x"), "space", None),
            P("space"),
            P(None, "space"),
            P("space", None),
            P("space"),
            P(),
            P(),
            P(),
        ),
        out_specs=(P(None, ("z", "x"), "space", None), P(None, "space")),
        check_vma=False,
    )
```

```python
import functools

import jax
import jax.numpy as jnp
from jax import lax
from jax.experimental import pallas as pl
from jax.experimental.pallas import tpu as pltpu
from jax.sharding import Mesh
from jax.sharding import PartitionSpec as P

S = 3
VG = 32
NZ = 64
CX = 2
NEWTON = 8
NSURF = 12
PATCHES = 4
N_Z = 8
N_X = 4

SPEED_LIMIT = 4.0
SPACING = 2.0 * SPEED_LIMIT / VG
WEIGHT = SPACING * SPACING * SPACING
SPECIES_MASS = (1.0, 2.0, 4.0)
COLLISION_RATE = (0.3, 0.2, 0.15)
TIME_STEP = 0.08
SURFACE_STEP = 2.0
DAMPING = 0.25
ACTIVATION = 2.0

PAIRS = VG // 2
HALF = PAIRS // 2
BLOCKS = 12
KYS = S * VG // BLOCKS
GROUP = KYS // 2
TILE = (8, 128)
PRECISE = lax.Precision.HIGHEST


def rows():
    return lax.broadcasted_iota(jnp.int32, TILE, 0)


def lanes():
    return lax.broadcasted_iota(jnp.int32, TILE, 1)


def down(value, by):
    return pltpu.roll(value, by % 8, 0)


def along(value, by):
    return pltpu.roll(value, by % 128, 1)


def pair_speed():
    parity = (rows() >= 4).astype(jnp.float32)
    return (parity + 0.5) * SPACING - SPEED_LIMIT


def speed_of(position):
    return (position.astype(jnp.float32) + 0.5) * SPACING - SPEED_LIMIT


def chunk(src, dst, sems, c):
    part = pl.ds(c * KYS, KYS)
    return pltpu.make_async_copy(src.at[part], dst.at[part], sems.at[c])


def half_chunk(src, dst, sems, c):
    part = pl.ds(c * GROUP, GROUP)
    return pltpu.make_async_copy(src.at[part], dst.at[part], sems.at[c])


def moments_kernel(
    f_hbm, own_ref, to_far_ref, to_near_ref, f_ref, far_ref, near_ref, acc_ref, f_sem,
):
    for c in range(BLOCKS):
        chunk(f_hbm, f_ref, f_sem, c).start()
    base = pair_speed()
    speeds = [jnp.abs(base + 2.0 * SPACING * j) for j in range(PAIRS)]
    acc_ref[...] = jnp.zeros_like(acc_ref)
    second = lax.axis_index("space") % 2 == 1
    far_row = jnp.where(second, 65, 0)
    near_row = 65 - far_row

    def one(k, carry):
        zero = jnp.zeros(TILE, jnp.float32)
        sums = []
        for side in range(2):
            n0, n1, n2, n3 = zero, zero, zero, zero
            for j in range(side * HALF, (side + 1) * HALF):
                f = f_ref[k, 8 * j : 8 * j + 8, :]
                g = f * speeds[j]
                n0 = n0 + f
                n1 = n1 + g
                g = g * speeds[j]
                n2 = n2 + g
                n3 = n3 + g * speeds[j]
            sums.append((n0, n1, n2, n3))
        (a0, a1, a2, a3), (b0, b1, b2, b3) = sums
        for h in range(2):
            for q in range(2):
                to = pl.ds(16 * h + 8 * q, 8)
                far_ref[k, to, :] = f_ref[k, pl.ds(far_row + 32 * q + 2 * h, 8, 4), :]
                near_ref[k, to, :] = f_ref[k, pl.ds(near_row + 32 * q + 2 * h, 8, 4), :]
        cy = speed_of(k % VG)
        cy2 = cy * cy
        acy = jnp.abs(cy)
        d = a0 + b0
        x1 = b1 - a1
        e = a2 + b2 + cy2 * d
        yd = cy * d
        new = (
            d, x1, yd, e,
            b1, b2, cy * b1, b3 + cy2 * b1,
            a1, -a2, cy * a1, a3 + cy2 * a1,
            acy * d, acy * x1, acy * yd, acy * e,
        )
        return tuple(c + n for c, n in zip(carry, new))

    start = tuple(jnp.zeros(TILE, jnp.float32) for _ in range(16))
    def turn(c, carry):
        species, half = c // 4, c % 4 // 2
        chunk(f_hbm, f_ref, f_sem, c).wait()
        total = lax.fori_loop(0, KYS, lambda i, v: one(c * KYS + i, v), start, unroll=8)
        for q in range(12):
            acc_ref[species, q] += total[q]
        for q in range(4):
            acc_ref[species, 12 + 4 * half + q] += total[12 + q]
        return carry

    lax.fori_loop(0, BLOCKS, turn, 0)
    row = rows()
    lane = lanes()
    cz = own_speed_z()
    acz = jnp.abs(cz)
    rise = cz > 0.0
    odd = row % 2 == 1
    upper_h = (row // 2) % 2 == 1
    low = lane < 64
    own = []
    rim = []
    incident = []
    for s in range(S):
        full = []
        for q in range(20):
            v = acc_ref[s, q]
            full.append(v + down(v, 4))
        for q in range(4):
            b, xp, xm = full[q], full[4 + q], full[8 + q]
            ym, yp = full[12 + q], full[16 + q]
            zp = jnp.where(lane % 64 == 0, along(b, 65), along(b, 1))
            zm = jnp.where(lane % 64 == 63, along(b, 63), along(b, 127))
            shifted_z = jnp.where(rise, zp, zm)
            rp = along(yp, 64)
            rm = along(ym, 64)
            from_low = jnp.where(low, jnp.where(upper_h, down(rp, 2), 0.0), rp)
            from_high = jnp.where(low, rm, jnp.where(upper_h, ym, down(rm, -2)))
            inner = jnp.where(odd, down(xp, 1), down(xm, -1))
            stay = (1.0 - TIME_STEP * acz) * b - TIME_STEP * (xp + xm + yp + ym)
            own.append(
                stay
                + TIME_STEP * (acz * shifted_z + from_low + from_high + inner)
            )
            rim.append(TIME_STEP * jnp.where(odd, xp, xm))
        ym = full[12]
        incident.append(jnp.where(low, ym, along(down(ym, -1), 64)))
    for values, out in ((own, own_ref), (rim, None)):
        packed = [values[0], values[4], values[8]]
        momenta = [0.0, 0.0, 0.0, 0.0]
        for s in range(S):
            m = SPECIES_MASS[s]
            d, px, py, e = values[4 * s : 4 * s + 4]
            momenta[0] = momenta[0] + m * px
            momenta[1] = momenta[1] + m * py
            momenta[2] = momenta[2] + (m * cz) * d
            momenta[3] = momenta[3] + m * (e + cz * cz * d)
        packed = packed + momenta
        if out is own_ref:
            last = jnp.where(
                row == 4,
                down(incident[0], 4),
                jnp.where(
                    row == 5,
                    down(incident[1], 5),
                    jnp.where(row == 6, down(incident[2], 6), 0.0),
                ),
            )
        else:
            last = jnp.zeros(TILE, jnp.float32)
        packed.append(last)
        for t in range(4):
            value = WEIGHT * jnp.where(row < 4, packed[2 * t], packed[2 * t + 1])
            if out is own_ref:
                out[t] = value
            else:
                to_right = jnp.where(odd, 0.0, down(value, -1))
                to_left = jnp.where(odd, down(value, 1), 0.0)
                to_far_ref[t] = jnp.where(second, to_right, to_left)
                to_near_ref[t] = jnp.where(second, to_left, to_right)


def own_speed_z():
    return speed_of(lax.axis_index("z") * lax.axis_size("x") + lax.axis_index("x"))


def selector(face_cell):
    column = lax.broadcasted_iota(jnp.int32, (128, 128), 0)
    return (column == face_cell).astype(jnp.float32)


def to_tile(value):
    row = rows() % 4
    low = lanes() < 64
    wide = jnp.broadcast_to(value, TILE)
    return jnp.where(
        jnp.logical_and(row == 0, low),
        wide,
        jnp.where(jnp.logical_and(row == 1, low), along(wide, 64), 0.0),
    )


def wall_kernel(
    stoich_ref, stick_ref, rates_ref, temp_ref, cover_ref, cell_ref, owner_ref,
    surface_ref, sums_ref, wall_x_ref, wall_y_ref,
):
    select = selector(cell_ref[...])
    pieces = jnp.concatenate(
        [cover_ref[...], temp_ref[...], owner_ref[...].astype(jnp.float32),
         jnp.zeros((2, 128), jnp.float32)], axis=0,
    )
    placed = lax.dot_general(
        pieces, select, (((1,), (1,)), ((), ())), precision=PRECISE,
        preferred_element_type=jnp.float32,
    )
    temp = placed[12:13]
    owner = placed[13:14]
    arrhenius = jnp.exp(ACTIVATION * (1.0 - 1.0 / temp))
    zero = jnp.zeros((1, 128), jnp.float32)
    masks = [jnp.abs(owner - float(p)) < 0.5 for p in range(PATCHES)]

    def by_owner(read):
        value = zero
        for p in range(PATCHES):
            value = jnp.where(masks[p], read(p), value)
        return value

    surface_ref[0] = jnp.concatenate([placed[0:12], jnp.zeros((4, 128), jnp.float32)], axis=0)
    desorb = [by_owner(lambda p: rates_ref[p, 0, j]) * arrhenius for j in range(NSURF)]
    lateral = [by_owner(lambda p: rates_ref[p, 1, j]) for j in range(NSURF)]
    stick = [by_owner(lambda p: stick_ref[p, s]) for s in range(S)]
    surface_ref[1] = jnp.concatenate(desorb + [zero] * 4, axis=0)
    surface_ref[2] = jnp.concatenate(lateral + [zero] * 4, axis=0)
    counts = [[stoich_ref[s, j].astype(jnp.float32) for s in range(S)] for j in range(NSURF)]
    for s in range(S):
        column_sum = counts[0][s]
        for j in range(1, NSURF):
            column_sum = column_sum + counts[j][s]
        into = jnp.concatenate(
            [(zero + counts[j][s]) / (zero + (1.0 + column_sum)) * stick[s] for j in range(NSURF)]
            + [zero] * 4, axis=0,
        )
        out = jnp.concatenate(
            [(zero + counts[j][s]) / (zero + (1.0 + counts[j][0] + counts[j][1] + counts[j][2]))
             for j in range(NSURF)]
            + [zero] * 4, axis=0,
        )
        surface_ref[3 + s] = into
        surface_ref[6 + s] = out

    k_rows = lax.broadcasted_iota(jnp.int32, (VG, 128), 0)
    c = speed_of(k_rows)
    up = jnp.maximum(c, 0.0)
    cz = own_speed_z()
    cy = c[VG // 2 :]
    temps = [temp, pltpu.roll(temp, 64, 1)]
    low = lax.broadcasted_iota(jnp.int32, (VG, 128), 1) < 64
    for s in range(S):
        m = SPECIES_MASS[s]
        e = jnp.exp(-m * (c * c) / (2.0 * temp))

        def total(v):
            return jnp.sum(v, axis=0, keepdims=True)

        s0 = total(e)
        s1 = total(c * e)
        s2 = total(c * c * e)
        u1 = total(up * e)
        u2 = total(up * c * e)
        u3 = total(up * c * c * e)
        norm = WEIGHT * u1 * s0 * s0
        scale = WEIGHT * TIME_STEP
        sums_ref[s] = jnp.concatenate(
            [
                1.0 / norm,
                scale * u1 * s0 * s0,
                scale * u1 * s1 * s0,
                scale * u2 * s0 * s0,
                scale * u1 * s0 * s1,
                scale * (u3 * s0 * s0 + u1 * s2 * s0 + u1 * s0 * s2),
                stick[s],
                zero,
            ],
            axis=0,
        )
        for x in range(CX):
            rate = -m / (2.0 * temps[x])
            wall_x_ref[s, x] = jnp.where(low, jnp.exp(rate * (c * c)), 0.0)
            wall_y_ref[s, x] = (cy / jnp.abs(cz)) * jnp.exp(rate * (cy * cy)) * jnp.exp(rate * (cz * cz))


def shift_kernel(s, f_ref, t_ref, z0_ref, z1_ref):
    low = lanes() < 64
    cz = own_speed_z()
    acz = jnp.abs(cz)
    coef_z = TIME_STEP * acz
    octet = speed_of(lax.broadcasted_iota(jnp.int32, TILE, 0))
    coef_x = [jnp.abs(octet + 8.0 * SPACING * q) / acz for q in range(4)]
    source = lax.broadcasted_iota(jnp.int32, (256, 128), 0) % 128
    target = lax.broadcasted_iota(jnp.int32, (256, 128), 1)
    wanted = target // 64 * 64 + (target % 64 + jnp.where(cz > 0.0, 63, 1)) % 64
    turn = (source == wanted).astype(jnp.float32).astype(jnp.bfloat16)

    def along_z(first, to):
        value = f_ref[pl.ds(first, GROUP)].reshape(GROUP * 128, 128)
        high = value.astype(jnp.bfloat16)
        rest = (value - high.astype(jnp.float32)).astype(jnp.bfloat16)
        to[...] = jnp.dot(
            jnp.concatenate([high, rest], axis=1), turn, preferred_element_type=jnp.float32
        )

    def advance(first, lower, z_ref):
        for i in range(GROUP):
            k = first + i
            coef_y = jnp.abs(speed_of(k % VG)) / acz
            own = (1.0 / coef_z - 1.0) - coef_y
            for q in range(4):
                f = [f_ref[k, pl.ds(32 * q + r, 8, 4), :] for r in range(4)]
                far = [along(v, 64) for v in f]
                coef_own = own - coef_x[q]
                for r in range(4):
                    h, x = r // 2, r % 2
                    value = coef_own * f[r] + z_ref[pl.ds(128 * i + 32 * q + r, 8, 4), :]
                    if q < 2 and x == 0:
                        value = value + coef_x[q] * f[r + 1]
                    if q >= 2 and x == 1:
                        value = value + coef_x[q] * f[r - 1]
                    if lower and h == 0:
                        value = value + jnp.where(low, 0.0, coef_y * far[r])
                    elif lower or h == 0:
                        value = value + coef_y * jnp.where(low, far[x], far[x + 2])
                    else:
                        value = value + coef_y * jnp.where(low, far[r], f[r])
                    t_ref[k - s * VG, 32 * r + 8 * q : 32 * r + 8 * q + 8, :] = value

    def one_chunk(c, lower):
        first = s * VG + c * KYS
        after = s * VG + jnp.minimum(c + 1, 3) * KYS
        along_z(first + GROUP, z1_ref)
        advance(first, lower, z0_ref)
        along_z(after, z0_ref)
        advance(first + GROUP, lower, z1_ref)

    along_z(s * VG, z0_ref)
    for lower in (False, True):

        def part(p, carry, lower=lower):
            one_chunk(2 * int(lower) + p, lower)
            return carry

        lax.fori_loop(0, 2, part, 0)


def step_kernel(
    part0_ref, part1_ref, part2_ref, part3_ref, surface_ref, sums_ref, cell_ref,
    wall_x_ref, wall_y_ref, far_ref, near_ref, t0_ref, t1_ref, t2_ref,
    cover_ref, out_hbm,
    out_ref, ex_ref, ey_ref, wy_ref, keep_ref, out_sem,
):
    row = rows()
    totals = []
    for t in range(4):
        totals.append((part0_ref[t] + part1_ref[t]) + (part2_ref[t] + part3_ref[t]))
    incident = [totals[3][4 + s : 5 + s] for s in range(S)]
    start = [surface_ref[0, j : j + 1, :] for j in range(NSURF)]
    desorb = [surface_ref[1, j : j + 1, :] for j in range(NSURF)]
    lateral = [surface_ref[2, j : j + 1, :] for j in range(NSURF)]
    feed = [
        surface_ref[3, j : j + 1, :] * incident[0]
        + surface_ref[4, j : j + 1, :] * incident[1]
        + surface_ref[5, j : j + 1, :] * incident[2]
        for j in range(NSURF)
    ]

    def tree(values):
        values = list(values)
        while len(values) > 1:
            values = [
                values[i] + values[i + 1] if i + 1 < len(values) else values[i]
                for i in range(0, len(values), 2)
            ]
        return values[0]

    def total(v):
        return jnp.sum(v, axis=0, keepdims=True)

    covers = start
    for _ in range(NEWTON):
        vacant = 1.0 - tree(covers)
        scaled, coupling = [], []
        for j in range(NSURF):
            th = covers[j]
            squared = lateral[j] * (th * th)
            net = feed[j] * vacant - desorb[j] * th - squared * th
            residual = th - start[j] - SURFACE_STEP * net
            inverse = 1.0 / (1.0 + SURFACE_STEP * (desorb[j] + 3.0 * squared))
            scaled.append(residual * inverse)
            coupling.append((SURFACE_STEP * feed[j]) * inverse)
        ratio = tree(scaled) / (1.0 + tree(coupling))
        covers = [
            th - DAMPING * (y - u * ratio) for th, y, u in zip(covers, scaled, coupling)
        ]
    released = [
        desorb[j] * covers[j] + lateral[j] * (covers[j] * covers[j] * covers[j])
        for j in range(NSURF)
    ]
    vacant = 1.0 - tree(covers)

    def quantity(q):
        v = totals[q // 2]
        other = down(v, 4)
        return jnp.where(row < 4, v, other) if q % 2 == 0 else jnp.where(row < 4, other, v)

    dens = [quantity(s) for s in range(S)]
    mom = [quantity(3 + a) for a in range(3)]
    energy = quantity(6)
    wall_dens = []
    wall_mom = [0.0, 0.0, 0.0]
    wall_energy = 0.0
    for s in range(S):
        m = SPECIES_MASS[s]
        emitted = incident[s] * (1.0 - sums_ref[s, 6:7] * vacant) + tree(
            [surface_ref[6 + s, j : j + 1, :] * released[j] for j in range(NSURF)]
        )
        wd = emitted * sums_ref[s, 0:1]
        wall_dens.append(wd)
        dens[s] = dens[s] + to_tile(wd * sums_ref[s, 1:2])
        for a in range(3):
            wall_mom[a] = wall_mom[a] + (m * wd) * sums_ref[s, 2 + a : 3 + a]
        wall_energy = wall_energy + (m * wd) * sums_ref[s, 5:6]
    mom = [mom[a] + to_tile(wall_mom[a]) for a in range(3)]
    energy = energy + to_tile(wall_energy)
    gas = dens[0] + dens[1] + dens[2]
    mass = SPECIES_MASS[0] * dens[0] + SPECIES_MASS[1] * dens[1] + SPECIES_MASS[2] * dens[2]
    bulk = [v / mass for v in mom]
    flow = bulk[0] * bulk[0] + bulk[1] * bulk[1] + bulk[2] * bulk[2]
    temperature = (energy - mass * flow) / (3.0 * gas)
    cz = own_speed_z()
    acz = jnp.abs(cz)
    coef_z = TIME_STEP * acz
    grid = speed_of(lax.broadcasted_iota(jnp.int32, (VG, 128), 0))
    for s in range(S):
        rate = -SPECIES_MASS[s] / (2.0 * temperature)
        keep = jnp.exp((-TIME_STEP * COLLISION_RATE[s]) * gas)
        off = cz - bulk[2]
        scale = (1.0 - keep) * dens[s] * jnp.exp(rate * (off * off))
        keep_ref[s] = coef_z * keep
        for r in range(4):
            at = slice(r, r + 1)

            def table(drift):
                gap = grid - drift[at]
                return jnp.exp(rate[at] * (gap * gap))

            ex = table(bulk[0])
            ey = table(bulk[1])
            factor = scale[at] / (WEIGHT * total(ex) * total(ey) * total(table(bulk[2])))
            ex_ref[s, r] = ex
            ey_ref[s, r] = ey * factor
        other = pltpu.roll(wall_dens[s], 64, 1)
        wy_ref[s, 0] = wall_y_ref[s, 0] * wall_dens[s]
        wy_ref[s, 1] = wall_y_ref[s, 1] * other

    octet = speed_of(lax.broadcasted_iota(jnp.int32, TILE, 0))
    coef_x = [jnp.abs(octet + 8.0 * SPACING * q) / acz for q in range(4)]
    second = lax.axis_index("space") % 2 == 1

    def advance(first, s, lower):
        t_ref = (t0_ref, t1_ref, t2_ref)[s]
        keep = [jnp.broadcast_to(keep_ref[s, r : r + 1, :], TILE) for r in range(4)]
        for i in range(GROUP):
            k = first + i
            ky = k - s * VG
            ey = [jnp.broadcast_to(ey_ref[s, r, pl.ds(ky, 1), :], TILE) for r in range(4)]
            if lower:
                wy = [
                    jnp.broadcast_to(wy_ref[s, x, pl.ds(ky - PAIRS, 1), :], TILE)
                    for x in range(CX)
                ]
            for q in range(4):
                for r in range(4):
                    h, x = r // 2, r % 2
                    value = t_ref[ky, 32 * r + 8 * q : 32 * r + 8 * q + 8, :]
                    at = pl.ds(16 * h + 8 * (q % 2), 8)
                    if q < 2 and x == 1:
                        beside = jnp.where(second, far_ref[k, at, :], near_ref[k, at, :])
                        value = value + coef_x[q] * beside
                    if q >= 2 and x == 0:
                        beside = jnp.where(second, near_ref[k, at, :], far_ref[k, at, :])
                        value = value + coef_x[q] * beside
                    if lower and h == 0:
                        value = value + wall_x_ref[s, x, 8 * q : 8 * q + 8, :] * wy[x]
                    value = keep[r] * value + ex_ref[s, r, 8 * q : 8 * q + 8, :] * ey[r]
                    out_ref[k, pl.ds(32 * q + r, 8, 4), :] = value

    for s in range(S):
        for lower in (False, True):

            def part(p, carry, s=s, lower=lower):
                g = 8 * s + 4 * int(lower) + p
                advance(g * GROUP, s, lower)
                half_chunk(out_ref, out_hbm, out_sem, g).start()
                return carry

            lax.fori_loop(0, 4, part, 0)
    cover_ref[...] = jnp.dot(
        jnp.concatenate(covers, axis=0), selector(cell_ref[...]), precision=PRECISE,
        preferred_element_type=jnp.float32,
    )
    for c in range(2 * BLOCKS):
        half_chunk(out_ref, out_hbm, out_sem, c).wait()


SMEM = pl.BlockSpec(memory_space=pltpu.SMEM)
VMEM = pl.BlockSpec(memory_space=pltpu.VMEM)
HBM = pl.BlockSpec(memory_space=pl.ANY)
F32 = jnp.float32
BIG = pltpu.CompilerParams(vmem_limit_bytes=16 * 1024 * 1024)
SMALL = pltpu.CompilerParams(vmem_limit_bytes=4 * 1024 * 1024)
DMA = pltpu.SemaphoreType.DMA
LONG = pl.CostEstimate(flops=10**10, bytes_accessed=10**7, transcendentals=0)


def shape(*dims):
    return jax.ShapeDtypeStruct(dims, F32)


def near(value):
    return pltpu.with_memory_space_constraint(value, pltpu.VMEM)


def moments_call(field):
    return pl.pallas_call(
        moments_kernel,
        in_specs=[HBM],
        out_specs=[VMEM] * 6,
        out_shape=[pltpu.VMEM((4, 8, 128), F32)] * 3
        + [pltpu.VMEM((S * VG, 128, 128), F32)]
        + [pltpu.VMEM((S * VG, 32, 128), F32)] * 2,
        scratch_shapes=[
            pltpu.VMEM((S, 20, 8, 128), F32),
            DMA((BLOCKS,)),
        ],
        compiler_params=BIG,
    )(field)


def wall_call(*args):
    return pl.pallas_call(
        wall_kernel,
        in_specs=[SMEM] * 3 + [VMEM] * 4,
        out_specs=[VMEM] * 4,
        out_shape=[
            pltpu.VMEM((9, 16, 128), F32),
            pltpu.VMEM((S, 8, 128), F32),
            pltpu.VMEM((S, CX, VG, 128), F32),
            pltpu.VMEM((S, CX, VG // 2, 128), F32),
        ],
        compiler_params=SMALL,
    )(*args)


def shift_call(s, field):
    return pl.pallas_call(
        functools.partial(shift_kernel, s),
        in_specs=[VMEM],
        out_specs=VMEM,
        out_shape=pltpu.VMEM((VG, 128, 128), F32),
        scratch_shapes=[
            pltpu.VMEM((GROUP * 128, 128), F32),
            pltpu.VMEM((GROUP * 128, 128), F32),
        ],
        compiler_params=BIG,
        cost_estimate=LONG,
    )(near(field))


def step_call(*args):
    return pl.pallas_call(
        step_kernel,
        in_specs=[VMEM] * 14,
        out_specs=[VMEM, HBM],
        out_shape=[shape(NSURF, 128), shape(S * VG, 128, 128)],
        scratch_shapes=[
            pltpu.VMEM((S * VG, 128, 128), F32),
            pltpu.VMEM((S, 4, VG, 128), F32),
            pltpu.VMEM((S, 4, VG, 128), F32),
            pltpu.VMEM((S, CX, VG // 2, 128), F32),
            pltpu.VMEM((S, 8, 128), F32),
            DMA((2 * BLOCKS,)),
        ],
        compiler_params=BIG,
    )(*args)


def paired(value, axis, by=1):
    peers = lax.axis_size(axis)
    return lax.ppermute(value, axis, [(i, i ^ by) for i in range(peers)])


def crossed(value, axis, by):
    peers = lax.axis_size(axis)
    pairs = [(i, (i + (by if i % 2 else -by)) % peers) for i in range(peers)]
    return lax.ppermute(value, axis, pairs)


def per_device(
    distribution, wall_temp, coverage, face_cell, face_owner, stoichiometry, sticking, surface_rates
):
    field = (
        distribution.reshape(S, VG * VG, CX, 2, 128)
        .transpose(0, 1, 3, 2, 4)
        .reshape(S * VG, 128, 128)
    )
    field = pltpu.with_memory_space_constraint(field, pltpu.HBM)
    own, to_far, to_near, held, far, nigh = moments_call(field)
    together = lax.optimization_barrier
    face_row = face_cell.reshape(1, 128)

    own = own + crossed(to_far, "space", 1) + paired(to_near, "space")
    own, held = together((own, held))

    far = crossed(near(far), "space", 1)
    nigh = paired(near(nigh), "space")
    moved0 = shift_call(0, held)
    own = own + paired(own, "x", 1) + paired(own, "x", 3) + paired(own, "x", 2)
    own, moved0, held = together((own, moved0, held))

    temp, own = together((wall_temp.reshape(1, 128), own))
    walls = wall_call(
        stoichiometry.T, sticking, surface_rates, temp, coverage, face_row,
        face_owner.reshape(1, 128),
    )
    moved1 = shift_call(1, held)
    own = own + paired(own, "z")
    own, moved1, held, walls = together((own, moved1, held, walls))

    moved2 = shift_call(2, held)
    parts = [own] + [crossed(own, "z", by) for by in (1, 2, 3)]
    surface, sums, wall_x, wall_y = walls
    vmem = [near(v) for v in parts + [surface, sums]]
    covers, advanced = step_call(
        *vmem, face_row, near(wall_x), near(wall_y), near(far), near(nigh),
        near(moved0), near(moved1), near(moved2),
    )
    advanced = (
        advanced.reshape(S, VG * VG, 2, CX, 128)
        .transpose(0, 1, 3, 2, 4)
        .reshape(distribution.shape)
    )
    return advanced, covers


def solution(mesh):
    fine = Mesh(mesh.devices.reshape(N_Z, N_X, mesh.shape["space"]), ("z", "x", "space"))
    return jax.shard_map(
        per_device,
        mesh=fine,
        in_specs=(
            P(None, ("z", "x"), "space", None),
            P("space"),
            P(None, "space"),
            P("space", None),
            P("space"),
            P(),
            P(),
            P(),
        ),
        out_specs=(P(None, ("z", "x"), "space", None), P(None, "space")),
        check_vma=False,
    )
```

```python
import functools

import jax
import jax.numpy as jnp
from jax import lax
from jax.experimental import pallas as pl
from jax.experimental.pallas import tpu as pltpu
from jax.sharding import Mesh
from jax.sharding import PartitionSpec as P

S = 3
VG = 32
NZ = 64
CX = 2
NEWTON = 8
NSURF = 12
PATCHES = 4
N_Z = 8
N_X = 4

SPEED_LIMIT = 4.0
SPACING = 2.0 * SPEED_LIMIT / VG
WEIGHT = SPACING * SPACING * SPACING
SPECIES_MASS = (1.0, 2.0, 4.0)
COLLISION_RATE = (0.3, 0.2, 0.15)
TIME_STEP = 0.08
SURFACE_STEP = 2.0
DAMPING = 0.25
ACTIVATION = 2.0

PAIRS = VG // 2
HALF = PAIRS // 2
BLOCKS = 12
KYS = S * VG // BLOCKS
GROUP = KYS // 2
TILE = (8, 128)
PRECISE = lax.Precision.HIGHEST


def rows():
    return lax.broadcasted_iota(jnp.int32, TILE, 0)


def lanes():
    return lax.broadcasted_iota(jnp.int32, TILE, 1)


def down(value, by):
    return pltpu.roll(value, by % 8, 0)


def along(value, by):
    return pltpu.roll(value, by % 128, 1)


def pair_speed():
    parity = (rows() >= 4).astype(jnp.float32)
    return (parity + 0.5) * SPACING - SPEED_LIMIT


def speed_of(position):
    return (position.astype(jnp.float32) + 0.5) * SPACING - SPEED_LIMIT


def chunk(src, dst, sems, c):
    part = pl.ds(c * KYS, KYS)
    return pltpu.make_async_copy(src.at[part], dst.at[part], sems.at[c])


def half_chunk(src, dst, sems, c):
    part = pl.ds(c * GROUP, GROUP)
    return pltpu.make_async_copy(src.at[part], dst.at[part], sems.at[c])


def moments_kernel(
    f_hbm, own_ref, to_far_ref, to_near_ref, f_ref, far_ref, near_ref, acc_ref, f_sem,
):
    for c in range(BLOCKS):
        chunk(f_hbm, f_ref, f_sem, c).start()
    base = pair_speed()
    speeds = [jnp.abs(base + 2.0 * SPACING * j) for j in range(PAIRS)]
    acc_ref[...] = jnp.zeros_like(acc_ref)
    second = lax.axis_index("space") % 2 == 1
    far_row = jnp.where(second, 65, 0)
    near_row = 65 - far_row

    def one(k, carry):
        zero = jnp.zeros(TILE, jnp.float32)
        sums = []
        for side in range(2):
            n0, n1, n2, n3 = zero, zero, zero, zero
            for j in range(side * HALF, (side + 1) * HALF):
                f = f_ref[k, 8 * j : 8 * j + 8, :]
                g = f * speeds[j]
                n0 = n0 + f
                n1 = n1 + g
                g = g * speeds[j]
                n2 = n2 + g
                n3 = n3 + g * speeds[j]
            sums.append((n0, n1, n2, n3))
        (a0, a1, a2, a3), (b0, b1, b2, b3) = sums
        for h in range(2):
            for q in range(2):
                to = pl.ds(16 * h + 8 * q, 8)
                far_ref[k, to, :] = f_ref[k, pl.ds(far_row + 32 * q + 2 * h, 8, 4), :]
                near_ref[k, to, :] = f_ref[k, pl.ds(near_row + 32 * q + 2 * h, 8, 4), :]
        cy = speed_of(k % VG)
        cy2 = cy * cy
        acy = jnp.abs(cy)
        d = a0 + b0
        x1 = b1 - a1
        e = a2 + b2 + cy2 * d
        yd = cy * d
        new = (
            d, x1, yd, e,
            b1, b2, cy * b1, b3 + cy2 * b1,
            a1, -a2, cy * a1, a3 + cy2 * a1,
            acy * d, acy * x1, acy * yd, acy * e,
        )
        return tuple(c + n for c, n in zip(carry, new))

    start = tuple(jnp.zeros(TILE, jnp.float32) for _ in range(16))
    def turn(c, carry):
        species, half = c // 4, c % 4 // 2
        chunk(f_hbm, f_ref, f_sem, c).wait()
        total = lax.fori_loop(0, KYS, lambda i, v: one(c * KYS + i, v), start, unroll=8)
        for q in range(12):
            acc_ref[species, q] += total[q]
        for q in range(4):
            acc_ref[species, 12 + 4 * half + q] += total[12 + q]
        return carry

    lax.fori_loop(0, BLOCKS, turn, 0)
    row = rows()
    lane = lanes()
    cz = own_speed_z()
    acz = jnp.abs(cz)
    rise = cz > 0.0
    odd = row % 2 == 1
    upper_h = (row // 2) % 2 == 1
    low = lane < 64
    own = []
    rim = []
    incident = []
    for s in range(S):
        full = []
        for q in range(20):
            v = acc_ref[s, q]
            full.append(v + down(v, 4))
        for q in range(4):
            b, xp, xm = full[q], full[4 + q], full[8 + q]
            ym, yp = full[12 + q], full[16 + q]
            zp = jnp.where(lane % 64 == 0, along(b, 65), along(b, 1))
            zm = jnp.where(lane % 64 == 63, along(b, 63), along(b, 127))
            shifted_z = jnp.where(rise, zp, zm)
            rp = along(yp, 64)
            rm = along(ym, 64)
            from_low = jnp.where(low, jnp.where(upper_h, down(rp, 2), 0.0), rp)
            from_high = jnp.where(low, rm, jnp.where(upper_h, ym, down(rm, -2)))
            inner = jnp.where(odd, down(xp, 1), down(xm, -1))
            stay = (1.0 - TIME_STEP * acz) * b - TIME_STEP * (xp + xm + yp + ym)
            own.append(
                stay
                + TIME_STEP * (acz * shifted_z + from_low + from_high + inner)
            )
            rim.append(TIME_STEP * jnp.where(odd, xp, xm))
        ym = full[12]
        incident.append(jnp.where(low, ym, along(down(ym, -1), 64)))
    for values, out in ((own, own_ref), (rim, None)):
        packed = [values[0], values[4], values[8]]
        momenta = [0.0, 0.0, 0.0, 0.0]
        for s in range(S):
            m = SPECIES_MASS[s]
            d, px, py, e = values[4 * s : 4 * s + 4]
            momenta[0] = momenta[0] + m * px
            momenta[1] = momenta[1] + m * py
            momenta[2] = momenta[2] + (m * cz) * d
            momenta[3] = momenta[3] + m * (e + cz * cz * d)
        packed = packed + momenta
        if out is own_ref:
            last = jnp.where(
                row == 4,
                down(incident[0], 4),
                jnp.where(
                    row == 5,
                    down(incident[1], 5),
                    jnp.where(row == 6, down(incident[2], 6), 0.0),
                ),
            )
        else:
            last = jnp.zeros(TILE, jnp.float32)
        packed.append(last)
        for t in range(4):
            value = WEIGHT * jnp.where(row < 4, packed[2 * t], packed[2 * t + 1])
            if out is own_ref:
                out[t] = value
            else:
                to_right = jnp.where(odd, 0.0, down(value, -1))
                to_left = jnp.where(odd, down(value, 1), 0.0)
                to_far_ref[t] = jnp.where(second, to_right, to_left)
                to_near_ref[t] = jnp.where(second, to_left, to_right)


def own_speed_z():
    return speed_of(lax.axis_index("z") * lax.axis_size("x") + lax.axis_index("x"))


def selector(face_cell):
    column = lax.broadcasted_iota(jnp.int32, (128, 128), 0)
    return (column == face_cell).astype(jnp.float32)


def to_tile(value):
    row = rows() % 4
    low = lanes() < 64
    wide = jnp.broadcast_to(value, TILE)
    return jnp.where(
        jnp.logical_and(row == 0, low),
        wide,
        jnp.where(jnp.logical_and(row == 1, low), along(wide, 64), 0.0),
    )


def wall_kernel(
    stoich_ref, stick_ref, rates_ref, temp_ref, cover_ref, cell_ref, owner_ref,
    surface_ref, sums_ref, wall_x_ref, wall_y_ref,
):
    select = selector(cell_ref[...])
    pieces = jnp.concatenate(
        [cover_ref[...], temp_ref[...], owner_ref[...].astype(jnp.float32),
         jnp.zeros((2, 128), jnp.float32)], axis=0,
    )
    placed = lax.dot_general(
        pieces, select, (((1,), (1,)), ((), ())), precision=PRECISE,
        preferred_element_type=jnp.float32,
    )
    temp = placed[12:13]
    owner = placed[13:14]
    arrhenius = jnp.exp(ACTIVATION * (1.0 - 1.0 / temp))
    zero = jnp.zeros((1, 128), jnp.float32)
    masks = [jnp.abs(owner - float(p)) < 0.5 for p in range(PATCHES)]

    def by_owner(read):
        value = zero
        for p in range(PATCHES):
            value = jnp.where(masks[p], read(p), value)
        return value

    surface_ref[0] = jnp.concatenate([placed[0:12], jnp.zeros((4, 128), jnp.float32)], axis=0)
    desorb = [by_owner(lambda p: rates_ref[p, 0, j]) * arrhenius for j in range(NSURF)]
    lateral = [by_owner(lambda p: rates_ref[p, 1, j]) for j in range(NSURF)]
    stick = [by_owner(lambda p: stick_ref[p, s]) for s in range(S)]
    surface_ref[1] = jnp.concatenate(desorb + [zero] * 4, axis=0)
    surface_ref[2] = jnp.concatenate(lateral + [zero] * 4, axis=0)
    counts = [[stoich_ref[s, j].astype(jnp.float32) for s in range(S)] for j in range(NSURF)]
    for s in range(S):
        column_sum = counts[0][s]
        for j in range(1, NSURF):
            column_sum = column_sum + counts[j][s]
        into = jnp.concatenate(
            [(zero + counts[j][s]) / (zero + (1.0 + column_sum)) * stick[s] for j in range(NSURF)]
            + [zero] * 4, axis=0,
        )
        out = jnp.concatenate(
            [(zero + counts[j][s]) / (zero + (1.0 + counts[j][0] + counts[j][1] + counts[j][2]))
             for j in range(NSURF)]
            + [zero] * 4, axis=0,
        )
        surface_ref[3 + s] = into
        surface_ref[6 + s] = out

    k_rows = lax.broadcasted_iota(jnp.int32, (VG, 128), 0)
    c = speed_of(k_rows)
    up = jnp.maximum(c, 0.0)
    cz = own_speed_z()
    cy = c[VG // 2 :]
    temps = [temp, pltpu.roll(temp, 64, 1)]
    low = lax.broadcasted_iota(jnp.int32, (VG, 128), 1) < 64
    for s in range(S):
        m = SPECIES_MASS[s]
        e = jnp.exp(-m * (c * c) / (2.0 * temp))

        def total(v):
            return jnp.sum(v, axis=0, keepdims=True)

        s0 = total(e)
        s1 = total(c * e)
        s2 = total(c * c * e)
        u1 = total(up * e)
        u2 = total(up * c * e)
        u3 = total(up * c * c * e)
        norm = WEIGHT * u1 * s0 * s0
        scale = WEIGHT * TIME_STEP
        sums_ref[s] = jnp.concatenate(
            [
                1.0 / norm,
                scale * u1 * s0 * s0,
                scale * u1 * s1 * s0,
                scale * u2 * s0 * s0,
                scale * u1 * s0 * s1,
                scale * (u3 * s0 * s0 + u1 * s2 * s0 + u1 * s0 * s2),
                stick[s],
                zero,
            ],
            axis=0,
        )
        for x in range(CX):
            rate = -m / (2.0 * temps[x])
            wall_x_ref[s, x] = jnp.where(low, jnp.exp(rate * (c * c)), 0.0)
            wall_y_ref[s, x] = (cy / jnp.abs(cz)) * jnp.exp(rate * (cy * cy)) * jnp.exp(rate * (cz * cz))


def shift_kernel(s, f_ref, t_ref, z0_ref, z1_ref):
    low = lanes() < 64
    cz = own_speed_z()
    acz = jnp.abs(cz)
    coef_z = TIME_STEP * acz
    octet = speed_of(lax.broadcasted_iota(jnp.int32, TILE, 0))
    coef_x = [jnp.abs(octet + 8.0 * SPACING * q) / acz for q in range(4)]
    source = lax.broadcasted_iota(jnp.int32, (256, 128), 0) % 128
    target = lax.broadcasted_iota(jnp.int32, (256, 128), 1)
    wanted = target // 64 * 64 + (target % 64 + jnp.where(cz > 0.0, 63, 1)) % 64
    turn = (source == wanted).astype(jnp.float32).astype(jnp.bfloat16)

    def along_z(first, to):
        value = f_ref[pl.ds(first, GROUP)].reshape(GROUP * 128, 128)
        high = value.astype(jnp.bfloat16)
        rest = (value - high.astype(jnp.float32)).astype(jnp.bfloat16)
        to[...] = jnp.dot(
            jnp.concatenate([high, rest], axis=1), turn, preferred_element_type=jnp.float32
        )

    def advance(first, lower, z_ref):
        for i in range(GROUP):
            k = first + i
            coef_y = jnp.abs(speed_of(k % VG)) / acz
            own = (1.0 / coef_z - 1.0) - coef_y
            for q in range(4):
                f = [f_ref[k, pl.ds(32 * q + r, 8, 4), :] for r in range(4)]
                far = [along(v, 64) for v in f]
                coef_own = own - coef_x[q]
                for r in range(4):
                    h, x = r // 2, r % 2
                    value = coef_own * f[r] + z_ref[pl.ds(128 * i + 32 * q + r, 8, 4), :]
                    if q < 2 and x == 0:
                        value = value + coef_x[q] * f[r + 1]
                    if q >= 2 and x == 1:
                        value = value + coef_x[q] * f[r - 1]
                    if lower and h == 0:
                        value = value + jnp.where(low, 0.0, coef_y * far[r])
                    elif lower or h == 0:
                        value = value + coef_y * jnp.where(low, far[x], far[x + 2])
                    else:
                        value = value + coef_y * jnp.where(low, far[r], f[r])
                    t_ref[k - s * VG, 32 * r + 8 * q : 32 * r + 8 * q + 8, :] = value

    def one_chunk(c, lower):
        first = s * VG + c * KYS
        after = s * VG + jnp.minimum(c + 1, 3) * KYS
        along_z(first + GROUP, z1_ref)
        advance(first, lower, z0_ref)
        along_z(after, z0_ref)
        advance(first + GROUP, lower, z1_ref)

    along_z(s * VG, z0_ref)
    for lower in (False, True):

        def part(p, carry, lower=lower):
            one_chunk(2 * int(lower) + p, lower)
            return carry

        lax.fori_loop(0, 2, part, 0)


def step_kernel(
    part0_ref, part1_ref, part2_ref, part3_ref, surface_ref, sums_ref, cell_ref,
    wall_x_ref, wall_y_ref, far_ref, near_ref, t0_ref, t1_ref, t2_ref,
    cover_ref, out_hbm,
    out_ref, ex_ref, ey_ref, wy_ref, keep_ref, out_sem,
):
    row = rows()
    totals = []
    for t in range(4):
        totals.append((part0_ref[t] + part1_ref[t]) + (part2_ref[t] + part3_ref[t]))
    incident = [totals[3][4 + s : 5 + s] for s in range(S)]
    start = [surface_ref[0, j : j + 1, :] for j in range(NSURF)]
    desorb = [surface_ref[1, j : j + 1, :] for j in range(NSURF)]
    lateral = [surface_ref[2, j : j + 1, :] for j in range(NSURF)]
    feed = [
        surface_ref[3, j : j + 1, :] * incident[0]
        + surface_ref[4, j : j + 1, :] * incident[1]
        + surface_ref[5, j : j + 1, :] * incident[2]
        for j in range(NSURF)
    ]

    def tree(values):
        values = list(values)
        while len(values) > 1:
            values = [
                values[i] + values[i + 1] if i + 1 < len(values) else values[i]
                for i in range(0, len(values), 2)
            ]
        return values[0]

    def total(v):
        return jnp.sum(v, axis=0, keepdims=True)

    covers = start
    for _ in range(NEWTON):
        vacant = 1.0 - tree(covers)
        scaled, coupling = [], []
        for j in range(NSURF):
            th = covers[j]
            squared = lateral[j] * (th * th)
            net = feed[j] * vacant - desorb[j] * th - squared * th
            residual = th - start[j] - SURFACE_STEP * net
            inverse = 1.0 / (1.0 + SURFACE_STEP * (desorb[j] + 3.0 * squared))
            scaled.append(residual * inverse)
            coupling.append((SURFACE_STEP * feed[j]) * inverse)
        ratio = tree(scaled) / (1.0 + tree(coupling))
        covers = [
            th - DAMPING * (y - u * ratio) for th, y, u in zip(covers, scaled, coupling)
        ]
    released = [
        desorb[j] * covers[j] + lateral[j] * (covers[j] * covers[j] * covers[j])
        for j in range(NSURF)
    ]
    vacant = 1.0 - tree(covers)

    def quantity(q):
        v = totals[q // 2]
        other = down(v, 4)
        return jnp.where(row < 4, v, other) if q % 2 == 0 else jnp.where(row < 4, other, v)

    dens = [quantity(s) for s in range(S)]
    mom = [quantity(3 + a) for a in range(3)]
    energy = quantity(6)
    wall_dens = []
    wall_mom = [0.0, 0.0, 0.0]
    wall_energy = 0.0
    for s in range(S):
        m = SPECIES_MASS[s]
        emitted = incident[s] * (1.0 - sums_ref[s, 6:7] * vacant) + tree(
            [surface_ref[6 + s, j : j + 1, :] * released[j] for j in range(NSURF)]
        )
        wd = emitted * sums_ref[s, 0:1]
        wall_dens.append(wd)
        dens[s] = dens[s] + to_tile(wd * sums_ref[s, 1:2])
        for a in range(3):
            wall_mom[a] = wall_mom[a] + (m * wd) * sums_ref[s, 2 + a : 3 + a]
        wall_energy = wall_energy + (m * wd) * sums_ref[s, 5:6]
    mom = [mom[a] + to_tile(wall_mom[a]) for a in range(3)]
    energy = energy + to_tile(wall_energy)
    gas = dens[0] + dens[1] + dens[2]
    mass = SPECIES_MASS[0] * dens[0] + SPECIES_MASS[1] * dens[1] + SPECIES_MASS[2] * dens[2]
    bulk = [v / mass for v in mom]
    flow = bulk[0] * bulk[0] + bulk[1] * bulk[1] + bulk[2] * bulk[2]
    temperature = (energy - mass * flow) / (3.0 * gas)
    cz = own_speed_z()
    acz = jnp.abs(cz)
    coef_z = TIME_STEP * acz
    grid = speed_of(lax.broadcasted_iota(jnp.int32, (VG, 128), 0))
    for s in range(S):
        rate = -SPECIES_MASS[s] / (2.0 * temperature)
        keep = jnp.exp((-TIME_STEP * COLLISION_RATE[s]) * gas)
        off = cz - bulk[2]
        scale = (1.0 - keep) * dens[s] * jnp.exp(rate * (off * off))
        keep_ref[s] = coef_z * keep
        for r in range(4):
            at = slice(r, r + 1)

            def table(drift):
                gap = grid - drift[at]
                return jnp.exp(rate[at] * (gap * gap))

            ex = table(bulk[0])
            ey = table(bulk[1])
            factor = scale[at] / (WEIGHT * total(ex) * total(ey) * total(table(bulk[2])))
            ex_ref[s, r] = ex
            ey_ref[s, r] = ey * factor
        other = pltpu.roll(wall_dens[s], 64, 1)
        wy_ref[s, 0] = wall_y_ref[s, 0] * wall_dens[s]
        wy_ref[s, 1] = wall_y_ref[s, 1] * other

    octet = speed_of(lax.broadcasted_iota(jnp.int32, TILE, 0))
    coef_x = [jnp.abs(octet + 8.0 * SPACING * q) / acz for q in range(4)]
    second = lax.axis_index("space") % 2 == 1

    def advance(first, s, lower):
        t_ref = (t0_ref, t1_ref, t2_ref)[s]
        keep = [jnp.broadcast_to(keep_ref[s, r : r + 1, :], TILE) for r in range(4)]
        for i in range(GROUP):
            k = first + i
            ky = k - s * VG
            ey = [jnp.broadcast_to(ey_ref[s, r, pl.ds(ky, 1), :], TILE) for r in range(4)]
            if lower:
                wy = [
                    jnp.broadcast_to(wy_ref[s, x, pl.ds(ky - PAIRS, 1), :], TILE)
                    for x in range(CX)
                ]
            for q in range(4):
                for r in range(4):
                    h, x = r // 2, r % 2
                    value = t_ref[ky, 32 * r + 8 * q : 32 * r + 8 * q + 8, :]
                    at = pl.ds(16 * h + 8 * (q % 2), 8)
                    if q < 2 and x == 1:
                        beside = jnp.where(second, far_ref[k, at, :], near_ref[k, at, :])
                        value = value + coef_x[q] * beside
                    if q >= 2 and x == 0:
                        beside = jnp.where(second, near_ref[k, at, :], far_ref[k, at, :])
                        value = value + coef_x[q] * beside
                    if lower and h == 0:
                        value = value + wall_x_ref[s, x, 8 * q : 8 * q + 8, :] * wy[x]
                    value = keep[r] * value + ex_ref[s, r, 8 * q : 8 * q + 8, :] * ey[r]
                    out_ref[k, pl.ds(32 * q + r, 8, 4), :] = value

    for s in range(S):
        for lower in (False, True):

            def part(p, carry, s=s, lower=lower):
                g = 8 * s + 4 * int(lower) + p
                advance(g * GROUP, s, lower)
                half_chunk(out_ref, out_hbm, out_sem, g).start()
                return carry

            lax.fori_loop(0, 4, part, 0)
    cover_ref[...] = jnp.dot(
        jnp.concatenate(covers, axis=0), selector(cell_ref[...]), precision=PRECISE,
        preferred_element_type=jnp.float32,
    )
    for c in range(2 * BLOCKS):
        half_chunk(out_ref, out_hbm, out_sem, c).wait()


SMEM = pl.BlockSpec(memory_space=pltpu.SMEM)
VMEM = pl.BlockSpec(memory_space=pltpu.VMEM)
HBM = pl.BlockSpec(memory_space=pl.ANY)
F32 = jnp.float32
BIG = pltpu.CompilerParams(vmem_limit_bytes=16 * 1024 * 1024)
SMALL = pltpu.CompilerParams(vmem_limit_bytes=4 * 1024 * 1024)
DMA = pltpu.SemaphoreType.DMA
LONG = pl.CostEstimate(flops=10**10, bytes_accessed=10**7, transcendentals=0)


def shape(*dims):
    return jax.ShapeDtypeStruct(dims, F32)


def near(value):
    return pltpu.with_memory_space_constraint(value, pltpu.VMEM)


def moments_call(field):
    return pl.pallas_call(
        moments_kernel,
        in_specs=[HBM],
        out_specs=[VMEM] * 6,
        out_shape=[pltpu.VMEM((4, 8, 128), F32)] * 3
        + [pltpu.VMEM((S * VG, 128, 128), F32)]
        + [pltpu.VMEM((S * VG, 32, 128), F32)] * 2,
        scratch_shapes=[
            pltpu.VMEM((S, 20, 8, 128), F32),
            DMA((BLOCKS,)),
        ],
        compiler_params=BIG,
    )(field)


def wall_call(*args):
    return pl.pallas_call(
        wall_kernel,
        in_specs=[SMEM] * 3 + [VMEM] * 4,
        out_specs=[VMEM] * 4,
        out_shape=[
            pltpu.VMEM((9, 16, 128), F32),
            pltpu.VMEM((S, 8, 128), F32),
            pltpu.VMEM((S, CX, VG, 128), F32),
            pltpu.VMEM((S, CX, VG // 2, 128), F32),
        ],
        compiler_params=SMALL,
    )(*args)


def shift_call(s, field):
    return pl.pallas_call(
        functools.partial(shift_kernel, s),
        in_specs=[VMEM],
        out_specs=VMEM,
        out_shape=pltpu.VMEM((VG, 128, 128), F32),
        scratch_shapes=[
            pltpu.VMEM((GROUP * 128, 128), F32),
            pltpu.VMEM((GROUP * 128, 128), F32),
        ],
        compiler_params=BIG,
        cost_estimate=LONG,
    )(near(field))


def step_call(*args):
    return pl.pallas_call(
        step_kernel,
        in_specs=[VMEM] * 14,
        out_specs=[VMEM, HBM],
        out_shape=[shape(NSURF, 128), shape(S * VG, 128, 128)],
        scratch_shapes=[
            pltpu.VMEM((S * VG, 128, 128), F32),
            pltpu.VMEM((S, 4, VG, 128), F32),
            pltpu.VMEM((S, 4, VG, 128), F32),
            pltpu.VMEM((S, CX, VG // 2, 128), F32),
            pltpu.VMEM((S, 8, 128), F32),
            DMA((2 * BLOCKS,)),
        ],
        compiler_params=BIG,
    )(*args)


def paired(value, axis, by=1):
    peers = lax.axis_size(axis)
    return lax.ppermute(value, axis, [(i, i ^ by) for i in range(peers)])


def crossed(value, axis, by):
    peers = lax.axis_size(axis)
    pairs = [(i, (i + (by if i % 2 else -by)) % peers) for i in range(peers)]
    return lax.ppermute(value, axis, pairs)


def per_device(
    distribution, wall_temp, coverage, face_cell, face_owner, stoichiometry, sticking, surface_rates
):
    field = (
        distribution.reshape(S, VG * VG, CX, 2, 128)
        .transpose(0, 1, 3, 2, 4)
        .reshape(S * VG, 128, 128)
    )
    field = pltpu.with_memory_space_constraint(field, pltpu.HBM)
    own, to_far, to_near, held, far, nigh = moments_call(field)
    together = lax.optimization_barrier
    face_row = face_cell.reshape(1, 128)

    own = own + crossed(to_far, "space", 1) + paired(to_near, "space")
    own, held = together((own, held))

    far = crossed(near(far), "space", 1)
    nigh = paired(near(nigh), "space")
    moved0 = shift_call(0, held)
    own = own + paired(own, "x", 1) + paired(own, "x", 3) + paired(own, "x", 2)
    own, moved0, held = together((own, moved0, held))

    temp, own = together((wall_temp.reshape(1, 128), own))
    walls = wall_call(
        stoichiometry.T, sticking, surface_rates, temp, coverage, face_row,
        face_owner.reshape(1, 128),
    )
    moved1 = shift_call(1, held)
    own = own + paired(own, "z")
    own, moved1, held, walls = together((own, moved1, held, walls))

    moved2 = shift_call(2, held)
    parts = [own] + [crossed(own, "z", by) for by in (1, 3, 2)]
    surface, sums, wall_x, wall_y = walls
    vmem = [near(v) for v in parts + [surface, sums]]
    covers, advanced = step_call(
        *vmem, face_row, near(wall_x), near(wall_y), near(far), near(nigh),
        near(moved0), near(moved1), near(moved2),
    )
    advanced = (
        advanced.reshape(S, VG * VG, 2, CX, 128)
        .transpose(0, 1, 3, 2, 4)
        .reshape(distribution.shape)
    )
    return advanced, covers


def solution(mesh):
    fine = Mesh(mesh.devices.reshape(N_Z, N_X, mesh.shape["space"]), ("z", "x", "space"))
    return jax.shard_map(
        per_device,
        mesh=fine,
        in_specs=(
            P(None, ("z", "x"), "space", None),
            P("space"),
            P(None, "space"),
            P("space", None),
            P("space"),
            P(),
            P(),
            P(),
        ),
        out_specs=(P(None, ("z", "x"), "space", None), P(None, "space")),
        check_vma=False,
    )
```
